32 devices in a mesh: rows: 4 (over y, x), blk: 8 (over z, core).
Axes of the slice: x: 2, y: 2, z: 4, core: 2. Of those that a mesh axis runs over, the one named last changes fastest.
Arguments:
- tokens: bfloat16 [4, 1024, 2048], P('rows', 'blk'), may hold values from -6 to 6
- segments: int32 [4, 1024], P('rows', 'blk'), may hold values from 0 to 4, as said below
- cotangent: bfloat16 [4, 1024, 2048], P('rows', 'blk'), may hold values from -6 to 6
- attend_gain: bfloat16 [2048], P(('rows', 'blk')), may hold values from 0.5 to 1.5
- attend_shift: bfloat16 [2048], P(('rows', 'blk')), may hold values from -3 to 3
- project_weight: bfloat16 [2048, 6144], P(('rows', 'blk')), may hold values from -0.125 to 0.125
- project_bias: bfloat16 [6144], P(('rows', 'blk')), may hold values from -3 to 3
- output_weight: bfloat16 [2048, 2048], P(('rows', 'blk')), may hold values from -0.75 to 0.75
- feed_gain: bfloat16 [2048], P(('rows', 'blk')), may hold values from 0.5 to 1.5
- feed_shift: bfloat16 [2048], P(('rows', 'blk')), may hold values from -3 to 3
- gate_weight: bfloat16 [2048, 5632], P(('rows', 'blk')), may hold values from -0.125 to 0.125
- up_weight: bfloat16 [2048, 5632], P(('rows', 'blk')), may hold values from -0.125 to 0.125
- down_weight: bfloat16 [5632, 2048], P(('rows', 'blk')), may hold values from -0.078125 to 0.078125
Outputs:
- output: bfloat16 [4, 1024, 2048], P('rows', 'blk')
- tokens_grad: float32 [4, 1024, 2048], P('rows', 'blk')
- attend_gain_grad: float32 [2048], P(('rows', 'blk'))
- attend_shift_grad: float32 [2048], P(('rows', 'blk'))
- project_weight_grad: float32 [2048, 6144], P(('rows', 'blk'))
- project_bias_grad: float32 [6144], P(('rows', 'blk'))
- output_weight_grad: float32 [2048, 2048], P(('rows', 'blk'))
- feed_gain_grad: float32 [2048], P(('rows', 'blk'))
- feed_shift_grad: float32 [2048], P(('rows', 'blk'))
- gate_weight_grad: float32 [2048, 5632], P(('rows', 'blk'))
- up_weight_grad: float32 [2048, 5632], P(('rows', 'blk'))
- down_weight_grad: float32 [5632, 2048], P(('rows', 'blk'))
The draws below stay inside these ranges and needn't reach their ends.
Inputs may be any that keep to these rules, and one draw needn't show every extreme that they name: `segments`: in each sequence the segment ids start at 0, never fall and rise by one at each of four document starts; one document begins within the first 128 tokens and ends within the last 128 tokens, at least two tokens from either end.
All inputs are finite; a program needn't handle non-finite values.
Results may differ from the reference program's by a relative error of at most 0.039.
Values may be sent and summed in bfloat16 or wider, within the bound.
A program may use at most 312 MiB of HBM per device.

```python
import math
import jax
import jax.numpy as jnp
from jax import lax

D = 2048
HEADS = 32
FF = 5632
ROT = 16
BLK = 128
HD = 64
LEN = 1024
ROWS = 4


def draw_segments(key, part):
    key = jax.random.fold_in(key, 11)
    first_key, early_key, late_key, last_key = jax.random.split(key, 4)
    first_cut = jax.random.randint(first_key, (ROWS, 1), 2, BLK, dtype=jnp.int32)
    early_cut = jax.random.randint(early_key, (ROWS, 1), 1, first_cut, dtype=jnp.int32)
    late_cut = jax.random.randint(late_key, (ROWS, 1), LEN - BLK + 1, LEN - 1, dtype=jnp.int32)
    last_cut = jax.random.randint(last_key, (ROWS, 1), late_cut + 1, LEN, dtype=jnp.int32)
    positions = jnp.arange(LEN, dtype=jnp.int32)[None, :]
    return (positions >= early_cut).astype(jnp.int32) + (positions >= first_cut).astype(jnp.int32) + (positions >= late_cut).astype(jnp.int32) + (positions >= last_cut).astype(jnp.int32)


def shard_levels(stream_key, extent, cuts, smallest, top_value):
    factor_of, own = 1.0, jax.random.fold_in(stream_key, 6)
    for position, shards_of in cuts:
        draws = jnp.exp(jax.random.uniform(jax.random.fold_in(own, position), (shards_of,), jnp.float32, smallest / len(cuts), top_value / len(cuts)))
        factor_of = factor_of * jnp.repeat(draws, extent[position] // shards_of).reshape([-1 if axis == position else 1 for axis in range(len(extent))])
    return factor_of


def gaussian(key, extent, deviation, reach, shards=(), held_as=jnp.bfloat16):
    level = shard_levels(key, extent, shards, -0.22, 0.18) if shards else 1.0
    values = jax.random.normal(key, extent, jnp.float32) * deviation * level
    return jnp.minimum(jnp.maximum(values, -reach), reach).astype(held_as)


def setup_inputs(seed: int = 0) -> dict:
    arg_keys = jax.random.split(jax.random.key(seed), 14)
    return {
        "tokens": gaussian(arg_keys[0], (ROWS, LEN, D), 1.0, 6.0, ((0, 4), (1, 8))),
        "segments": draw_segments(jax.random.fold_in(arg_keys[13], 71), 0),
        "cotangent": gaussian(arg_keys[2], (ROWS, LEN, D), 1.0, 6.0, ((0, 4), (1, 8))),
        "attend_gain": jnp.clip(1.0 + 0.1 * jax.random.normal(arg_keys[3], (D,), jnp.float32), 0.5, 1.5).astype(jnp.bfloat16),
        "attend_shift": gaussian(arg_keys[4], (D,), 0.5, 3.0, ((0, 32),)),
        "project_weight": gaussian(arg_keys[5], (D, 3 * D), D ** -0.5, 0.125, ((0, 32),)),
        "project_bias": gaussian(arg_keys[6], (3 * D,), 0.5, 3.0, ((0, 32),)),
        "output_weight": gaussian(arg_keys[7], (D, D), (D // 32) ** -0.5, 0.75, ((0, 32),)),
        "feed_gain": jnp.clip(1.0 + 0.1 * jax.random.normal(arg_keys[8], (D,), jnp.float32), 0.5, 1.5).astype(jnp.bfloat16),
        "feed_shift": gaussian(arg_keys[9], (D,), 0.5, 3.0, ((0, 32),)),
        "gate_weight": gaussian(arg_keys[10], (D, FF), D ** -0.5, 0.125, ((0, 32),)),
        "up_weight": gaussian(arg_keys[11], (D, FF), D ** -0.5, 0.125, ((0, 32),)),
        "down_weight": gaussian(arg_keys[12], (FF, D), FF ** -0.5, 0.078125, ((0, 32),)),
    }


epsilon = 1e-05
rotary_base = 10000.0
masked_value = -1e+30
highest = lax.Precision.HIGHEST

@jax.custom_vjp
def low(v):
    return lax.optimization_barrier(v.astype(jnp.bfloat16)).astype(jnp.float32)

@jax.custom_vjp
def low_back(v):
    return v

def low_keep(v):
    return (low(v), None)

def low_pass(kept, grad):
    return (grad,)

def back_keep(v):
    return (v, None)

def back_low(kept, grad):
    return (low(grad),)
low.defvjp(low_keep, low_pass)
low_back.defvjp(back_keep, back_low)

def layer_norm(inputs, gain, shift):
    row_mean = lax.optimization_barrier(jnp.mean(inputs, axis=-1, keepdims=True))
    centered = inputs - row_mean
    variance = lax.optimization_barrier(jnp.mean(centered * centered, axis=-1, keepdims=True))
    return centered * lax.rsqrt(variance + epsilon) * gain + shift

def rotary(columns, places, head_count, rot_dims):
    head_width = columns.shape[-1] // head_count
    split_heads = columns.reshape(columns.shape[:-1] + (head_count, head_width))
    half_rot = rot_dims // 2
    frequency = jnp.power(rotary_base, -jnp.arange(half_rot, dtype=jnp.int32).astype(jnp.float32) / half_rot)
    angles = places.astype(jnp.float32)[..., None] * frequency
    cosine = jnp.cos(angles)[..., None, :]
    sine_part = jnp.sin(angles)[..., None, :]
    first_part = split_heads[..., :half_rot]
    second_part = split_heads[..., half_rot:rot_dims]
    rest_part = split_heads[..., rot_dims:]
    turned = jnp.concatenate([first_part * cosine - second_part * sine_part, second_part * cosine + first_part * sine_part, rest_part], axis=-1)
    return turned.reshape(columns.shape)

def places_of(row_segments, query_segments, query_index):
    doc_starts = lax.optimization_barrier(jnp.sum((row_segments[None, :] < query_segments[:, None]).astype(jnp.int32), axis=1))
    return query_index - doc_starts

def allowed(query_index, query_segments, key_index, key_segments):
    return (key_index[None, :] <= query_index[:, None]) & (key_segments[None, :] == query_segments[:, None])

def attention_row(queries, key_rows, value_rows, row_segments):
    seq_length = queries.shape[0]
    query_block = min(512, seq_length)
    score_scale = 1.0 / math.sqrt(HD)
    positions = jnp.arange(seq_length, dtype=jnp.int32)

    def block_attention(block_args):
        query_part, query_index, query_segments = block_args
        raw = low_back(jnp.einsum('qhd,khd->hqk', query_part, key_rows, precision=highest))
        scores = raw * score_scale
        allowed_mask = allowed(query_index, query_segments, positions, row_segments)[None]
        scores = jnp.where(allowed_mask, scores, masked_value)
        row_top = lax.optimization_barrier(jnp.max(scores, axis=2, keepdims=True))
        weights = jnp.where(allowed_mask, jnp.exp(scores - row_top), 0.0)
        row_total = lax.optimization_barrier(jnp.sum(weights, axis=2))
        summed = jnp.einsum('hqk,khd->qhd', low(weights), value_rows, precision=highest)
        return summed / jnp.transpose(row_total)[:, :, None]
    block_outputs = lax.map(jax.checkpoint(block_attention), (queries.reshape(seq_length // query_block, query_block, HEADS, HD), positions.reshape(seq_length // query_block, query_block), row_segments.reshape(seq_length // query_block, query_block)))
    return block_outputs.reshape(seq_length, HEADS, HD)

def forward(inputs, parameters, segments):
    attend_gain, attend_shift, project_weight, project_bias, output_weight, feed_gain, feed_shift, gate_weight, up_weight, down_weight = parameters
    seq_length = inputs.shape[1]
    positions = jnp.arange(seq_length, dtype=jnp.int32)
    places = lax.map(lambda row_segments: places_of(row_segments, row_segments, positions), segments)
    normed_first = low(layer_norm(inputs, attend_gain, attend_shift))
    mixed_proj = low_back(jnp.dot(normed_first, project_weight, precision=highest) + project_bias)
    queries = low(rotary(mixed_proj[..., :D], places, HEADS, ROT))
    key_rows = low(rotary(mixed_proj[..., D:2 * D], places, HEADS, ROT))
    value_rows = low(mixed_proj[..., 2 * D:])
    head_shape = (inputs.shape[0], seq_length, HEADS, HD)
    attended = lax.map(lambda block_args: attention_row(block_args[0], block_args[1], block_args[2], block_args[3]), (queries.reshape(head_shape), key_rows.reshape(head_shape), value_rows.reshape(head_shape), segments))
    attended_low = low(low_back(attended.reshape(inputs.shape)))
    resid_mid = inputs + low_back(jnp.dot(attended_low, output_weight, precision=highest))
    normed_second = low(layer_norm(resid_mid, feed_gain, feed_shift))
    gate_value = low_back(jnp.dot(normed_second, gate_weight, precision=highest))
    up_value = low_back(jnp.dot(normed_second, up_weight, precision=highest))
    hidden = low(jax.nn.silu(gate_value) * up_value)
    return resid_mid + low_back(jnp.dot(hidden, down_weight, precision=highest))

def reference(tokens, segments, cotangent, attend_gain, attend_shift, project_weight, project_bias, output_weight, feed_gain, feed_shift, gate_weight, up_weight, down_weight):
    parameters = (attend_gain.astype(jnp.float32), attend_shift.astype(jnp.float32), project_weight.astype(jnp.float32), project_bias.astype(jnp.float32), output_weight.astype(jnp.float32), feed_gain.astype(jnp.float32), feed_shift.astype(jnp.float32), gate_weight.astype(jnp.float32), up_weight.astype(jnp.float32), down_weight.astype(jnp.float32))
    inputs = tokens.astype(jnp.float32)
    result, pullback = jax.vjp(lambda layer_in, layer_params: forward(layer_in, layer_params, segments), inputs, parameters)
    grad_tokens, grad_params = pullback(cotangent.astype(jnp.float32))
    return (result.astype(jnp.bfloat16), grad_tokens, grad_params[0], grad_params[1], grad_params[2], grad_params[3], grad_params[4], grad_params[5], grad_params[6], grad_params[7], grad_params[8], grad_params[9])
```

```python
import math

import jax
import jax.numpy as jnp
from jax import lax
from jax.sharding import PartitionSpec as P

HEADS = 32
ROT = 16
BOTH = ("rows", "blk")

epsilon = 1e-05
rotary_base = 10000.0
masked_value = -1e30


def dot(left, right, contract):
    return lax.dot_general(
        left, right, (contract, ((), ())), preferred_element_type=jnp.float32
    )


def norm_stats(inputs):
    row_mean = jnp.mean(inputs, axis=-1, keepdims=True)
    centered = inputs - row_mean
    variance = jnp.mean(centered * centered, axis=-1, keepdims=True)
    inverse = lax.rsqrt(variance + epsilon)
    return centered * inverse, inverse


def norm_back(incoming, unit, inverse, gain):
    gain_part = jnp.sum(incoming * unit, axis=0)
    shift_part = jnp.sum(incoming, axis=0)
    unit_grad = incoming * gain
    grad = inverse * (
        unit_grad
        - jnp.mean(unit_grad, axis=-1, keepdims=True)
        - unit * jnp.mean(unit_grad * unit, axis=-1, keepdims=True)
    )
    return grad, gain_part, shift_part


def rotate(columns, cosine, sine, head_width):
    half = cosine.shape[1]
    heads = columns.reshape(columns.shape[0], -1, head_width)
    cosine, sine = cosine[:, None, :], sine[:, None, :]
    first, second, rest = heads[..., :half], heads[..., half : 2 * half], heads[..., 2 * half :]
    return jnp.concatenate(
        [first * cosine - second * sine, second * cosine + first * sine, rest], axis=-1
    ).reshape(columns.shape)


def gather_blk(rows):
    return lax.all_gather(rows, "blk", axis=0, tiled=True)


def scatter_blk(partial):
    return lax.psum_scatter(
        partial.astype(jnp.bfloat16), "blk", scatter_dimension=0, tiled=True
    ).astype(jnp.float32)


def gather_rows(shard):
    return lax.all_gather(shard, "rows", axis=0, tiled=True)


def scatter_rows(partial):
    return lax.psum_scatter(
        partial.astype(jnp.bfloat16), "rows", scatter_dimension=0, tiled=True
    )


def exchange_blk(pieces):
    return lax.all_to_all(pieces, "blk", split_axis=0, concat_axis=0, tiled=True)


def make_body(group, ranks):
    def columns_of(shard, parts, inner):
        depth = shard.shape[0]
        pieces = shard.reshape(depth, parts, ranks, inner).transpose(2, 0, 1, 3)
        pieces = exchange_blk(pieces.reshape(ranks, depth, parts * inner))
        return gather_rows(pieces.reshape(ranks * depth, parts * inner))

    def columns_back(grad, parts, inner):
        owned = scatter_rows(grad)
        depth = owned.shape[0] // ranks
        pieces = exchange_blk(owned.reshape(ranks, depth, parts * inner))
        pieces = pieces.reshape(ranks, depth, parts, inner).transpose(1, 2, 0, 3)
        return pieces.reshape(depth, parts * ranks * inner).astype(jnp.float32)

    def body(
        tokens,
        segments,
        cotangent,
        attend_gain,
        attend_shift,
        project_weight,
        project_bias,
        output_weight,
        feed_gain,
        feed_shift,
        gate_weight,
        up_weight,
        down_weight,
    ):
        own_rows, width = tokens.shape[1], tokens.shape[2]
        length = own_rows * ranks
        head_width = width // HEADS
        local_heads = HEADS // ranks
        local_width = local_heads * head_width
        score_scale = 1.0 / math.sqrt(head_width)
        hidden_shard = down_weight.shape[0]
        shard = attend_gain.shape[0]
        me = lax.axis_index("blk")

        packed = jnp.concatenate(
            [
                attend_gain,
                attend_shift,
                feed_gain,
                feed_shift,
                project_bias,
                segments[0].astype(jnp.bfloat16),
            ]
        )
        packed = lax.all_gather(packed, BOTH, axis=0, tiled=False)
        a_gain = packed[:, :shard].reshape(-1).astype(jnp.float32)
        a_shift = packed[:, shard : 2 * shard].reshape(-1).astype(jnp.float32)
        f_gain = packed[:, 2 * shard : 3 * shard].reshape(-1).astype(jnp.float32)
        f_shift = packed[:, 3 * shard : 4 * shard].reshape(-1).astype(jnp.float32)
        bias = packed[:, 4 * shard : 7 * shard].reshape(3, ranks, local_width)
        bias = lax.dynamic_index_in_dim(bias, me, 1, False).reshape(-1).astype(jnp.float32)
        doc = packed[:, 7 * shard :].reshape(group, ranks * own_rows)
        doc = lax.dynamic_index_in_dim(doc, lax.axis_index("rows"), 0, False)

        w_project = columns_of(project_weight, 3, local_width)
        w_gate = columns_of(gate_weight, group, hidden_shard)
        w_up = columns_of(up_weight, group, hidden_shard)
        w_down = gather_rows(down_weight)
        w_out = lax.all_gather(output_weight, BOTH, axis=0, tiled=True)

        doc = doc.astype(jnp.int32)
        index = jnp.arange(length, dtype=jnp.int32)
        places = index - jnp.sum((doc[None, :] < doc[:, None]).astype(jnp.int32), axis=1)
        half = ROT // 2
        frequency = jnp.power(
            rotary_base, -jnp.arange(half, dtype=jnp.int32).astype(jnp.float32) / half
        )
        angles = places.astype(jnp.float32)[:, None] * frequency
        cosine, sine = jnp.cos(angles), jnp.sin(angles)
        mask = ((index[None, :] <= index[:, None]) & (doc[None, :] == doc[:, None]))[None]

        inputs = tokens[0].astype(jnp.float32)
        unit_first, inverse_first = norm_stats(inputs)
        normed_first = gather_blk((unit_first * a_gain + a_shift).astype(jnp.bfloat16))
        grad_out = gather_blk(cotangent[0])
        mixed = dot(normed_first, w_project, ((1,), (0,))) + bias
        queries = rotate(mixed[:, :local_width], cosine, sine, head_width).astype(jnp.bfloat16)
        keys = rotate(mixed[:, local_width : 2 * local_width], cosine, sine, head_width)
        keys = keys.astype(jnp.bfloat16)
        values = mixed[:, 2 * local_width :].astype(jnp.bfloat16)
        q_heads = queries.reshape(length, local_heads, head_width)
        k_heads = keys.reshape(length, local_heads, head_width)
        v_heads = values.reshape(length, local_heads, head_width)
        scores = jnp.einsum("qhd,khd->hqk", q_heads, k_heads, preferred_element_type=jnp.float32)
        scores = jnp.where(mask, scores * score_scale, masked_value)
        top = jnp.max(scores, axis=2, keepdims=True)
        weights = jnp.where(mask, jnp.exp(scores - top), 0.0)
        total = jnp.sum(weights, axis=2, keepdims=True)
        attended = jnp.einsum(
            "hqk,khd->qhd",
            weights.astype(jnp.bfloat16),
            v_heads,
            preferred_element_type=jnp.float32,
        ) / jnp.transpose(total[:, :, 0])[:, :, None]
        log_total = top + jnp.log(total)
        attended_flat = attended.reshape(length, local_width)
        attended_low = exchange_blk(
            attended_flat.astype(jnp.bfloat16).reshape(ranks, own_rows, local_width)
        )
        attended_low = attended_low.transpose(1, 0, 2).reshape(own_rows, width)
        resid_mid = inputs + dot(attended_low, w_out, ((1,), (0,)))

        unit_second, inverse_second = norm_stats(resid_mid)
        normed_second = gather_blk((unit_second * f_gain + f_shift).astype(jnp.bfloat16))
        gate_value = dot(normed_second, w_gate, ((1,), (0,)))
        up_value = dot(normed_second, w_up, ((1,), (0,)))
        gate_sigmoid = jax.nn.sigmoid(gate_value)
        silu = gate_value * gate_sigmoid
        hidden = (silu * up_value).astype(jnp.bfloat16)
        output = (resid_mid + scatter_blk(dot(hidden, w_down, ((1,), (0,))))).astype(jnp.bfloat16)

        grad_hidden = dot(grad_out, w_down, ((1,), (1,)))
        grad_gate = (
            grad_hidden * up_value * gate_sigmoid * (1.0 + gate_value * (1.0 - gate_sigmoid))
        ).astype(jnp.bfloat16)
        grad_up = (grad_hidden * silu).astype(jnp.bfloat16)
        grad_second = scatter_blk(
            dot(grad_gate, w_gate, ((1,), (1,))) + dot(grad_up, w_up, ((1,), (1,)))
        )
        down_grad = scatter_rows(dot(hidden, grad_out, ((0,), (0,)))).astype(jnp.float32)
        gate_grad = columns_back(dot(normed_second, grad_gate, ((0,), (0,))), group, hidden_shard)
        up_grad = columns_back(dot(normed_second, grad_up, ((0,), (0,))), group, hidden_shard)
        mid_part, f_gain_part, f_shift_part = norm_back(
            grad_second, unit_second, inverse_second, f_gain
        )
        grad_mid = cotangent[0].astype(jnp.float32) + mid_part
        grad_mid_low = grad_mid.astype(jnp.bfloat16)
        grad_attended = dot(grad_mid_low, w_out, ((1,), (1,))).astype(jnp.bfloat16)
        grad_attended = exchange_blk(
            grad_attended.reshape(own_rows, ranks, local_width).transpose(1, 0, 2)
        ).reshape(length, local_width)
        out_grad = lax.psum_scatter(
            dot(attended_low, grad_mid_low, ((0,), (0,))).astype(jnp.bfloat16),
            BOTH,
            scatter_dimension=0,
            tiled=True,
        ).astype(jnp.float32)

        g_heads = grad_attended.reshape(length, local_heads, head_width)
        delta = jnp.transpose(jnp.sum(g_heads.astype(jnp.float32) * attended, axis=2))
        probs = jnp.where(mask, jnp.exp(scores - log_total), 0.0)
        values_grad = jnp.einsum(
            "hqk,qhd->khd", probs.astype(jnp.bfloat16), g_heads, preferred_element_type=jnp.float32
        )
        grad_probs = jnp.einsum("qhd,khd->hqk", g_heads, v_heads, preferred_element_type=jnp.float32)
        grad_scores = (probs * (grad_probs - delta[:, :, None]) * score_scale).astype(jnp.bfloat16)
        grad_queries = jnp.einsum(
            "hqk,khd->qhd", grad_scores, k_heads, preferred_element_type=jnp.float32
        )
        keys_grad = jnp.einsum(
            "hqk,qhd->khd", grad_scores, q_heads, preferred_element_type=jnp.float32
        )
        grad_mixed = jnp.concatenate(
            [
                rotate(grad_queries.reshape(length, local_width), cosine, -sine, head_width),
                rotate(keys_grad.reshape(length, local_width), cosine, -sine, head_width),
                values_grad.reshape(length, local_width),
            ],
            axis=1,
        ).astype(jnp.bfloat16)
        grad_first = scatter_blk(dot(grad_mixed, w_project, ((1,), (1,))))
        project_grad = columns_back(
            dot(normed_first, grad_mixed, ((0,), (0,))), 3, local_width
        )
        bias_part = jnp.sum(grad_mixed.astype(jnp.float32), axis=0).reshape(3, 1, local_width)
        bias_part = jnp.where(jnp.arange(ranks)[None, :, None] == me, bias_part, 0.0)
        input_part, a_gain_part, a_shift_part = norm_back(
            grad_first, unit_first, inverse_first, a_gain
        )
        grad_tokens = grad_mid + input_part
        vectors = jnp.concatenate(
            [
                a_gain_part.reshape(-1, shard),
                a_shift_part.reshape(-1, shard),
                f_gain_part.reshape(-1, shard),
                f_shift_part.reshape(-1, shard),
                bias_part.reshape(-1, 3 * shard),
            ],
            axis=1,
        )
        vectors = lax.psum_scatter(vectors, BOTH, scatter_dimension=0, tiled=True)[0]
        return (
            output[None],
            grad_tokens[None],
            vectors[:shard],
            vectors[shard : 2 * shard],
            project_grad,
            vectors[4 * shard :],
            out_grad,
            vectors[2 * shard : 3 * shard],
            vectors[3 * shard : 4 * shard],
            gate_grad,
            up_grad,
            down_grad,
        )

    return body


def solution(mesh):
    tokens = P("rows", "blk", None)
    vector, matrix = P(BOTH), P(BOTH, None)
    in_specs = (
        tokens, P("rows", "blk"), tokens, vector, vector, matrix, vector, matrix, vector, vector,
        matrix, matrix, matrix,
    )
    out_specs = (
        tokens, tokens, vector, vector, matrix, vector, matrix, vector, vector, matrix, matrix, matrix,
    )
    body = make_body(mesh.shape["rows"], mesh.shape["blk"])
    return jax.shard_map(body, mesh=mesh, in_specs=in_specs, out_specs=out_specs, check_vma=False)
```

```python
import functools
import math

import jax
import jax.numpy as jnp
from jax import lax
from jax.experimental import pallas as pl
from jax.experimental.pallas import tpu as pltpu
from jax.sharding import PartitionSpec as P

HEADS = 32
ROT = 16
BOTH = ("rows", "blk")

epsilon = 1e-05
rotary_base = 10000.0
masked_value = -1e30


def dot(left, right, contract):
    return lax.dot_general(
        left, right, (contract, ((), ())), preferred_element_type=jnp.float32
    )


def norm_stats(inputs):
    row_mean = jnp.mean(inputs, axis=-1, keepdims=True)
    centered = inputs - row_mean
    variance = jnp.mean(centered * centered, axis=-1, keepdims=True)
    inverse = lax.rsqrt(variance + epsilon)
    return centered * inverse, inverse


def norm_back(incoming, unit, inverse, gain):
    gain_part = jnp.sum(incoming * unit, axis=0)
    shift_part = jnp.sum(incoming, axis=0)
    unit_grad = incoming * gain
    grad = inverse * (
        unit_grad
        - jnp.mean(unit_grad, axis=-1, keepdims=True)
        - unit * jnp.mean(unit_grad * unit, axis=-1, keepdims=True)
    )
    return grad, gain_part, shift_part


def rotate(columns, cosine, sine, head_width):
    half = cosine.shape[1]
    heads = columns.reshape(columns.shape[0], -1, head_width)
    cosine, sine = cosine[:, None, :], sine[:, None, :]
    first, second, rest = heads[..., :half], heads[..., half : 2 * half], heads[..., 2 * half :]
    return jnp.concatenate(
        [first * cosine - second * sine, second * cosine + first * sine, rest], axis=-1
    ).reshape(columns.shape)


def gather_blk(rows):
    return lax.all_gather(rows, "blk", axis=0, tiled=True)


def scatter_blk(partial):
    return lax.psum_scatter(
        partial.astype(jnp.bfloat16), "blk", scatter_dimension=0, tiled=True
    ).astype(jnp.float32)


def gather_rows(shard):
    return lax.all_gather(shard, "rows", axis=0, tiled=True)


def scatter_rows(partial):
    return lax.psum_scatter(
        partial.astype(jnp.bfloat16), "rows", scatter_dimension=0, tiled=True
    )


def exchange_blk(pieces):
    return lax.all_to_all(pieces, "blk", split_axis=0, concat_axis=0, tiled=True)


def make_body(group, ranks):
    def columns_of(shard, parts, inner):
        depth = shard.shape[0]
        pieces = shard.reshape(depth, parts, ranks, inner).transpose(2, 0, 1, 3)
        pieces = exchange_blk(pieces.reshape(ranks, depth, parts * inner))
        return gather_rows(pieces.reshape(ranks * depth, parts * inner))

    def columns_back(grad, parts, inner):
        owned = scatter_rows(grad)
        depth = owned.shape[0] // ranks
        pieces = exchange_blk(owned.reshape(ranks, depth, parts * inner))
        pieces = pieces.reshape(ranks, depth, parts, inner).transpose(1, 2, 0, 3)
        return pieces.reshape(depth, parts * ranks * inner).astype(jnp.float32)

    def body(
        tokens,
        segments,
        cotangent,
        attend_gain,
        attend_shift,
        project_weight,
        project_bias,
        output_weight,
        feed_gain,
        feed_shift,
        gate_weight,
        up_weight,
        down_weight,
    ):
        own_rows, width = tokens.shape[1], tokens.shape[2]
        length = own_rows * ranks
        head_width = width // HEADS
        local_heads = HEADS // ranks
        local_width = local_heads * head_width
        score_scale = 1.0 / math.sqrt(head_width)
        hidden_shard = down_weight.shape[0]
        shard = attend_gain.shape[0]
        me = lax.axis_index("blk")

        packed = jnp.concatenate(
            [
                attend_gain,
                attend_shift,
                feed_gain,
                feed_shift,
                project_bias,
                segments[0].astype(jnp.bfloat16),
            ]
        )
        packed = lax.all_gather(packed, BOTH, axis=0, tiled=False)
        a_gain = packed[:, :shard].reshape(-1).astype(jnp.float32)
        a_shift = packed[:, shard : 2 * shard].reshape(-1).astype(jnp.float32)
        f_gain = packed[:, 2 * shard : 3 * shard].reshape(-1).astype(jnp.float32)
        f_shift = packed[:, 3 * shard : 4 * shard].reshape(-1).astype(jnp.float32)
        bias = packed[:, 4 * shard : 7 * shard].reshape(3, ranks, local_width)
        bias = lax.dynamic_index_in_dim(bias, me, 1, False).reshape(-1).astype(jnp.float32)
        doc = packed[:, 7 * shard :].reshape(group, ranks * own_rows)
        doc = lax.dynamic_index_in_dim(doc, lax.axis_index("rows"), 0, False)

        w_project = columns_of(project_weight, 3, local_width)
        w_gate = columns_of(gate_weight, group, hidden_shard)
        w_up = columns_of(up_weight, group, hidden_shard)
        w_down = gather_rows(down_weight)
        w_out = lax.all_gather(output_weight, BOTH, axis=0, tiled=True)

        doc = doc.astype(jnp.int32)
        index = jnp.arange(length, dtype=jnp.int32)
        places = index - jnp.sum((doc[None, :] < doc[:, None]).astype(jnp.int32), axis=1)
        half = ROT // 2
        frequency = jnp.power(
            rotary_base, -jnp.arange(half, dtype=jnp.int32).astype(jnp.float32) / half
        )
        angles = places.astype(jnp.float32)[:, None] * frequency
        cosine, sine = jnp.cos(angles), jnp.sin(angles)
        mask = ((index[None, :] <= index[:, None]) & (doc[None, :] == doc[:, None]))[None]

        inputs = tokens[0].astype(jnp.float32)
        unit_first, inverse_first = norm_stats(inputs)
        normed_first = gather_blk((unit_first * a_gain + a_shift).astype(jnp.bfloat16))
        grad_out = gather_blk(cotangent[0])
        mixed = dot(normed_first, w_project, ((1,), (0,))) + bias
        queries = rotate(mixed[:, :local_width], cosine, sine, head_width).astype(jnp.bfloat16)
        keys = rotate(mixed[:, local_width : 2 * local_width], cosine, sine, head_width)
        keys = keys.astype(jnp.bfloat16)
        values = mixed[:, 2 * local_width :].astype(jnp.bfloat16)
        q_heads = queries.reshape(length, local_heads, head_width)
        k_heads = keys.reshape(length, local_heads, head_width)
        v_heads = values.reshape(length, local_heads, head_width)
        scores = jnp.einsum("qhd,khd->hqk", q_heads, k_heads, preferred_element_type=jnp.float32)
        scores = jnp.where(mask, scores * score_scale, masked_value)
        top = jnp.max(scores, axis=2, keepdims=True)
        weights = jnp.where(mask, jnp.exp(scores - top), 0.0)
        total = jnp.sum(weights, axis=2, keepdims=True)
        attended = jnp.einsum(
            "hqk,khd->qhd",
            weights.astype(jnp.bfloat16),
            v_heads,
            preferred_element_type=jnp.float32,
        ) / jnp.transpose(total[:, :, 0])[:, :, None]
        log_total = top + jnp.log(total)
        attended_flat = attended.reshape(length, local_width)
        attended_low = exchange_blk(
            attended_flat.astype(jnp.bfloat16).reshape(ranks, own_rows, local_width)
        )
        attended_low = attended_low.transpose(1, 0, 2).reshape(own_rows, width)
        resid_mid = inputs + dot(attended_low, w_out, ((1,), (0,)))

        unit_second, inverse_second = norm_stats(resid_mid)
        normed_second = gather_blk((unit_second * f_gain + f_shift).astype(jnp.bfloat16))
        gate_value = dot(normed_second, w_gate, ((1,), (0,)))
        up_value = dot(normed_second, w_up, ((1,), (0,)))
        gate_sigmoid = jax.nn.sigmoid(gate_value)
        silu = gate_value * gate_sigmoid
        hidden = (silu * up_value).astype(jnp.bfloat16)
        output = (resid_mid + scatter_blk(dot(hidden, w_down, ((1,), (0,))))).astype(jnp.bfloat16)

        grad_hidden = dot(grad_out, w_down, ((1,), (1,)))
        grad_gate = (
            grad_hidden * up_value * gate_sigmoid * (1.0 + gate_value * (1.0 - gate_sigmoid))
        ).astype(jnp.bfloat16)
        grad_up = (grad_hidden * silu).astype(jnp.bfloat16)
        grad_second = scatter_blk(
            dot(grad_gate, w_gate, ((1,), (1,))) + dot(grad_up, w_up, ((1,), (1,)))
        )
        down_grad = scatter_rows(dot(hidden, grad_out, ((0,), (0,)))).astype(jnp.float32)
        gate_grad = columns_back(dot(normed_second, grad_gate, ((0,), (0,))), group, hidden_shard)
        up_grad = columns_back(dot(normed_second, grad_up, ((0,), (0,))), group, hidden_shard)
        mid_part, f_gain_part, f_shift_part = norm_back(
            grad_second, unit_second, inverse_second, f_gain
        )
        grad_mid = cotangent[0].astype(jnp.float32) + mid_part
        grad_mid_low = grad_mid.astype(jnp.bfloat16)
        grad_attended = dot(grad_mid_low, w_out, ((1,), (1,))).astype(jnp.bfloat16)
        grad_attended = exchange_blk(
            grad_attended.reshape(own_rows, ranks, local_width).transpose(1, 0, 2)
        ).reshape(length, local_width)
        out_grad = lax.psum_scatter(
            dot(attended_low, grad_mid_low, ((0,), (0,))).astype(jnp.bfloat16),
            BOTH,
            scatter_dimension=0,
            tiled=True,
        ).astype(jnp.float32)

        g_heads = grad_attended.reshape(length, local_heads, head_width)
        delta = jnp.transpose(jnp.sum(g_heads.astype(jnp.float32) * attended, axis=2))
        probs = jnp.where(mask, jnp.exp(scores - log_total), 0.0)
        values_grad = jnp.einsum(
            "hqk,qhd->khd", probs.astype(jnp.bfloat16), g_heads, preferred_element_type=jnp.float32
        )
        grad_probs = jnp.einsum("qhd,khd->hqk", g_heads, v_heads, preferred_element_type=jnp.float32)
        grad_scores = (probs * (grad_probs - delta[:, :, None]) * score_scale).astype(jnp.bfloat16)
        grad_queries = jnp.einsum(
            "hqk,khd->qhd", grad_scores, k_heads, preferred_element_type=jnp.float32
        )
        keys_grad = jnp.einsum(
            "hqk,qhd->khd", grad_scores, q_heads, preferred_element_type=jnp.float32
        )
        grad_mixed = jnp.concatenate(
            [
                rotate(grad_queries.reshape(length, local_width), cosine, -sine, head_width),
                rotate(keys_grad.reshape(length, local_width), cosine, -sine, head_width),
                values_grad.reshape(length, local_width),
            ],
            axis=1,
        ).astype(jnp.bfloat16)
        grad_first = scatter_blk(dot(grad_mixed, w_project, ((1,), (1,))))
        project_grad = columns_back(
            dot(normed_first, grad_mixed, ((0,), (0,))), 3, local_width
        )
        bias_part = jnp.sum(grad_mixed.astype(jnp.float32), axis=0).reshape(3, 1, local_width)
        bias_part = jnp.where(jnp.arange(ranks)[None, :, None] == me, bias_part, 0.0)
        input_part, a_gain_part, a_shift_part = norm_back(
            grad_first, unit_first, inverse_first, a_gain
        )
        grad_tokens = grad_mid + input_part
        vectors = jnp.concatenate(
            [
                a_gain_part.reshape(-1, shard),
                a_shift_part.reshape(-1, shard),
                f_gain_part.reshape(-1, shard),
                f_shift_part.reshape(-1, shard),
                bias_part.reshape(-1, 3 * shard),
            ],
            axis=1,
        )
        vectors = lax.psum_scatter(vectors, BOTH, scatter_dimension=0, tiled=True)[0]
        return (
            output[None],
            grad_tokens[None],
            vectors[:shard],
            vectors[shard : 2 * shard],
            project_grad,
            vectors[4 * shard :],
            out_grad,
            vectors[2 * shard : 3 * shard],
            vectors[3 * shard : 4 * shard],
            gate_grad,
            up_grad,
            down_grad,
        )

    return body


MESH_ID = pl.DeviceIdType.MESH
DMA = pltpu.SemaphoreType.DMA
HBM = pl.ANY
VMEM = pltpu.VMEM
LIMIT = 56 * 1024 * 1024


class Place:
    def __init__(self):
        self.r = lax.axis_index("rows")
        self.b = lax.axis_index("blk")
        self.z = self.b // 2
        self.c = lax.rem(self.b, 2)
        self.sibling = 2 * self.z + 1 - self.c
        self.rx = self.r + 1 - 2 * lax.rem(self.r, 2)
        self.ry = lax.rem(self.r + 2, 4)
        self.rd = 3 - self.r

    def barrier(self, diagonal=False):
        sem = pltpu.get_barrier_semaphore()
        peers = [(self.r, lax.rem(self.b + k, 8)) for k in range(1, 8)]
        peers += [(self.rx, self.b), (self.ry, self.b)]
        if diagonal:
            peers.append((self.rd, self.b))
        for peer in peers:
            pl.semaphore_signal(sem, inc=1, device_id=peer, device_id_type=MESH_ID)
        pl.semaphore_wait(sem, len(peers))


def remote(src, dst, send, recv, r, b):
    return pltpu.make_async_remote_copy(
        src_ref=src, dst_ref=dst, send_sem=send, recv_sem=recv, device_id=(r, b), device_id_type=MESH_ID
    )


def drive(*jobs):
    active = list(jobs)
    while active:
        for job in list(active):
            try:
                next(job)
            except StopIteration:
                active.remove(job)


CHUNKS = 2


def line_gather_sems():
    return [DMA((4, CHUNKS))] * 4 + [DMA((7, CHUNKS))] * 2 + [DMA]


def line_gather(at, own, full, sems):
    up_send, down_send, up_recv, down_recv, pair_send, pair_recv, local_sem = sems
    count = own.shape[0]
    size = count // CHUNKS

    def rows(device, k):
        return full.at[pl.ds(pl.multiple_of(device * count + k * size, size), size)]

    def up(d, k, src):
        return remote(src, rows(at.b - 2 * d, k), up_send.at[d, k], up_recv.at[d, k], at.r, at.b + 2)

    def down(d, k, src):
        return remote(
            src, rows(at.b + 2 * d, k), down_send.at[d, k], down_recv.at[d, k], at.r, at.b - 2
        )

    def up_in(d, k):
        piece = rows(at.b - 2 * d - 2, k)
        return remote(piece, piece, up_send.at[d, k], up_recv.at[d, k], at.r, at.b + 2)

    def down_in(d, k):
        piece = rows(at.b + 2 * d + 2, k)
        return remote(piece, piece, down_send.at[d, k], down_recv.at[d, k], at.r, at.b - 2)

    def pair(i, k, device, src):
        return remote(src, rows(device, k), pair_send.at[i, k], pair_recv.at[i, k], at.r, at.sibling)

    def pair_in(i, k, device):
        piece = rows(device, k)
        return remote(piece, piece, pair_send.at[i, k], pair_recv.at[i, k], at.r, at.sibling)

    local = pltpu.make_async_copy(own, full.at[pl.ds(at.b * count, count)], local_sem)
    local.start()
    for k in range(CHUNKS):
        src = own.at[pl.ds(k * size, size)]
        pl.when(at.z < 3)(lambda: up(0, k, src).start())
        pl.when(at.z > 0)(lambda: down(0, k, src).start())
        pair(0, k, at.b, src).start()
    yield
    for d in range(3):
        for k in range(CHUNKS):

            @pl.when(at.z - 1 - d >= 0)
            def _():
                device = at.b - 2 * d - 2
                up_in(d, k).wait_recv()
                if d < 2:
                    pl.when(at.z < 3)(lambda: up(d + 1, k, rows(device, k)).start())
                pair(1 + d, k, device, rows(device, k)).start()

            @pl.when(at.z + 1 + d <= 3)
            def _():
                device = at.b + 2 * d + 2
                down_in(d, k).wait_recv()
                if d < 2:
                    pl.when(at.z > 0)(lambda: down(d + 1, k, rows(device, k)).start())
                pair(4 + d, k, device, rows(device, k)).start()

            yield
    local.wait()
    for k in range(CHUNKS):
        src = own.at[pl.ds(k * size, size)]
        pair(0, k, at.b, src).wait_send()
        pair_in(0, k, at.sibling).wait_recv()
        pl.when(at.z < 3)(lambda: up(0, k, src).wait_send())
        pl.when(at.z > 0)(lambda: down(0, k, src).wait_send())
        for d in range(3):

            @pl.when(at.z - 1 - d >= 0)
            def _():
                device = at.b - 2 * d - 2
                pair(1 + d, k, device, rows(device, k)).wait_send()
                pair_in(1 + d, k, at.sibling - 2 * d - 2).wait_recv()
                if d < 2:
                    pl.when(at.z < 3)(lambda: up(d + 1, k, rows(device, k)).wait_send())

            @pl.when(at.z + 1 + d <= 3)
            def _():
                device = at.b + 2 * d + 2
                pair(4 + d, k, device, rows(device, k)).wait_send()
                pair_in(4 + d, k, at.sibling + 2 * d + 2).wait_recv()
                if d < 2:
                    pl.when(at.z > 0)(lambda: down(d + 1, k, rows(device, k)).wait_send())


def line_scatter_scratch(count, width):
    block = VMEM((4, count, width), jnp.bfloat16)
    arrive = VMEM((3, count, width), jnp.bfloat16)
    return [block, arrive, arrive] + [DMA((4, CHUNKS))] * 2 + [DMA((3, CHUNKS))] * 4


def line_scatter(at, partial, result, scratch):
    held, from_below, from_above, pair_send, pair_recv, up_send, up_recv, down_send, down_recv = scratch
    count = held.shape[1]
    size = count // CHUNKS

    def cut(k):
        return pl.ds(k * size, size)

    def block(z, c, k):
        return pl.ds(pl.multiple_of((2 * z + c) * count + k * size, size), size)

    def pair(z, k):
        return remote(
            partial.at[block(z, 1 - at.c, k)],
            held.at[z, cut(k)],
            pair_send.at[z, k],
            pair_recv.at[z, k],
            at.r,
            at.sibling,
        )

    def up(z, k):
        return remote(
            held.at[z, cut(k)],
            from_below.at[z - 1, cut(k)],
            up_send.at[z - 1, k],
            up_recv.at[z - 1, k],
            at.r,
            at.b + 2,
        )

    def down(z, k):
        return remote(
            held.at[z, cut(k)],
            from_above.at[z, cut(k)],
            down_send.at[z, k],
            down_recv.at[z, k],
            at.r,
            at.b - 2,
        )

    def wide(ref):
        return ref[...].astype(jnp.float32)

    def own(z, k):
        return wide(partial.at[block(z, at.c, k)]) + wide(held.at[z, cut(k)])

    for z in (3, 0, 2, 1):
        for k in range(CHUNKS):
            pair(z, k).start()
    yield
    for step in range(3):
        for k in range(CHUNKS):
            far, near = 3 - step, step

            @pl.when(at.z < far)
            def _():
                pair(far, k).wait_recv()

                @pl.when(at.z == 0)
                def _():
                    held[far, cut(k)] = own(far, k).astype(jnp.bfloat16)

                @pl.when(at.z > 0)
                def _():
                    up(far, k).wait_recv()
                    held[far, cut(k)] = (
                        own(far, k) + wide(from_below.at[far - 1, cut(k)])
                    ).astype(jnp.bfloat16)

                up(far, k).start()

            @pl.when(at.z > near)
            def _():
                pair(near, k).wait_recv()

                @pl.when(at.z == 3)
                def _():
                    held[near, cut(k)] = own(near, k).astype(jnp.bfloat16)

                @pl.when(at.z < 3)
                def _():
                    down(near, k).wait_recv()
                    held[near, cut(k)] = (
                        own(near, k) + wide(from_above.at[near, cut(k)])
                    ).astype(jnp.bfloat16)

                down(near, k).start()

            yield
    for z in range(4):
        for k in range(CHUNKS):

            @pl.when(at.z == z)
            def _():
                pair(z, k).wait_recv()
                total = own(z, k)
                if z > 0:
                    up(z, k).wait_recv()
                    total += wide(from_below.at[z - 1, cut(k)])
                if z < 3:
                    down(z, k).wait_recv()
                    total += wide(from_above.at[z, cut(k)])
                result[cut(k)] = total.astype(result.dtype)

    for z in range(4):
        for k in range(CHUNKS):
            pair(z, k).wait_send()
            if z > 0:
                pl.when(at.z < z)(lambda: up(z, k).wait_send())
            if z < 3:
                pl.when(at.z > z)(lambda: down(z, k).wait_send())


def half_of(ref, axis, which):
    size = ref.shape[axis] // 2
    return ref.at[pl.ds(which * size, size)] if axis == 0 else ref.at[:, pl.ds(which * size, size)]


def square_gather_sems():
    return [DMA((6,)), DMA((6,)), DMA]


def square_gather(at, own, full, sems, axis=0):
    send, recv, local_sem = sems
    count = own.shape[0]

    def part(r, which):
        return half_of(full.at[pl.ds(pl.multiple_of(r * count, count), count)], axis, which)

    def copy(i, src, r_of, which, to):
        return remote(src, part(r_of, which), send.at[i], recv.at[i], to, at.b)

    outs = [
        copy(0, half_of(own, axis, 0), at.r, 0, at.rx),
        copy(1, half_of(own, axis, 1), at.r, 1, at.ry),
        copy(2, half_of(own, axis, 1), at.r, 1, at.rx),
        copy(3, half_of(own, axis, 0), at.r, 0, at.ry),
    ]
    ins = [
        copy(0, part(at.rx, 0), at.rx, 0, at.rx),
        copy(1, part(at.ry, 1), at.ry, 1, at.ry),
        copy(2, part(at.rx, 1), at.rx, 1, at.rx),
        copy(3, part(at.ry, 0), at.ry, 0, at.ry),
        copy(4, part(at.rd, 0), at.rd, 0, at.ry),
        copy(5, part(at.rd, 1), at.rd, 1, at.rx),
    ]
    local = pltpu.make_async_copy(own, full.at[pl.ds(at.r * count, count)], local_sem)
    local.start()
    for out in outs:
        out.start()
    yield
    ins[0].wait_recv()
    outs.append(copy(4, part(at.rx, 0), at.rx, 0, at.ry))
    outs[4].start()
    yield
    ins[1].wait_recv()
    outs.append(copy(5, part(at.ry, 1), at.ry, 1, at.rx))
    outs[5].start()
    yield
    local.wait()
    for i in (2, 3, 4, 5):
        ins[i].wait_recv()
    for out in outs:
        out.wait_send()


def square_scatter_scratch(count, width, axis=0):
    half = (count // 2, width) if axis == 0 else (count, width // 2)
    piece = VMEM((count, width), jnp.bfloat16)
    part = VMEM(half, jnp.bfloat16)
    return [piece, piece, part, part, part, part, DMA((6,)), DMA((6,))]


def square_scatter(at, partial, result, scratch, axis=0):
    from_x, from_y, far_x, far_y, out_x, out_y, send, recv = scratch
    count = from_x.shape[0]

    def part(r, which):
        return half_of(partial.at[pl.ds(pl.multiple_of(r * count, count), count)], axis, which)

    def wide(ref):
        return ref[...].astype(jnp.float32)

    copies = [
        remote(part(at.rd, 0), far_x, send.at[0], recv.at[0], at.rx, at.b),
        remote(part(at.rd, 1), far_y, send.at[1], recv.at[1], at.ry, at.b),
        remote(part(at.rx, 0), half_of(from_x, axis, 0), send.at[2], recv.at[2], at.rx, at.b),
        remote(part(at.ry, 1), half_of(from_y, axis, 1), send.at[3], recv.at[3], at.ry, at.b),
        remote(out_y, half_of(from_y, axis, 0), send.at[4], recv.at[4], at.ry, at.b),
        remote(out_x, half_of(from_x, axis, 1), send.at[5], recv.at[5], at.rx, at.b),
    ]
    for copy in copies[:4]:
        copy.start()
    yield
    copies[0].wait_recv()
    out_y[...] = (wide(part(at.ry, 0)) + wide(far_x)).astype(jnp.bfloat16)
    copies[4].start()
    yield
    copies[1].wait_recv()
    out_x[...] = (wide(part(at.rx, 1)) + wide(far_y)).astype(jnp.bfloat16)
    copies[5].start()
    yield
    for i in (2, 3, 4, 5):
        copies[i].wait_recv()
    for which in range(2):
        total = (
            wide(part(at.r, which)) + wide(half_of(from_x, axis, which)) + wide(half_of(from_y, axis, which))
        )
        spot = half_of(result, axis, which)
        spot[...] = total.astype(result.dtype)
    for copy in copies:
        copy.wait_send()


def exchange_sems(parts=1):
    return [DMA((7, parts)), DMA((7, parts)), DMA((parts,))]


def exchange(at, take, put, sems, parts=1):
    send, recv, local_sem = sems
    locals_ = [
        pltpu.make_async_copy(take(at.b, p), put(at.b, p), local_sem.at[p]) for p in range(parts)
    ]
    outs, ins = [], []
    for k in (4, 3, 5, 2, 6, 1, 7):
        to, source = lax.rem(at.b + k, 8), lax.rem(at.b + 8 - k, 8)
        for p in range(parts):
            pair = (send.at[k - 1, p], recv.at[k - 1, p])
            outs.append(remote(take(to, p), put(at.b, p), *pair, at.r, to))
            ins.append(remote(put(source, p), put(source, p), *pair, at.r, source))
    for copy in locals_ + outs:
        copy.start()
    yield
    for copy in ins:
        copy.wait_recv()
    for copy in locals_:
        copy.wait()
    for copy in outs:
        copy.wait_send()


def call(kernel, ins, outs, scratch, number, *args):
    return pl.pallas_call(
        kernel,
        out_shape=[jax.ShapeDtypeStruct(shape, kind) for shape, kind, _ in outs],
        in_specs=[pl.BlockSpec(memory_space=space) for space in ins],
        out_specs=[pl.BlockSpec(memory_space=space) for _, _, space in outs],
        scratch_shapes=scratch,
        compiler_params=pltpu.CompilerParams(
            collective_id=number, has_side_effects=True, vmem_limit_bytes=LIMIT
        ),
    )(*args)


def vector_gather(at, own, full, sems):
    send, recv, local_sem = sems
    mine = 8 * at.r + at.b
    outs, ins = [], []
    for k in range(1, 8):
        to, source = lax.rem(at.b + k, 8), lax.rem(at.b + 8 - k, 8)
        outs.append(remote(own, full.at[mine], send.at[k - 1], recv.at[k - 1], at.r, to))
        piece = full.at[8 * at.r + source]
        ins.append(remote(piece, piece, send.at[k - 1], recv.at[k - 1], at.r, source))
    local = pltpu.make_async_copy(own, full.at[mine], local_sem)
    local.start()
    for out in outs:
        out.start()
    yield
    for copy in ins:
        copy.wait_recv()
    local.wait()
    group = full.at[pl.ds(8 * at.r, 8)]
    later = []
    for i, row in enumerate((at.rx, at.ry, at.rd)):
        outs.append(remote(group, group, send.at[7 + i], recv.at[7 + i], row, at.b))
        outs[-1].start()
        theirs = full.at[pl.ds(8 * row, 8)]
        later.append(remote(theirs, theirs, send.at[7 + i], recv.at[7 + i], row, at.b))
    yield
    for copy in later:
        copy.wait_recv()
    for out in outs:
        out.wait_send()


def start_kernel(
    x_ref, vector_ref, project_ref, down_ref,
    vectors, normed, pieces, w_project, w_down,
    unit, own, vector_sems, exchange_sem, square_sem, down_sem, line_sems,
):
    at = Place()
    at.barrier(diagonal=True)
    width = x_ref.shape[1]
    vector_job = vector_gather(at, vector_ref, vectors, vector_sems)
    next(vector_job)
    inner = w_project.shape[1] // 3
    depth = project_ref.shape[0]
    project_job = exchange(
        at,
        lambda b, p: project_ref.at[:, pl.ds(pl.multiple_of(p * width + b * inner, inner), inner)],
        lambda b, p: pieces.at[
            pl.ds(pl.multiple_of(b * depth, depth), depth), pl.ds(p * inner, inner)
        ],
        exchange_sem,
        3,
    )
    next(project_job)
    down_job = square_gather(at, down_ref, w_down, down_sem, axis=1)
    next(down_job)
    x = x_ref[...].astype(jnp.float32)
    centered = x - jnp.mean(x, axis=1, keepdims=True)
    unit[...] = centered * lax.rsqrt(jnp.mean(centered * centered, axis=1, keepdims=True) + epsilon)
    drive(vector_job)
    for tile in range(width // 128):
        lanes = slice(tile * 128, tile * 128 + 128)
        both = vectors[2 * tile].astype(jnp.float32) + vectors[2 * tile + 1].astype(jnp.float32)
        own[:, lanes] = (unit[:, lanes] * both[0:1] + both[1:2]).astype(jnp.bfloat16)
    line_job = line_gather(at, own, normed, line_sems)
    next(line_job)
    drive(project_job)
    square_job = square_gather(at, pieces, w_project, square_sem)
    drive(square_job, line_job, down_job)


def pack_sems(groups):
    flat, spans = [], []
    for group in groups:
        spans.append((len(flat), len(flat) + len(group)))
        flat += group
    return flat, spans


def grouped(kernel, lead, spans):
    def run(*refs):
        rest = refs[lead:]
        return kernel(*refs[:lead], *[rest[a:b] for a, b in spans])

    return run


def start_call(x, vector, project, down):
    rows, width = x.shape
    depth = project.shape[0]
    inner = project.shape[1] // 8
    bf = jnp.bfloat16
    groups = [
        [DMA((10,)), DMA((10,)), DMA], exchange_sems(3), square_gather_sems(), square_gather_sems(),
        line_gather_sems(),
    ]
    flat, spans = pack_sems(groups)
    outs = [
        ((32, 16, 128), bf, VMEM), ((8 * rows, width), bf, HBM), ((8 * depth, inner), bf, HBM),
        ((32 * depth, inner), bf, HBM), ((4 * down.shape[0], width), bf, HBM),
    ]
    scratch = [VMEM((rows, width), jnp.float32), VMEM((rows, width), bf)] + flat
    vectors, normed, _, w_project, w_down = call(
        grouped(start_kernel, 11, spans), [VMEM, VMEM, HBM, HBM], outs, scratch, 0, x, vector, project, down
    )
    return vectors, normed, w_project, w_down


def turned(columns, cosine, minus, plus):
    half = ROT // 2
    return (
        columns * cosine
        + pltpu.roll(columns, 128 - half, 1) * minus
        + pltpu.roll(columns, half, 1) * plus
    )


def score_mask(first_row, rows, keys, start):
    row = lax.broadcasted_iota(jnp.int32, (rows, keys), 0) + first_row
    col = lax.broadcasted_iota(jnp.int32, (rows, keys), 1)
    return (col <= row) & (col >= start)


QROWS = 256


def attend_forward_kernel(
    x_ref, w_ref, bias, start, cosine, minus, plus, gate_up,
    queries, keys, values, attended, log_total, mixed_heads, gate_up_all,
    low, own_sems, gate_up_sems,
):
    at = Place()
    at.barrier()
    length, local = queries.shape
    depth = gate_up.shape[1]
    gate_up_job = exchange(
        at, lambda b, p: gate_up.at[b], lambda b, p: gate_up_all.at[b], gate_up_sems
    )
    next(gate_up_job)
    scale = 1.0 / math.sqrt(local * 8 // HEADS)
    blocks = length // QROWS

    @pl.loop(0, blocks)
    def _(i):
        rows = pl.ds(pl.multiple_of(i * QROWS, QROWS), QROWS)
        mixed = dot(x_ref[rows], w_ref[...], ((1,), (0,))) + bias[...]
        tables = (cosine[rows], minus[rows], plus[rows])
        for pair in range(local // 128):
            lanes = slice(pair * 128, pair * 128 + 128)
            queries[rows, lanes] = turned(mixed[:, lanes], *tables).astype(jnp.bfloat16)
            shifted = slice(local + pair * 128, local + pair * 128 + 128)
            keys[rows, lanes] = turned(mixed[:, shifted], *tables).astype(jnp.bfloat16)
        values[rows] = mixed[:, 2 * local :].astype(jnp.bfloat16)

    send, recv, local_sem = own_sems

    def deliver(to):
        rows = low.at[pl.ds(to * 128, 128)]
        spot = mixed_heads.at[:, pl.ds(pl.multiple_of(at.b * local, local), local)]
        return remote(rows, spot, send.at[to], recv.at[at.b], at.r, to)

    for i in range(blocks):
        rows = slice(i * QROWS, (i + 1) * QROWS)
        count = (i + 1) * QROWS

        @pl.loop(0, local // 128)
        def _(pair):
            lanes = pl.ds(pl.multiple_of(pair * 128, 128), 128)
            lane = lax.broadcasted_iota(jnp.int32, (QROWS, 128), 1)
            q, k, v = queries[rows, lanes], keys[:count, lanes], values[:count, lanes]
            allowed = score_mask(i * QROWS, QROWS, count, start[rows])
            found = []
            for head in range(2):
                mine = (lane >= 64) if head else (lane < 64)
                scores = dot(jnp.where(mine, q, jnp.zeros_like(q)), k, ((1,), (1,))) * scale
                scores = jnp.where(allowed, scores, masked_value)
                top = jnp.max(scores, axis=1, keepdims=True)
                weights = jnp.exp(scores - top)
                total = jnp.sum(weights, axis=1, keepdims=True)
                found.append(
                    (dot(weights.astype(jnp.bfloat16), v, ((1,), (0,))) / total, top + jnp.log(total))
                )
            both = jnp.where(lane < 64, found[0][0], found[1][0])
            attended[rows, lanes] = both
            low[rows, lanes] = both.astype(jnp.bfloat16)
            log_total[rows, lanes] = jnp.where(lane < 64, found[0][1], found[1][1])

        for to in range(i * QROWS // 128, (i + 1) * QROWS // 128):
            pl.when(at.b != to)(lambda: deliver(to).start())

            @pl.when(at.b == to)
            def _():
                pltpu.make_async_copy(
                    low.at[pl.ds(to * 128, 128)],
                    mixed_heads.at[:, pl.ds(pl.multiple_of(at.b * local, local), local)],
                    local_sem,
                ).start()

    for source in range(8):

        @pl.when(at.b != source)
        def _():
            spot = mixed_heads.at[:, pl.ds(source * local, local)]
            remote(spot, spot, send.at[source], recv.at[source], at.r, source).wait_recv()

        @pl.when(at.b == source)
        def _():
            pltpu.make_async_copy(
                low.at[pl.ds(source * 128, 128)],
                mixed_heads.at[:, pl.ds(source * local, local)],
                local_sem,
            ).wait()

    drive(gate_up_job)
    for to in range(8):
        pl.when(at.b != to)(lambda: deliver(to).wait_send())


def attend_forward(x, w, bias, start, tables, gate_up):
    length, local = x.shape[0], w.shape[1] // 3
    bf, f32 = jnp.bfloat16, jnp.float32
    flat, spans = pack_sems([[DMA((8,)), DMA((8,)), DMA], exchange_sems()])
    outs = [((length, local), bf, VMEM)] * 3 + [((length, local), f32, VMEM)] * 2
    outs += [((length // 8, 8 * local), bf, VMEM), (gate_up.shape, bf, HBM)]
    return call(
        grouped(attend_forward_kernel, 16, spans), [VMEM] * 7 + [HBM], outs,
        [VMEM((length, local), bf)] + flat, 1, x, w, bias, start, *tables, gate_up,
    )


def second_gather_kernel(own, gate_up, normed, w_gate_up, line_sems, square_sems):
    at = Place()
    at.barrier()
    drive(
        line_gather(at, own, normed, line_sems), square_gather(at, gate_up, w_gate_up, square_sems)
    )


def second_gather(own, gate_up):
    flat, spans = pack_sems([line_gather_sems(), square_gather_sems()])
    bf = jnp.bfloat16
    outs = [
        ((8 * own.shape[0], own.shape[1]), bf, HBM), ((4 * gate_up.shape[0], gate_up.shape[1]), bf, HBM)
    ]
    return call(
        grouped(second_gather_kernel, 4, spans), [HBM, HBM], outs, flat, 2, own, gate_up
    )


def reduce_kernel(axis, partial, weight, result, weight_result, line_scratch, square_scratch):
    at = Place()
    at.barrier()
    drive(
        line_scatter(at, partial, result, line_scratch),
        square_scatter(at, weight, weight_result, square_scratch, axis),
    )


def reduce_call(partial, weight, number, axis, kind):
    rows, width = partial.shape[0] // 8, partial.shape[1]
    owned = (weight.shape[0] // 4, weight.shape[1])
    flat, spans = pack_sems([line_scatter_scratch(rows, width), square_scatter_scratch(*owned, axis)])
    outs = [((rows, width), jnp.float32, VMEM), (owned, kind, VMEM)]
    return call(
        grouped(functools.partial(reduce_kernel, axis), 4, spans), [VMEM, VMEM], outs, flat, number,
        partial, weight,
    )


def attend_backward_kernel(
    grad_rows, queries, keys, values, attended, log_total, start, cosine, minus, plus, weight,
    grad_mixed, weight_result,
    grad, keys_sum, values_sum, own_sems, square_scratch,
):
    at = Place()
    at.barrier()
    length, local = queries.shape
    scale = 1.0 / math.sqrt(local * 8 // HEADS)
    blocks = length // QROWS
    own_job = exchange(
        at,
        lambda b, p: grad_rows.at[:, pl.ds(pl.multiple_of(b * local, local), local)],
        lambda b, p: grad.at[pl.ds(pl.multiple_of(b * 128, 128), 128)],
        own_sems,
    )
    next(own_job)
    weight_job = square_scatter(at, weight, weight_result, square_scratch)
    next(weight_job)
    keys_sum[...] = jnp.zeros_like(keys_sum)
    values_sum[...] = jnp.zeros_like(values_sum)
    drive(own_job)
    for i in range(blocks):
        rows = slice(i * QROWS, (i + 1) * QROWS)
        count = (i + 1) * QROWS

        @pl.loop(0, local // 128)
        def _(pair):
            lanes = pl.ds(pl.multiple_of(pair * 128, 128), 128)
            lane = lax.broadcasted_iota(jnp.int32, (QROWS, 128), 1)
            q, g = queries[rows, lanes], grad[rows, lanes]
            k, v = keys[:count, lanes], values[:count, lanes]
            allowed = score_mask(i * QROWS, QROWS, count, start[rows])
            product = g.astype(jnp.float32) * attended[rows, lanes]
            logs = log_total[rows, lanes]
            queries_part, keys_part, values_part = [], [], []
            for head in range(2):
                mine = (lane >= 64) if head else (lane < 64)
                q_head = jnp.where(mine, q, jnp.zeros_like(q))
                g_head = jnp.where(mine, g, jnp.zeros_like(g))
                delta = jnp.sum(jnp.where(mine, product, 0.0), axis=1, keepdims=True)
                log_head = jnp.max(jnp.where(mine, logs, masked_value), axis=1, keepdims=True)
                scores = dot(q_head, k, ((1,), (1,))) * scale
                probs = jnp.exp(jnp.where(allowed, scores - log_head, masked_value))
                grad_probs = dot(g_head, v, ((1,), (1,)))
                grad_scores = (probs * (grad_probs - delta) * scale).astype(jnp.bfloat16)
                queries_part.append(dot(grad_scores, k, ((1,), (0,))))
                keys_part.append(dot(grad_scores, q_head, ((0,), (0,))))
                values_part.append(dot(probs.astype(jnp.bfloat16), g_head, ((0,), (0,))))
            both = jnp.where(lane < 64, queries_part[0], queries_part[1])
            tables = (cosine[rows], -minus[rows], -plus[rows])
            grad_mixed[rows, lanes] = turned(both, *tables).astype(jnp.bfloat16)
            keys_sum[:count, lanes] += keys_part[0] + keys_part[1]
            values_sum[:count, lanes] += values_part[0] + values_part[1]

        next(weight_job, None)

    @pl.loop(0, blocks)
    def _(i):
        rows = pl.ds(pl.multiple_of(i * QROWS, QROWS), QROWS)
        tables = (cosine[rows], -minus[rows], -plus[rows])
        for pair in range(local // 128):
            lanes = slice(pair * 128, pair * 128 + 128)
            shifted = slice(local + pair * 128, local + pair * 128 + 128)
            grad_mixed[rows, shifted] = turned(keys_sum[rows, lanes], *tables).astype(jnp.bfloat16)
        grad_mixed[rows, slice(2 * local, 3 * local)] = values_sum[rows].astype(jnp.bfloat16)

    drive(weight_job)


def attend_backward(grad_rows, queries, keys, values, attended, log_total, start, tables, weight):
    length, local = queries.shape
    bf, f32 = jnp.bfloat16, jnp.float32
    owned = (weight.shape[0] // 4, weight.shape[1])
    flat, spans = pack_sems([exchange_sems(), square_scatter_scratch(*owned)])
    outs = [((length, 3 * local), bf, VMEM), (owned, bf, VMEM)]
    scratch = [VMEM((length, local), bf), VMEM((length, local), f32), VMEM((length, local), f32)]
    return call(
        grouped(attend_backward_kernel, 16, spans), [VMEM] * 11, outs, scratch + flat, 4,
        grad_rows, queries, keys, values, attended, log_total, start, *tables, weight,
    )


def owners_kernel(
    project, gate_up, vectors, project_out, gate_up_out, vector_out,
    arrived, summed, rows_in, project_sems, gate_up_sems, vector_sems, row_sems,
):
    at = Place()
    at.barrier(diagonal=True)
    vector_job = exchange(at, lambda b, p: vectors.at[b], lambda b, p: arrived.at[b], vector_sems)
    next(vector_job)
    project_job = exchange(
        at, lambda b, p: project.at[b], lambda b, p: project_out.at[b], project_sems
    )
    next(project_job)
    gate_up_job = exchange(
        at, lambda b, p: gate_up.at[b], lambda b, p: gate_up_out.at[b], gate_up_sems
    )
    next(gate_up_job)
    drive(vector_job)
    summed[...] = jnp.sum(arrived[...], axis=0)
    send, recv = row_sems
    copies = [
        remote(summed.at[row], rows_in.at[i], send.at[i], recv.at[i], row, at.b)
        for i, row in enumerate((at.rx, at.ry, at.rd))
    ]
    for copy in copies:
        copy.start()
    for copy in copies:
        copy.wait()
    vector_out[...] = summed[at.r] + rows_in[0] + rows_in[1] + rows_in[2]
    drive(project_job, gate_up_job)


def owners_call(project, gate_up, vectors):
    f32 = jnp.float32
    flat, spans = pack_sems(
        [exchange_sems(), exchange_sems(), exchange_sems(), [DMA((3,)), DMA((3,))]]
    )
    tail = vectors.shape[1:]
    outs = [
        (project.shape, project.dtype, HBM), (gate_up.shape, gate_up.dtype, HBM), (tail[1:], f32, VMEM)
    ]
    scratch = [VMEM((8,) + tail, f32), VMEM(tail, f32), VMEM((3,) + tail[1:], f32)]
    return call(
        grouped(owners_kernel, 9, spans), [HBM, HBM, VMEM], outs, scratch + flat, 6,
        project, gate_up, vectors,
    )


def fast_body(
    tokens, segments, cotangent, attend_gain, attend_shift, project_weight, project_bias,
    output_weight, feed_gain, feed_shift, gate_weight, up_weight, down_weight,
):
    bf, f32 = jnp.bfloat16, jnp.float32
    own_rows, width = tokens.shape[1], tokens.shape[2]
    length = own_rows * 8
    head_width = width // HEADS
    local = width // 8
    hidden = down_weight.shape[0]
    shard = attend_gain.shape[0]
    r, b = lax.axis_index("rows"), lax.axis_index("blk")

    small = jnp.stack([attend_gain, attend_shift, feed_gain, feed_shift])
    zeros = jnp.zeros_like(small)
    small = jnp.where(
        b % 2 == 0, jnp.concatenate([small, zeros], 1), jnp.concatenate([zeros, small], 1)
    )
    rest = jnp.pad(project_bias, (0, 64)).reshape(2, 128)
    vector = jnp.concatenate(
        [small, rest, segments.astype(bf), jnp.zeros((9, 128), bf)], axis=0
    )

    def pieces_of(weight):
        depth = weight.shape[0]
        return weight.reshape(depth, 4, 8, hidden).transpose(2, 0, 1, 3).reshape(8, depth, 4 * hidden)

    w_out = lax.all_gather(output_weight, BOTH, axis=0, tiled=True)
    gate_up = jnp.concatenate([pieces_of(gate_weight), pieces_of(up_weight)], axis=2)

    vectors, normed_first, w_project, w_down = start_call(
        tokens[0], vector, project_weight, down_weight
    )
    grad_out = gather_blk(cotangent[0])

    def whole(row):
        pairs = vectors[:, row].reshape(16, 2, 128).astype(f32)
        return (pairs[:, 0] + pairs[:, 1]).reshape(-1)

    a_gain, f_gain, f_shift = whole(0), whole(2), whole(3)
    bias = vectors[:, 4:6].reshape(32, 256)[:, : 3 * shard].reshape(3, 8, local)
    bias = lax.dynamic_index_in_dim(bias, b, 1, False).reshape(1, -1).astype(f32)
    doc = lax.dynamic_slice_in_dim(vectors[:, 6], 8 * r, 8, 0).reshape(-1).astype(f32)
    starts = jnp.sum((doc[None, :] < doc[:, None]).astype(jnp.int32), axis=1)
    places = (jnp.arange(length, dtype=jnp.int32) - starts).astype(f32)
    half = ROT // 2
    frequency = jnp.power(rotary_base, -jnp.arange(half, dtype=jnp.int32).astype(f32) / half)
    angles = frequency[:, None] * places[None, :]
    cosine, sine = jnp.cos(angles), jnp.sin(angles)
    gap = jnp.zeros((head_width - ROT, length), f32)
    eight = jnp.zeros((half, length), f32)

    def table(first, second, fill):
        one = jnp.concatenate([first, second, gap + fill], axis=0)
        return jnp.transpose(jnp.concatenate([one, one], axis=0))

    tables = (table(cosine, cosine, 1.0), table(-sine, eight, 0.0), table(eight, sine, 0.0))
    start = starts[:, None]

    queries, keys, values, attended, log_total, attended_low, gate_up = attend_forward(
        normed_first, w_project, bias, start, tables, gate_up
    )
    inputs = tokens[0].astype(f32)
    resid_mid = inputs + dot(attended_low, w_out, ((1,), (0,)))
    unit_second, inverse_second = norm_stats(resid_mid)
    normed_second, w_gate_up = second_gather(
        (unit_second * f_gain + f_shift).astype(bf), gate_up.reshape(8 * shard, 8 * hidden)
    )
    both = dot(normed_second, w_gate_up, ((1,), (0,)))
    gate_value, up_value = both[:, : 4 * hidden], both[:, 4 * hidden :]
    gate_sigmoid = jax.nn.sigmoid(gate_value)
    silu = gate_value * gate_sigmoid
    hidden_low = (silu * up_value).astype(bf)
    grad_hidden = dot(grad_out, w_down, ((1,), (1,)))
    grad_gate = grad_hidden * up_value * gate_sigmoid * (1.0 + gate_value * (1.0 - gate_sigmoid))
    grad_both = jnp.concatenate([grad_gate.astype(bf), (grad_hidden * silu).astype(bf)], axis=1)
    grad_second = dot(grad_both, w_gate_up, ((1,), (1,))).astype(bf)
    down_partial = dot(hidden_low, grad_out, ((0,), (0,))).astype(bf)
    grad_second, down_grad = reduce_call(grad_second, down_partial, 3, 1, f32)
    output = (resid_mid + scatter_blk(dot(hidden_low, w_down, ((1,), (0,))))).astype(bf)
    gate_up_partial = dot(normed_second, grad_both, ((0,), (0,))).astype(bf)

    mid_part, f_gain_part, f_shift_part = norm_back(grad_second, unit_second, inverse_second, f_gain)
    grad_mid = cotangent[0].astype(f32) + mid_part
    grad_mid_low = grad_mid.astype(bf)
    grad_attended = dot(grad_mid_low, w_out, ((1,), (1,))).astype(bf)
    grad_mixed, gate_up_grad = attend_backward(
        grad_attended, queries, keys, values, attended, log_total, start, tables, gate_up_partial
    )
    out_grad = lax.psum_scatter(
        dot(attended_low, grad_mid_low, ((0,), (0,))).astype(bf), BOTH, scatter_dimension=0, tiled=True
    ).astype(f32)
    grad_first = dot(grad_mixed, w_project, ((1,), (1,))).astype(bf)
    project_partial = dot(normed_first, grad_mixed, ((0,), (0,))).astype(bf)
    grad_first, project_grad = reduce_call(grad_first, project_partial, 5, 0, bf)
    unit_first, inverse_first = norm_stats(inputs)
    input_part, a_gain_part, a_shift_part = norm_back(grad_first, unit_first, inverse_first, a_gain)
    grad_tokens = grad_mid + input_part

    bias_part = jnp.sum(grad_mixed.astype(f32), axis=0).reshape(3, 1, local)
    bias_part = jnp.where(jnp.arange(8)[None, :, None] == b, bias_part, 0.0)
    bias_part = jnp.pad(bias_part.reshape(32, 3 * shard), ((0, 0), (0, 64))).reshape(32, 2, 128)
    gains = jnp.stack(
        [part.reshape(32, shard) for part in (a_gain_part, a_shift_part, f_gain_part, f_shift_part)], axis=1
    )
    gains = jnp.pad(gains, ((0, 0), (0, 0), (0, 64)))
    sums = jnp.concatenate([gains, bias_part, jnp.zeros((32, 2, 128), f32)], axis=1)
    sums = sums.reshape(4, 8, 8, 128).transpose(1, 0, 2, 3)
    project_grad, gate_up_grad, vector = owners_call(
        project_grad.reshape(8, shard, 3 * local), gate_up_grad.reshape(8, shard, 8 * hidden), sums
    )

    def owned(pieces, parts):
        inner = pieces.shape[2] // parts
        pieces = pieces.reshape(8, shard, parts, inner).transpose(1, 2, 0, 3)
        return pieces.reshape(shard, 8 * parts * inner).astype(f32)

    return (
        output[None], grad_tokens[None], vector[0, :shard], vector[1, :shard],
        owned(project_grad, 3), vector[4:6].reshape(-1)[: 3 * shard], out_grad,
        vector[2, :shard], vector[3, :shard],
        owned(gate_up_grad[:, :, : 4 * hidden], 4), owned(gate_up_grad[:, :, 4 * hidden :], 4), down_grad,
    )


def solution(mesh):
    tokens = P("rows", "blk", None)
    vector, matrix = P(BOTH), P(BOTH, None)
    in_specs = (
        tokens, P("rows", "blk"), tokens, vector, vector, matrix, vector, matrix, vector, vector,
        matrix, matrix, matrix,
    )
    out_specs = (
        tokens, tokens, vector, vector, matrix, vector, matrix, vector, vector, matrix, matrix, matrix,
    )
    if (mesh.shape["rows"], mesh.shape["blk"]) == (4, 8):
        body = fast_body
    else:
        body = make_body(mesh.shape["rows"], mesh.shape["blk"])
    return jax.shard_map(body, mesh=mesh, in_specs=in_specs, out_specs=out_specs, check_vma=False)
```

```python
import functools
import math

import jax
import jax.numpy as jnp
from jax import lax
from jax.experimental import pallas as pl
from jax.experimental.pallas import tpu as pltpu
from jax.sharding import PartitionSpec as P

HEADS = 32
ROT = 16
BOTH = ("rows", "blk")

epsilon = 1e-05
rotary_base = 10000.0
masked_value = -1e30


def dot(left, right, contract):
    return lax.dot_general(
        left, right, (contract, ((), ())), preferred_element_type=jnp.float32
    )


def norm_stats(inputs):
    row_mean = jnp.mean(inputs, axis=-1, keepdims=True)
    centered = inputs - row_mean
    variance = jnp.mean(centered * centered, axis=-1, keepdims=True)
    inverse = lax.rsqrt(variance + epsilon)
    return centered * inverse, inverse


def norm_back(incoming, unit, inverse, gain):
    gain_part = jnp.sum(incoming * unit, axis=0)
    shift_part = jnp.sum(incoming, axis=0)
    unit_grad = incoming * gain
    grad = inverse * (
        unit_grad
        - jnp.mean(unit_grad, axis=-1, keepdims=True)
        - unit * jnp.mean(unit_grad * unit, axis=-1, keepdims=True)
    )
    return grad, gain_part, shift_part


def rotate(columns, cosine, sine, head_width):
    half = cosine.shape[1]
    heads = columns.reshape(columns.shape[0], -1, head_width)
    cosine, sine = cosine[:, None, :], sine[:, None, :]
    first, second, rest = heads[..., :half], heads[..., half : 2 * half], heads[..., 2 * half :]
    return jnp.concatenate(
        [first * cosine - second * sine, second * cosine + first * sine, rest], axis=-1
    ).reshape(columns.shape)


def gather_blk(rows):
    return lax.all_gather(rows, "blk", axis=0, tiled=True)


def scatter_blk(partial):
    return lax.psum_scatter(
        partial.astype(jnp.bfloat16), "blk", scatter_dimension=0, tiled=True
    ).astype(jnp.float32)


def gather_rows(shard):
    return lax.all_gather(shard, "rows", axis=0, tiled=True)


def scatter_rows(partial):
    return lax.psum_scatter(
        partial.astype(jnp.bfloat16), "rows", scatter_dimension=0, tiled=True
    )


def exchange_blk(pieces):
    return lax.all_to_all(pieces, "blk", split_axis=0, concat_axis=0, tiled=True)


def make_body(group, ranks):
    def columns_of(shard, parts, inner):
        depth = shard.shape[0]
        pieces = shard.reshape(depth, parts, ranks, inner).transpose(2, 0, 1, 3)
        pieces = exchange_blk(pieces.reshape(ranks, depth, parts * inner))
        return gather_rows(pieces.reshape(ranks * depth, parts * inner))

    def columns_back(grad, parts, inner):
        owned = scatter_rows(grad)
        depth = owned.shape[0] // ranks
        pieces = exchange_blk(owned.reshape(ranks, depth, parts * inner))
        pieces = pieces.reshape(ranks, depth, parts, inner).transpose(1, 2, 0, 3)
        return pieces.reshape(depth, parts * ranks * inner).astype(jnp.float32)

    def body(
        tokens,
        segments,
        cotangent,
        attend_gain,
        attend_shift,
        project_weight,
        project_bias,
        output_weight,
        feed_gain,
        feed_shift,
        gate_weight,
        up_weight,
        down_weight,
    ):
        own_rows, width = tokens.shape[1], tokens.shape[2]
        length = own_rows * ranks
        head_width = width // HEADS
        local_heads = HEADS // ranks
        local_width = local_heads * head_width
        score_scale = 1.0 / math.sqrt(head_width)
        hidden_shard = down_weight.shape[0]
        shard = attend_gain.shape[0]
        me = lax.axis_index("blk")

        packed = jnp.concatenate(
            [
                attend_gain,
                attend_shift,
                feed_gain,
                feed_shift,
                project_bias,
                segments[0].astype(jnp.bfloat16),
            ]
        )
        packed = lax.all_gather(packed, BOTH, axis=0, tiled=False)
        a_gain = packed[:, :shard].reshape(-1).astype(jnp.float32)
        a_shift = packed[:, shard : 2 * shard].reshape(-1).astype(jnp.float32)
        f_gain = packed[:, 2 * shard : 3 * shard].reshape(-1).astype(jnp.float32)
        f_shift = packed[:, 3 * shard : 4 * shard].reshape(-1).astype(jnp.float32)
        bias = packed[:, 4 * shard : 7 * shard].reshape(3, ranks, local_width)
        bias = lax.dynamic_index_in_dim(bias, me, 1, False).reshape(-1).astype(jnp.float32)
        doc = packed[:, 7 * shard :].reshape(group, ranks * own_rows)
        doc = lax.dynamic_index_in_dim(doc, lax.axis_index("rows"), 0, False)

        w_project = columns_of(project_weight, 3, local_width)
        w_gate = columns_of(gate_weight, group, hidden_shard)
        w_up = columns_of(up_weight, group, hidden_shard)
        w_down = gather_rows(down_weight)
        w_out = lax.all_gather(output_weight, BOTH, axis=0, tiled=True)

        doc = doc.astype(jnp.int32)
        index = jnp.arange(length, dtype=jnp.int32)
        places = index - jnp.sum((doc[None, :] < doc[:, None]).astype(jnp.int32), axis=1)
        half = ROT // 2
        frequency = jnp.power(
            rotary_base, -jnp.arange(half, dtype=jnp.int32).astype(jnp.float32) / half
        )
        angles = places.astype(jnp.float32)[:, None] * frequency
        cosine, sine = jnp.cos(angles), jnp.sin(angles)
        mask = ((index[None, :] <= index[:, None]) & (doc[None, :] == doc[:, None]))[None]

        inputs = tokens[0].astype(jnp.float32)
        unit_first, inverse_first = norm_stats(inputs)
        normed_first = gather_blk((unit_first * a_gain + a_shift).astype(jnp.bfloat16))
        grad_out = gather_blk(cotangent[0])
        mixed = dot(normed_first, w_project, ((1,), (0,))) + bias
        queries = rotate(mixed[:, :local_width], cosine, sine, head_width).astype(jnp.bfloat16)
        keys = rotate(mixed[:, local_width : 2 * local_width], cosine, sine, head_width)
        keys = keys.astype(jnp.bfloat16)
        values = mixed[:, 2 * local_width :].astype(jnp.bfloat16)
        q_heads = queries.reshape(length, local_heads, head_width)
        k_heads = keys.reshape(length, local_heads, head_width)
        v_heads = values.reshape(length, local_heads, head_width)
        scores = jnp.einsum("qhd,khd->hqk", q_heads, k_heads, preferred_element_type=jnp.float32)
        scores = jnp.where(mask, scores * score_scale, masked_value)
        top = jnp.max(scores, axis=2, keepdims=True)
        weights = jnp.where(mask, jnp.exp(scores - top), 0.0)
        total = jnp.sum(weights, axis=2, keepdims=True)
        attended = jnp.einsum(
            "hqk,khd->qhd",
            weights.astype(jnp.bfloat16),
            v_heads,
            preferred_element_type=jnp.float32,
        ) / jnp.transpose(total[:, :, 0])[:, :, None]
        log_total = top + jnp.log(total)
        attended_flat = attended.reshape(length, local_width)
        attended_low = exchange_blk(
            attended_flat.astype(jnp.bfloat16).reshape(ranks, own_rows, local_width)
        )
        attended_low = attended_low.transpose(1, 0, 2).reshape(own_rows, width)
        resid_mid = inputs + dot(attended_low, w_out, ((1,), (0,)))

        unit_second, inverse_second = norm_stats(resid_mid)
        normed_second = gather_blk((unit_second * f_gain + f_shift).astype(jnp.bfloat16))
        gate_value = dot(normed_second, w_gate, ((1,), (0,)))
        up_value = dot(normed_second, w_up, ((1,), (0,)))
        gate_sigmoid = jax.nn.sigmoid(gate_value)
        silu = gate_value * gate_sigmoid
        hidden = (silu * up_value).astype(jnp.bfloat16)
        output = (resid_mid + scatter_blk(dot(hidden, w_down, ((1,), (0,))))).astype(jnp.bfloat16)

        grad_hidden = dot(grad_out, w_down, ((1,), (1,)))
        grad_gate = (
            grad_hidden * up_value * gate_sigmoid * (1.0 + gate_value * (1.0 - gate_sigmoid))
        ).astype(jnp.bfloat16)
        grad_up = (grad_hidden * silu).astype(jnp.bfloat16)
        grad_second = scatter_blk(
            dot(grad_gate, w_gate, ((1,), (1,))) + dot(grad_up, w_up, ((1,), (1,)))
        )
        down_grad = scatter_rows(dot(hidden, grad_out, ((0,), (0,)))).astype(jnp.float32)
        gate_grad = columns_back(dot(normed_second, grad_gate, ((0,), (0,))), group, hidden_shard)
        up_grad = columns_back(dot(normed_second, grad_up, ((0,), (0,))), group, hidden_shard)
        mid_part, f_gain_part, f_shift_part = norm_back(
            grad_second, unit_second, inverse_second, f_gain
        )
        grad_mid = cotangent[0].astype(jnp.float32) + mid_part
        grad_mid_low = grad_mid.astype(jnp.bfloat16)
        grad_attended = dot(grad_mid_low, w_out, ((1,), (1,))).astype(jnp.bfloat16)
        grad_attended = exchange_blk(
            grad_attended.reshape(own_rows, ranks, local_width).transpose(1, 0, 2)
        ).reshape(length, local_width)
        out_grad = lax.psum_scatter(
            dot(attended_low, grad_mid_low, ((0,), (0,))).astype(jnp.bfloat16),
            BOTH,
            scatter_dimension=0,
            tiled=True,
        ).astype(jnp.float32)

        g_heads = grad_attended.reshape(length, local_heads, head_width)
        delta = jnp.transpose(jnp.sum(g_heads.astype(jnp.float32) * attended, axis=2))
        probs = jnp.where(mask, jnp.exp(scores - log_total), 0.0)
        values_grad = jnp.einsum(
            "hqk,qhd->khd", probs.astype(jnp.bfloat16), g_heads, preferred_element_type=jnp.float32
        )
        grad_probs = jnp.einsum("qhd,khd->hqk", g_heads, v_heads, preferred_element_type=jnp.float32)
        grad_scores = (probs * (grad_probs - delta[:, :, None]) * score_scale).astype(jnp.bfloat16)
        grad_queries = jnp.einsum(
            "hqk,khd->qhd", grad_scores, k_heads, preferred_element_type=jnp.float32
        )
        keys_grad = jnp.einsum(
            "hqk,qhd->khd", grad_scores, q_heads, preferred_element_type=jnp.float32
        )
        grad_mixed = jnp.concatenate(
            [
                rotate(grad_queries.reshape(length, local_width), cosine, -sine, head_width),
                rotate(keys_grad.reshape(length, local_width), cosine, -sine, head_width),
                values_grad.reshape(length, local_width),
            ],
            axis=1,
        ).astype(jnp.bfloat16)
        grad_first = scatter_blk(dot(grad_mixed, w_project, ((1,), (1,))))
        project_grad = columns_back(
            dot(normed_first, grad_mixed, ((0,), (0,))), 3, local_width
        )
        bias_part = jnp.sum(grad_mixed.astype(jnp.float32), axis=0).reshape(3, 1, local_width)
        bias_part = jnp.where(jnp.arange(ranks)[None, :, None] == me, bias_part, 0.0)
        input_part, a_gain_part, a_shift_part = norm_back(
            grad_first, unit_first, inverse_first, a_gain
        )
        grad_tokens = grad_mid + input_part
        vectors = jnp.concatenate(
            [
                a_gain_part.reshape(-1, shard),
                a_shift_part.reshape(-1, shard),
                f_gain_part.reshape(-1, shard),
                f_shift_part.reshape(-1, shard),
                bias_part.reshape(-1, 3 * shard),
            ],
            axis=1,
        )
        vectors = lax.psum_scatter(vectors, BOTH, scatter_dimension=0, tiled=True)[0]
        return (
            output[None],
            grad_tokens[None],
            vectors[:shard],
            vectors[shard : 2 * shard],
            project_grad,
            vectors[4 * shard :],
            out_grad,
            vectors[2 * shard : 3 * shard],
            vectors[3 * shard : 4 * shard],
            gate_grad,
            up_grad,
            down_grad,
        )

    return body


MESH_ID = pl.DeviceIdType.MESH
DMA = pltpu.SemaphoreType.DMA
HBM = pl.ANY
VMEM = pltpu.VMEM
LIMIT = 56 * 1024 * 1024


class Place:
    def __init__(self):
        self.r = lax.axis_index("rows")
        self.b = lax.axis_index("blk")
        self.z = self.b // 2
        self.c = lax.rem(self.b, 2)
        self.sibling = 2 * self.z + 1 - self.c
        self.rx = self.r + 1 - 2 * lax.rem(self.r, 2)
        self.ry = lax.rem(self.r + 2, 4)
        self.rd = 3 - self.r

    def barrier(self, diagonal=False):
        sem = pltpu.get_barrier_semaphore()
        peers = [(self.r, lax.rem(self.b + k, 8)) for k in range(1, 8)]
        peers += [(self.rx, self.b), (self.ry, self.b)]
        if diagonal:
            peers.append((self.rd, self.b))
        for peer in peers:
            pl.semaphore_signal(sem, inc=1, device_id=peer, device_id_type=MESH_ID)
        pl.semaphore_wait(sem, len(peers))


def remote(src, dst, send, recv, r, b):
    return pltpu.make_async_remote_copy(
        src_ref=src, dst_ref=dst, send_sem=send, recv_sem=recv, device_id=(r, b), device_id_type=MESH_ID
    )


def drive(*jobs):
    active = list(jobs)
    while active:
        for job in list(active):
            try:
                next(job)
            except StopIteration:
                active.remove(job)


CHUNKS = 2


def line_gather_sems():
    return [DMA((4, CHUNKS))] * 4 + [DMA((7, CHUNKS))] * 2 + [DMA((CHUNKS,))]


def line_gather(at, own, spot, sems, paired=True):
    up_send, down_send, up_recv, down_recv, pair_send, pair_recv, local_sem = sems

    def up(d, k, src):
        return remote(
            src, spot(at.z - d, at.c, k), up_send.at[d, k], up_recv.at[d, k], at.r, at.b + 2
        )

    def down(d, k, src):
        return remote(
            src, spot(at.z + d, at.c, k), down_send.at[d, k], down_recv.at[d, k], at.r, at.b - 2
        )

    def up_in(d, k):
        piece = spot(at.z - d - 1, at.c, k)
        return remote(piece, piece, up_send.at[d, k], up_recv.at[d, k], at.r, at.b + 2)

    def down_in(d, k):
        piece = spot(at.z + d + 1, at.c, k)
        return remote(piece, piece, down_send.at[d, k], down_recv.at[d, k], at.r, at.b - 2)

    def pair(i, k, z, src):
        return remote(
            src, spot(z, at.c, k), pair_send.at[i, k], pair_recv.at[i, k], at.r, at.sibling
        )

    def pair_in(i, k, z):
        piece = spot(z, 1 - at.c, k)
        return remote(piece, piece, pair_send.at[i, k], pair_recv.at[i, k], at.r, at.sibling)

    locals_ = [
        pltpu.make_async_copy(own(k), spot(at.z, at.c, k), local_sem.at[k]) for k in range(CHUNKS)
    ]
    for k in range(CHUNKS):
        locals_[k].start()
        pl.when(at.z < 3)(lambda: up(0, k, own(k)).start())
        pl.when(at.z > 0)(lambda: down(0, k, own(k)).start())
        if paired:
            pair(0, k, at.z, own(k)).start()
    yield
    for d in range(3):
        for k in range(CHUNKS):

            @pl.when(at.z - 1 - d >= 0)
            def _():
                z = at.z - 1 - d
                up_in(d, k).wait_recv()
                if d < 2:
                    pl.when(at.z < 3)(lambda: up(d + 1, k, spot(z, at.c, k)).start())
                if paired:
                    pair(1 + d, k, z, spot(z, at.c, k)).start()

            @pl.when(at.z + 1 + d <= 3)
            def _():
                z = at.z + 1 + d
                down_in(d, k).wait_recv()
                if d < 2:
                    pl.when(at.z > 0)(lambda: down(d + 1, k, spot(z, at.c, k)).start())
                if paired:
                    pair(4 + d, k, z, spot(z, at.c, k)).start()

            yield
    for k in range(CHUNKS):
        locals_[k].wait()
        if paired:
            pair(0, k, at.z, own(k)).wait_send()
            pair_in(0, k, at.z).wait_recv()
        pl.when(at.z < 3)(lambda: up(0, k, own(k)).wait_send())
        pl.when(at.z > 0)(lambda: down(0, k, own(k)).wait_send())
        for d in range(3):

            @pl.when(at.z - 1 - d >= 0)
            def _():
                z = at.z - 1 - d
                if paired:
                    pair(1 + d, k, z, spot(z, at.c, k)).wait_send()
                    pair_in(1 + d, k, z).wait_recv()
                if d < 2:
                    pl.when(at.z < 3)(lambda: up(d + 1, k, spot(z, at.c, k)).wait_send())

            @pl.when(at.z + 1 + d <= 3)
            def _():
                z = at.z + 1 + d
                if paired:
                    pair(4 + d, k, z, spot(z, at.c, k)).wait_send()
                    pair_in(4 + d, k, z).wait_recv()
                if d < 2:
                    pl.when(at.z > 0)(lambda: down(d + 1, k, spot(z, at.c, k)).wait_send())


def rows_of(ref, count):
    size = count // CHUNKS
    return lambda z, c, k: ref.at[pl.ds(pl.multiple_of((2 * z + c) * count + k * size, size), size)]


def cuts_of(ref):
    size = ref.shape[0] // CHUNKS
    return lambda k: ref.at[pl.ds(k * size, size)]


def line_scatter_scratch(count, width):
    block = VMEM((4, count, width), jnp.bfloat16)
    arrive = VMEM((3, count, width), jnp.bfloat16)
    return [block, arrive, arrive] + [DMA((4, CHUNKS))] * 2 + [DMA((3, CHUNKS))] * 4


def line_scatter(at, block, result, scratch, paired=True):
    held, from_below, from_above, pair_send, pair_recv, up_send, up_recv, down_send, down_recv = scratch
    count = held.shape[1]
    size = count // CHUNKS

    def cut(k):
        return pl.ds(k * size, size)

    def pair(z, k):
        return remote(
            block(z, 1 - at.c, k),
            held.at[z, cut(k)],
            pair_send.at[z, k],
            pair_recv.at[z, k],
            at.r,
            at.sibling,
        )

    def up(z, k):
        return remote(
            held.at[z, cut(k)],
            from_below.at[z - 1, cut(k)],
            up_send.at[z - 1, k],
            up_recv.at[z - 1, k],
            at.r,
            at.b + 2,
        )

    def down(z, k):
        return remote(
            held.at[z, cut(k)],
            from_above.at[z, cut(k)],
            down_send.at[z, k],
            down_recv.at[z, k],
            at.r,
            at.b - 2,
        )

    def wide(ref):
        return ref[...].astype(jnp.float32)

    def own(z, k):
        mine = wide(block(z, at.c, k))
        return mine + wide(held.at[z, cut(k)]) if paired else mine

    if paired:
        for z in (3, 0, 2, 1):
            for k in range(CHUNKS):
                pair(z, k).start()
    yield
    for step in range(3):
        for k in range(CHUNKS):
            far, near = 3 - step, step

            @pl.when(at.z < far)
            def _():
                if paired:
                    pair(far, k).wait_recv()

                @pl.when(at.z == 0)
                def _():
                    held[far, cut(k)] = own(far, k).astype(jnp.bfloat16)

                @pl.when(at.z > 0)
                def _():
                    up(far, k).wait_recv()
                    held[far, cut(k)] = (
                        own(far, k) + wide(from_below.at[far - 1, cut(k)])
                    ).astype(jnp.bfloat16)

                up(far, k).start()

            @pl.when(at.z > near)
            def _():
                if paired:
                    pair(near, k).wait_recv()

                @pl.when(at.z == 3)
                def _():
                    held[near, cut(k)] = own(near, k).astype(jnp.bfloat16)

                @pl.when(at.z < 3)
                def _():
                    down(near, k).wait_recv()
                    held[near, cut(k)] = (
                        own(near, k) + wide(from_above.at[near, cut(k)])
                    ).astype(jnp.bfloat16)

                down(near, k).start()

            yield
    for z in range(4):
        for k in range(CHUNKS):

            @pl.when(at.z == z)
            def _():
                if paired:
                    pair(z, k).wait_recv()
                total = own(z, k)
                if z > 0:
                    up(z, k).wait_recv()
                    total += wide(from_below.at[z - 1, cut(k)])
                if z < 3:
                    down(z, k).wait_recv()
                    total += wide(from_above.at[z, cut(k)])
                result[cut(k)] = total.astype(result.dtype)

    for z in range(4):
        for k in range(CHUNKS):
            if paired:
                pair(z, k).wait_send()
            if z > 0:
                pl.when(at.z < z)(lambda: up(z, k).wait_send())
            if z < 3:
                pl.when(at.z > z)(lambda: down(z, k).wait_send())


def half_of(ref, axis, which):
    size = ref.shape[axis] // 2
    return ref.at[pl.ds(which * size, size)] if axis == 0 else ref.at[:, pl.ds(which * size, size)]


def row_halves(ref, axis=0):
    count = ref.shape[0] // 4
    return lambda r, which: half_of(
        ref.at[pl.ds(pl.multiple_of(r * count, count), count)], axis, which
    )


def square_gather_sems():
    return [DMA((6,)), DMA((6,)), DMA((2,))]


def square_gather(at, own, spot, sems):
    send, recv, local_sem = sems

    def copy(i, src, r_of, which, to):
        return remote(src, spot(r_of, which), send.at[i], recv.at[i], to, at.b)

    outs = [
        copy(0, own(0), at.r, 0, at.rx),
        copy(1, own(1), at.r, 1, at.ry),
        copy(2, own(1), at.r, 1, at.rx),
        copy(3, own(0), at.r, 0, at.ry),
    ]
    ins = [
        copy(0, spot(at.rx, 0), at.rx, 0, at.rx),
        copy(1, spot(at.ry, 1), at.ry, 1, at.ry),
        copy(2, spot(at.rx, 1), at.rx, 1, at.rx),
        copy(3, spot(at.ry, 0), at.ry, 0, at.ry),
        copy(4, spot(at.rd, 0), at.rd, 0, at.ry),
        copy(5, spot(at.rd, 1), at.rd, 1, at.rx),
    ]
    locals_ = [pltpu.make_async_copy(own(h), spot(at.r, h), local_sem.at[h]) for h in range(2)]
    for copy_ in outs + locals_:
        copy_.start()
    yield
    ins[0].wait_recv()
    outs.append(copy(4, spot(at.rx, 0), at.rx, 0, at.ry))
    outs[4].start()
    yield
    ins[1].wait_recv()
    outs.append(copy(5, spot(at.ry, 1), at.ry, 1, at.rx))
    outs[5].start()
    yield
    for copy_ in locals_:
        copy_.wait()
    for i in (2, 3, 4, 5):
        ins[i].wait_recv()
    for out in outs:
        out.wait_send()


def square_scatter_scratch(count, width, axis=0):
    half = (count // 2, width) if axis == 0 else (count, width // 2)
    piece = VMEM((count, width), jnp.bfloat16)
    part = VMEM(half, jnp.bfloat16)
    return [piece, piece, part, part, part, part, DMA((6,)), DMA((6,))]


def square_scatter(at, part, result, scratch, axis=0, prepare=None):
    from_x, from_y, far_x, far_y, out_x, out_y, send, recv = scratch
    prepare = prepare or (lambda r: None)

    def wide(ref):
        return ref[...].astype(jnp.float32)

    copies = [
        remote(part(at.rd, 0), far_x, send.at[0], recv.at[0], at.rx, at.b),
        remote(part(at.rd, 1), far_y, send.at[1], recv.at[1], at.ry, at.b),
        remote(part(at.rx, 0), half_of(from_x, axis, 0), send.at[2], recv.at[2], at.rx, at.b),
        remote(part(at.ry, 1), half_of(from_y, axis, 1), send.at[3], recv.at[3], at.ry, at.b),
        remote(out_y, half_of(from_y, axis, 0), send.at[4], recv.at[4], at.ry, at.b),
        remote(out_x, half_of(from_x, axis, 1), send.at[5], recv.at[5], at.rx, at.b),
    ]
    prepare(at.rd)
    copies[0].start()
    copies[1].start()
    yield
    prepare(at.rx)
    copies[2].start()
    yield
    prepare(at.ry)
    copies[3].start()
    yield
    copies[0].wait_recv()
    out_y[...] = (wide(part(at.ry, 0)) + wide(far_x)).astype(jnp.bfloat16)
    copies[4].start()
    copies[1].wait_recv()
    out_x[...] = (wide(part(at.rx, 1)) + wide(far_y)).astype(jnp.bfloat16)
    copies[5].start()
    yield
    prepare(at.r)
    yield
    for i in (2, 3, 4, 5):
        copies[i].wait_recv()
    for which in range(2):
        total = (
            wide(part(at.r, which)) + wide(half_of(from_x, axis, which)) + wide(half_of(from_y, axis, which))
        )
        spot = half_of(result, axis, which)
        spot[...] = total.astype(result.dtype)
    for copy in copies:
        copy.wait_send()


def exchange_sems(parts=1):
    return [DMA((7, parts)), DMA((7, parts)), DMA((parts,))]


def exchange(at, take, put, sems, parts=1):
    send, recv, local_sem = sems
    locals_ = [
        pltpu.make_async_copy(take(at.b, p), put(at.b, p), local_sem.at[p]) for p in range(parts)
    ]
    outs, ins = [], []
    for k in (4, 3, 5, 2, 6, 1, 7):
        to, source = lax.rem(at.b + k, 8), lax.rem(at.b + 8 - k, 8)
        for p in range(parts):
            pair = (send.at[k - 1, p], recv.at[k - 1, p])
            outs.append(remote(take(to, p), put(at.b, p), *pair, at.r, to))
            ins.append(remote(put(source, p), put(source, p), *pair, at.r, source))
    for copy in locals_ + outs:
        copy.start()
    yield
    for copy in ins:
        copy.wait_recv()
    for copy in locals_:
        copy.wait()
    for copy in outs:
        copy.wait_send()


def call(kernel, ins, outs, scratch, number, *args):
    return pl.pallas_call(
        kernel,
        out_shape=[jax.ShapeDtypeStruct(shape, kind) for shape, kind, _ in outs],
        in_specs=[pl.BlockSpec(memory_space=space) for space in ins],
        out_specs=[pl.BlockSpec(memory_space=space) for _, _, space in outs],
        scratch_shapes=scratch,
        compiler_params=pltpu.CompilerParams(
            collective_id=number, has_side_effects=True, vmem_limit_bytes=LIMIT
        ),
    )(*args)


def vector_gather(at, own, full, sems):
    send, recv, local_sem = sems
    mine = 8 * at.r + at.b
    outs, ins = [], []
    for k in range(1, 8):
        to, source = lax.rem(at.b + k, 8), lax.rem(at.b + 8 - k, 8)
        outs.append(remote(own, full.at[mine], send.at[k - 1], recv.at[k - 1], at.r, to))
        piece = full.at[8 * at.r + source]
        ins.append(remote(piece, piece, send.at[k - 1], recv.at[k - 1], at.r, source))
    local = pltpu.make_async_copy(own, full.at[mine], local_sem)
    local.start()
    for out in outs:
        out.start()
    yield
    for copy in ins:
        copy.wait_recv()
    local.wait()
    group = full.at[pl.ds(8 * at.r, 8)]
    later = []
    for i, row in enumerate((at.rx, at.ry, at.rd)):
        outs.append(remote(group, group, send.at[7 + i], recv.at[7 + i], row, at.b))
        outs[-1].start()
        theirs = full.at[pl.ds(8 * row, 8)]
        later.append(remote(theirs, theirs, send.at[7 + i], recv.at[7 + i], row, at.b))
    yield
    for copy in later:
        copy.wait_recv()
    for out in outs:
        out.wait_send()


def make_tables(at, vectors, start, cosine, minus, plus):
    docs = jnp.concatenate(
        [vectors[8 * at.r + j, 6:7].astype(jnp.float32) for j in range(8)], axis=0
    )
    begins = jnp.zeros_like(docs)
    for doc in range(1, 5):
        before = jnp.sum((docs < doc).astype(jnp.float32), axis=(0, 1), keepdims=True)
        begins = jnp.where(docs == doc, before, begins)
    index = lax.broadcasted_iota(jnp.int32, docs.shape, 0) * 128
    index = (index + lax.broadcasted_iota(jnp.int32, docs.shape, 1)).astype(jnp.float32)
    places = index - begins
    half = ROT // 2
    row = lax.broadcasted_iota(jnp.int32, (half, 128), 0)
    frequency = jnp.zeros((half, 128), jnp.float32)
    for j in range(half):
        frequency = jnp.where(row == j, rotary_base ** (-j / half), frequency)
    eight = jnp.zeros((half, 128), jnp.float32)
    gap = jnp.zeros((48, 128), jnp.float32)
    for j in range(8):
        rows = slice(j * 128, j * 128 + 128)
        angles = frequency * places[j : j + 1]
        cos, sin = jnp.cos(angles), jnp.sin(angles)

        def table(first, second, rest):
            return jnp.transpose(jnp.concatenate([first, second, rest] * 2, axis=0))

        cosine[rows] = table(cos, cos, gap + 1.0)
        minus[rows] = table(-sin, eight, gap)
        plus[rows] = table(eight, sin, gap)
        start[rows] = jnp.transpose(jnp.broadcast_to(begins[j : j + 1], (128, 128))).astype(jnp.int32)


def start_kernel(
    x_ref, vector_ref, project_ref, down_ref, out_ref, gate_ref, up_ref,
    vectors, normed, pieces, w_project, w_down, w_out, gate_up, start, cosine, minus, plus,
    unit, own, vector_sems, exchange_sem, square_sem, down_sem, line_sems, out_sems,
):
    at = Place()
    at.barrier(diagonal=True)
    width = x_ref.shape[1]
    vector_job = vector_gather(at, vector_ref, vectors, vector_sems)
    next(vector_job)
    inner = w_project.shape[1] // 3
    depth = project_ref.shape[0]
    project_job = exchange(
        at,
        lambda b, p: project_ref.at[:, pl.ds(pl.multiple_of(p * width + b * inner, inner), inner)],
        lambda b, p: pieces.at[
            pl.ds(pl.multiple_of(b * depth, depth), depth), pl.ds(p * inner, inner)
        ],
        exchange_sem,
        3,
    )
    next(project_job)
    down_job = square_gather(
        at, lambda half: half_of(down_ref, 1, half), row_halves(w_down, 1), down_sem
    )
    next(down_job)
    x = x_ref[...].astype(jnp.float32)
    centered = x - jnp.mean(x, axis=1, keepdims=True)
    unit[...] = centered * lax.rsqrt(jnp.mean(centered * centered, axis=1, keepdims=True) + epsilon)
    drive(vector_job)
    for tile in range(width // 128):
        lanes = slice(tile * 128, tile * 128 + 128)
        both = vectors[2 * tile].astype(jnp.float32) + vectors[2 * tile + 1].astype(jnp.float32)
        own[:, lanes] = (unit[:, lanes] * both[0:1] + both[1:2]).astype(jnp.bfloat16)
    line_job = line_gather(at, cuts_of(own), rows_of(normed, own.shape[0]), line_sems)
    next(line_job)
    size = depth // CHUNKS
    out_job = line_gather(
        at, cuts_of(out_ref), lambda z, c, k: w_out.at[z, pl.ds(k * size, size)], out_sems, False
    )
    next(out_job)
    hidden = down_ref.shape[0]
    for b in range(8):
        for r in range(4):
            source = slice((8 * r + b) * hidden, (8 * r + b + 1) * hidden)
            gate_up[b, :, r * hidden : (r + 1) * hidden] = gate_ref[:, source]
            gate_up[b, :, (4 + r) * hidden : (5 + r) * hidden] = up_ref[:, source]
    drive(project_job)
    square_job = square_gather(
        at, lambda half: half_of(pieces, 0, half), row_halves(w_project), square_sem
    )
    next(square_job)
    make_tables(at, vectors, start, cosine, minus, plus)
    drive(square_job, line_job, down_job, out_job)


def pack_sems(groups):
    flat, spans = [], []
    for group in groups:
        spans.append((len(flat), len(flat) + len(group)))
        flat += group
    return flat, spans


def grouped(kernel, lead, spans):
    def run(*refs):
        rest = refs[lead:]
        return kernel(*refs[:lead], *[rest[a:b] for a, b in spans])

    return run


def start_call(x, vector, project, down, out_weight, gate, up):
    rows, width = x.shape
    depth = project.shape[0]
    inner = project.shape[1] // 8
    bf, f32 = jnp.bfloat16, jnp.float32
    groups = [
        [DMA((10,)), DMA((10,)), DMA], exchange_sems(3), square_gather_sems(), square_gather_sems(),
        line_gather_sems(), line_gather_sems(),
    ]
    flat, spans = pack_sems(groups)
    outs = [
        ((32, 16, 128), bf, VMEM), ((8 * rows, width), bf, HBM), ((8 * depth, inner), bf, HBM),
        ((32 * depth, inner), bf, HBM), ((4 * down.shape[0], width), bf, HBM),
        ((4, depth, width), bf, HBM), ((8, depth, 8 * down.shape[0]), bf, VMEM),
        ((8 * rows, 128), jnp.int32, VMEM),
    ] + [((8 * rows, 128), f32, VMEM)] * 3
    scratch = [VMEM((rows, width), f32), VMEM((rows, width), bf)] + flat
    vectors, normed, _, w_project, w_down, w_out, gate_up, start, *tables = call(
        grouped(start_kernel, 20, spans), [VMEM, VMEM, HBM, HBM, HBM, VMEM, VMEM], outs, scratch, 0,
        x, vector, project, down, out_weight, gate, up,
    )
    return vectors, normed, w_project, w_down, w_out, gate_up, start, tables


def turned(columns, cosine, minus, plus):
    half = ROT // 2
    return (
        columns * cosine
        + pltpu.roll(columns, 128 - half, 1) * minus
        + pltpu.roll(columns, half, 1) * plus
    )


def score_mask(first_row, rows, keys, start):
    row = lax.broadcasted_iota(jnp.int32, (rows, keys), 0) + first_row
    col = lax.broadcasted_iota(jnp.int32, (rows, keys), 1)
    return (col <= row) & (col >= start)


QROWS = 256


def attend_forward_kernel(
    x_ref, w_ref, bias, start, cosine, minus, plus, gate_up, out_ref,
    queries, keys, values, attended, log_total, mixed_heads, gate_up_all, w_out,
    low, own_sems, gate_up_sems, square_sems, pair_sems,
):
    at = Place()
    at.barrier()
    out_job = square_gather(
        at,
        lambda half: half_of(out_ref, 0, half),
        lambda r, half: w_out.at[r, pl.ds(2 * half, 2), at.c],
        square_sems,
    )
    next(out_job)
    length, local = queries.shape
    depth = gate_up.shape[1]
    gate_up_job = exchange(
        at, lambda b, p: gate_up.at[b], lambda b, p: gate_up_all.at[b], gate_up_sems
    )
    next(gate_up_job)
    scale = 1.0 / math.sqrt(local * 8 // HEADS)
    blocks = length // QROWS

    @pl.loop(0, blocks)
    def _(i):
        rows = pl.ds(pl.multiple_of(i * QROWS, QROWS), QROWS)
        mixed = dot(x_ref[rows], w_ref[...], ((1,), (0,))) + bias[...]
        tables = (cosine[rows], minus[rows], plus[rows])
        for pair in range(local // 128):
            lanes = slice(pair * 128, pair * 128 + 128)
            queries[rows, lanes] = turned(mixed[:, lanes], *tables).astype(jnp.bfloat16)
            shifted = slice(local + pair * 128, local + pair * 128 + 128)
            keys[rows, lanes] = turned(mixed[:, shifted], *tables).astype(jnp.bfloat16)
        values[rows] = mixed[:, 2 * local :].astype(jnp.bfloat16)

    send, recv, local_sem = own_sems

    def deliver(to):
        rows = low.at[pl.ds(to * 128, 128)]
        spot = mixed_heads.at[:, pl.ds(pl.multiple_of(at.b * local, local), local)]
        return remote(rows, spot, send.at[to], recv.at[at.b], at.r, to)

    for i in range(blocks):
        rows = slice(i * QROWS, (i + 1) * QROWS)
        count = (i + 1) * QROWS

        @pl.loop(0, local // 128)
        def _(pair):
            lanes = pl.ds(pl.multiple_of(pair * 128, 128), 128)
            lane = lax.broadcasted_iota(jnp.int32, (QROWS, 128), 1)
            q, k, v = queries[rows, lanes], keys[:count, lanes], values[:count, lanes]
            allowed = score_mask(i * QROWS, QROWS, count, start[rows, 0:1])
            found = []
            for head in range(2):
                mine = (lane >= 64) if head else (lane < 64)
                scores = dot(jnp.where(mine, q, jnp.zeros_like(q)), k, ((1,), (1,))) * scale
                scores = jnp.where(allowed, scores, masked_value)
                top = jnp.max(scores, axis=1, keepdims=True)
                weights = jnp.exp(scores - top)
                total = jnp.sum(weights, axis=1, keepdims=True)
                found.append(
                    (dot(weights.astype(jnp.bfloat16), v, ((1,), (0,))) / total, top + jnp.log(total))
                )
            both = jnp.where(lane < 64, found[0][0], found[1][0])
            attended[rows, lanes] = both
            low[rows, lanes] = both.astype(jnp.bfloat16)
            log_total[rows, lanes] = jnp.where(lane < 64, found[0][1], found[1][1])

        next(out_job, None)
        for to in range(i * QROWS // 128, (i + 1) * QROWS // 128):
            pl.when(at.b != to)(lambda: deliver(to).start())

            @pl.when(at.b == to)
            def _():
                pltpu.make_async_copy(
                    low.at[pl.ds(to * 128, 128)],
                    mixed_heads.at[:, pl.ds(pl.multiple_of(at.b * local, local), local)],
                    local_sem,
                ).start()

    drive(out_job)
    pair_send, pair_recv = pair_sems
    pairs = [
        remote(
            w_out.at[r, :, at.c], w_out.at[r, :, at.c], pair_send.at[r], pair_recv.at[r], at.r, at.sibling
        )
        for r in range(4)
    ]
    for copy in pairs:
        copy.start()
    for source in range(8):

        @pl.when(at.b != source)
        def _():
            spot = mixed_heads.at[:, pl.ds(source * local, local)]
            remote(spot, spot, send.at[source], recv.at[source], at.r, source).wait_recv()

        @pl.when(at.b == source)
        def _():
            pltpu.make_async_copy(
                low.at[pl.ds(source * 128, 128)],
                mixed_heads.at[:, pl.ds(source * local, local)],
                local_sem,
            ).wait()

    drive(gate_up_job)
    for to in range(8):
        pl.when(at.b != to)(lambda: deliver(to).wait_send())
    for r in range(4):
        theirs = w_out.at[r, :, 1 - at.c]
        remote(theirs, theirs, pair_send.at[r], pair_recv.at[r], at.r, at.sibling).wait_recv()
        pairs[r].wait_send()


def attend_forward(x, w, bias, start, tables, gate_up, w_out):
    length, local = x.shape[0], w.shape[1] // 3
    bf, f32 = jnp.bfloat16, jnp.float32
    flat, spans = pack_sems(
        [[DMA((8,)), DMA((8,)), DMA], exchange_sems(), square_gather_sems(), [DMA((4,)), DMA((4,))]]
    )
    outs = [((length, local), bf, VMEM)] * 3 + [((length, local), f32, VMEM)] * 2
    outs += [((length // 8, 8 * local), bf, VMEM), (gate_up.shape, bf, HBM)]
    outs += [((4, 4, 2) + w_out.shape[1:], bf, HBM)]
    return call(
        grouped(attend_forward_kernel, 18, spans), [VMEM] * 7 + [HBM, HBM], outs,
        [VMEM((length, local), bf)] + flat, 1, x, w, bias, start, *tables, gate_up, w_out,
    )


def second_gather_kernel(
    own, gate_up, cotangent, normed, w_gate_up, grad_out, line_sems, square_sems, other_sems
):
    at = Place()
    at.barrier()
    count = own.shape[0]
    drive(
        line_gather(at, cuts_of(own), rows_of(normed, count), line_sems),
        square_gather(at, lambda half: half_of(gate_up, 0, half), row_halves(w_gate_up), square_sems),
        line_gather(at, cuts_of(cotangent), rows_of(grad_out, count), other_sems),
    )


def second_gather(own, gate_up, cotangent):
    flat, spans = pack_sems([line_gather_sems(), square_gather_sems(), line_gather_sems()])
    bf = jnp.bfloat16
    full = ((8 * own.shape[0], own.shape[1]), bf, HBM)
    outs = [full, ((4 * gate_up.shape[0], gate_up.shape[1]), bf, HBM), full]
    return call(
        grouped(second_gather_kernel, 6, spans), [HBM] * 3, outs, flat, 2, own, gate_up, cotangent
    )


def feed_reduce_kernel(
    partial, out_partial, normed, grad_both, result, out_result, weight_result,
    weight, line_scratch, out_scratch, square_scratch,
):
    at = Place()
    at.barrier()
    rows = result.shape[0]
    depth = weight_result.shape[0]
    step = depth // 2

    def prepare(r):
        for half in range(2):
            spot = pl.ds(pl.multiple_of(r * depth + half * step, step), step)
            weight[spot] = dot(normed[:, spot], grad_both[...], ((0,), (0,))).astype(jnp.bfloat16)

    drive(
        line_scatter(at, rows_of(partial, rows), result, line_scratch),
        square_scatter(at, row_halves(weight), weight_result, square_scratch, 0, prepare),
        line_scatter(at, rows_of(out_partial, rows), out_result, out_scratch),
    )


def feed_reduce(partial, out_partial, normed, grad_both):
    rows, width = partial.shape[0] // 8, partial.shape[1]
    bf, f32 = jnp.bfloat16, jnp.float32
    owned = (width // 4, grad_both.shape[1])
    line = line_scatter_scratch(rows, width)
    flat, spans = pack_sems([line, line, square_scatter_scratch(*owned)])
    outs = [((rows, width), f32, VMEM)] * 2 + [(owned, bf, VMEM)]
    return call(
        grouped(feed_reduce_kernel, 8, spans), [VMEM] * 4, outs,
        [VMEM((width, owned[1]), bf)] + flat, 3, partial, out_partial, normed, grad_both,
    )


def attend_backward_kernel(
    grad_rows, queries, keys, values, attended, log_total, start, cosine, minus, plus, out_weight,
    gate_up, grad_mixed, out_result, gate_result, up_result,
    grad, keys_sum, values_sum, pieces, halves, own_sems, square_scratch, pair_sems, gate_up_sems,
):
    at = Place()
    at.barrier()
    length, local = queries.shape
    scale = 1.0 / math.sqrt(local * 8 // HEADS)
    blocks = length // QROWS
    own_job = exchange(
        at,
        lambda b, p: grad_rows.at[:, pl.ds(pl.multiple_of(b * local, local), local)],
        lambda b, p: grad.at[pl.ds(pl.multiple_of(b * 128, 128), 128)],
        own_sems,
    )
    next(own_job)
    pair_send, pair_recv = pair_sems
    pairs = [
        remote(
            out_weight.at[r, :, 1 - at.c], halves.at[r], pair_send.at[r], pair_recv.at[r], at.r, at.sibling
        )
        for r in range(4)
    ]
    for copy in pairs:
        copy.start()
    gate_up_job = exchange(at, lambda b, p: gate_up.at[b], lambda b, p: pieces.at[b], gate_up_sems)
    next(gate_up_job)
    keys_sum[...] = jnp.zeros_like(keys_sum)
    values_sum[...] = jnp.zeros_like(values_sum)
    for r in range(4):
        pairs[r].wait()
        mine = out_weight[r, :, at.c].astype(jnp.float32) + halves[r].astype(jnp.float32)
        halves[r] = mine.astype(jnp.bfloat16)
    out_job = square_scatter(
        at,
        lambda r, half: halves.at[r, pl.ds(2 * half, 2)],
        out_result,
        square_scratch,
    )
    next(out_job)
    next(out_job)
    next(out_job)
    drive(own_job)
    for i in range(blocks):
        rows = slice(i * QROWS, (i + 1) * QROWS)
        count = (i + 1) * QROWS

        @pl.loop(0, local // 128)
        def _(pair):
            lanes = pl.ds(pl.multiple_of(pair * 128, 128), 128)
            lane = lax.broadcasted_iota(jnp.int32, (QROWS, 128), 1)
            q, g = queries[rows, lanes], grad[rows, lanes]
            k, v = keys[:count, lanes], values[:count, lanes]
            allowed = score_mask(i * QROWS, QROWS, count, start[rows, 0:1])
            product = g.astype(jnp.float32) * attended[rows, lanes]
            logs = log_total[rows, lanes]
            queries_part, keys_part, values_part = [], [], []
            for head in range(2):
                mine = (lane >= 64) if head else (lane < 64)
                q_head = jnp.where(mine, q, jnp.zeros_like(q))
                g_head = jnp.where(mine, g, jnp.zeros_like(g))
                delta = jnp.sum(jnp.where(mine, product, 0.0), axis=1, keepdims=True)
                log_head = jnp.max(jnp.where(mine, logs, masked_value), axis=1, keepdims=True)
                scores = dot(q_head, k, ((1,), (1,))) * scale
                probs = jnp.exp(jnp.where(allowed, scores - log_head, masked_value))
                grad_probs = dot(g_head, v, ((1,), (1,)))
                grad_scores = (probs * (grad_probs - delta) * scale).astype(jnp.bfloat16)
                queries_part.append(dot(grad_scores, k, ((1,), (0,))))
                keys_part.append(dot(grad_scores, q_head, ((0,), (0,))))
                values_part.append(dot(probs.astype(jnp.bfloat16), g_head, ((0,), (0,))))
            both = jnp.where(lane < 64, queries_part[0], queries_part[1])
            tables = (cosine[rows], -minus[rows], -plus[rows])
            grad_mixed[rows, lanes] = turned(both, *tables).astype(jnp.bfloat16)
            keys_sum[:count, lanes] += keys_part[0] + keys_part[1]
            values_sum[:count, lanes] += values_part[0] + values_part[1]

        next(out_job, None)

    @pl.loop(0, blocks)
    def _(i):
        rows = pl.ds(pl.multiple_of(i * QROWS, QROWS), QROWS)
        tables = (cosine[rows], -minus[rows], -plus[rows])
        for pair in range(local // 128):
            lanes = slice(pair * 128, pair * 128 + 128)
            shifted = slice(local + pair * 128, local + pair * 128 + 128)
            grad_mixed[rows, shifted] = turned(keys_sum[rows, lanes], *tables).astype(jnp.bfloat16)
        grad_mixed[rows, slice(2 * local, 3 * local)] = values_sum[rows].astype(jnp.bfloat16)

    drive(out_job)
    drive(gate_up_job)
    hidden = pieces.shape[2] // 8
    for b in range(8):
        for r in range(4):
            source = slice((8 * r + b) * hidden, (8 * r + b + 1) * hidden)
            gate_result[:, source] = pieces[b, :, r * hidden : (r + 1) * hidden].astype(jnp.float32)
            up_result[:, source] = pieces[b, :, (4 + r) * hidden : (5 + r) * hidden].astype(jnp.float32)


def attend_backward(
    grad_rows, queries, keys, values, attended, log_total, start, tables, out_weight, gate_up
):
    length, local = queries.shape
    bf, f32 = jnp.bfloat16, jnp.float32
    depth, width = out_weight.shape[3:]
    quarter = [VMEM((4, depth, width), bf)] * 2 + [VMEM((2, depth, width), bf)] * 4
    flat, spans = pack_sems(
        [
            exchange_sems(), quarter + [DMA((6,)), DMA((6,))], [DMA((4,)), DMA((4,))], exchange_sems(),
        ]
    )
    shard = (gate_up.shape[1], 4 * gate_up.shape[2])
    outs = [((length, 3 * local), bf, VMEM), ((4, depth, width), bf, VMEM)] + [(shard, f32, VMEM)] * 2
    scratch = [VMEM((length, local), bf), VMEM((length, local), f32), VMEM((length, local), f32)]
    scratch += [VMEM(gate_up.shape, bf), VMEM((4, 4, depth, width), bf)]
    return call(
        grouped(attend_backward_kernel, 21, spans), [VMEM] * 11 + [HBM], outs, scratch + flat, 4,
        grad_rows, queries, keys, values, attended, log_total, start, *tables, out_weight, gate_up,
    )


def finish_kernel(
    partial, normed, grad_mixed, down_partial, out_part, x_ref, gain, grad_mid, feed_sums, bias_sums,
    tokens_grad, project_grad, down_grad, out_grad, vector_out,
    weight, weight_result, pieces, first, sums, arrived, summed, rows_in,
    line_scratch, project_scratch, down_scratch, out_scratch, piece_sems, vector_sems, row_sems,
):
    at = Place()
    at.barrier(diagonal=True)
    rows, width = first.shape
    depth = weight_result.shape[0]

    def prepare(r):
        spot = pl.ds(pl.multiple_of(r * depth, depth), depth)
        weight[spot] = dot(normed[:, spot], grad_mixed[...], ((0,), (0,))).astype(jnp.bfloat16)

    shard = depth // 8
    size = shard // CHUNKS
    line_job = line_scatter(at, rows_of(partial, rows), first, line_scratch)
    next(line_job)
    out_job = line_scatter(
        at, lambda z, c, k: out_part.at[z, pl.ds(k * size, size)], out_grad, out_scratch, False
    )
    next(out_job)

    def project_work():
        yield from square_scatter(at, row_halves(weight), weight_result, project_scratch, 0, prepare)
        yield from exchange(
            at,
            lambda b, p: weight_result.at[pl.ds(pl.multiple_of(b * shard, shard), shard)],
            lambda b, p: pieces.at[b],
            piece_sems,
        )

    project_job = project_work()
    down_job = square_scatter(at, row_halves(down_partial, 1), down_grad, down_scratch, 1)

    def vector_work():
        x = x_ref[...].astype(jnp.float32)
        centered = x - jnp.mean(x, axis=1, keepdims=True)
        inverse = lax.rsqrt(jnp.mean(centered * centered, axis=1, keepdims=True) + epsilon)
        unit = centered * inverse
        incoming = first[...]
        product = incoming * unit
        parts = jnp.concatenate(
            [
                jnp.sum(product, axis=0, keepdims=True),
                jnp.sum(incoming, axis=0, keepdims=True),
                feed_sums[...],
            ],
            axis=0,
        )
        for b in range(8):
            for r in range(4):
                lanes = slice((4 * r + b // 2) * 128, (4 * r + b // 2 + 1) * 128)
                sums[b, r, 0:4] = parts[:, lanes]
                sums[b, r, 4:6] = bias_sums[b, r]
                sums[b, r, 6:8] = jnp.zeros((2, 128), jnp.float32)
        spread = exchange(at, lambda b, p: sums.at[b], lambda b, p: arrived.at[b], vector_sems)
        next(spread)
        unit_grad = incoming * gain[...]
        tokens_grad[...] = grad_mid[...] + inverse * (
            unit_grad
            - jnp.mean(unit_grad, axis=1, keepdims=True)
            - unit * jnp.mean(unit_grad * unit, axis=1, keepdims=True)
        )
        drive(spread)
        summed[...] = jnp.sum(arrived[...], axis=0)
        send, recv = row_sems
        copies = [
            remote(summed.at[row], rows_in.at[i], send.at[i], recv.at[i], row, at.b)
            for i, row in enumerate((at.rx, at.ry, at.rd))
        ]
        for copy in copies:
            copy.start()
        for copy in copies:
            copy.wait()
        vector_out[...] = summed[at.r] + rows_in[0] + rows_in[1] + rows_in[2]

    drive(line_job, project_job_steps(project_job, 6), down_job)
    vector_work()
    drive(project_job, out_job)
    inner = pieces.shape[2] // 3
    for b in range(8):
        for p in range(3):
            lanes = slice(p * width + b * inner, p * width + (b + 1) * inner)
            project_grad[:, lanes] = pieces[b, :, p * inner : (p + 1) * inner].astype(jnp.float32)


def project_job_steps(job, count):
    for _ in range(count):
        next(job)
        yield


def finish(
    partial, normed, grad_mixed, down_partial, out_part, x, gain, grad_mid, feed_sums, bias_sums
):
    bf, f32 = jnp.bfloat16, jnp.float32
    rows, width = x.shape
    inner = grad_mixed.shape[1]
    depth = width // 4
    shard = depth // 8
    down_owned = (down_partial.shape[0] // 4, width)
    flat, spans = pack_sems(
        [
            line_scatter_scratch(rows, width),
            square_scatter_scratch(depth, inner),
            square_scatter_scratch(*down_owned, 1),
            line_scatter_scratch(shard, width),
            exchange_sems(), exchange_sems(), [DMA((3,)), DMA((3,))],
        ]
    )
    outs = [
        ((rows, width), f32, VMEM), ((shard, 8 * inner), f32, VMEM), (down_owned, f32, VMEM),
        ((shard, width), f32, VMEM), ((8, 128), f32, VMEM),
    ]
    scratch = [
        VMEM((width, inner), bf), VMEM((depth, inner), bf), VMEM((8, shard, inner), bf),
        VMEM((rows, width), f32), VMEM((8, 4, 8, 128), f32), VMEM((8, 4, 8, 128), f32),
        VMEM((4, 8, 128), f32), VMEM((3, 8, 128), f32),
    ]
    return call(
        grouped(finish_kernel, 23, spans), [VMEM] * 10, outs, scratch + flat, 5,
        partial, normed, grad_mixed, down_partial, out_part, x, gain, grad_mid, feed_sums, bias_sums,
    )


def fast_body(
    tokens, segments, cotangent, attend_gain, attend_shift, project_weight, project_bias,
    output_weight, feed_gain, feed_shift, gate_weight, up_weight, down_weight,
):
    bf, f32 = jnp.bfloat16, jnp.float32
    own_rows, width = tokens.shape[1], tokens.shape[2]
    length = own_rows * 8
    head_width = width // HEADS
    local = width // 8
    hidden = down_weight.shape[0]
    shard = attend_gain.shape[0]
    r, b = lax.axis_index("rows"), lax.axis_index("blk")

    small = jnp.stack([attend_gain, attend_shift, feed_gain, feed_shift])
    zeros = jnp.zeros_like(small)
    small = jnp.where(
        b % 2 == 0, jnp.concatenate([small, zeros], 1), jnp.concatenate([zeros, small], 1)
    )
    rest = jnp.pad(project_bias, (0, 64)).reshape(2, 128)
    vector = jnp.concatenate(
        [small, rest, segments.astype(bf), jnp.zeros((9, 128), bf)], axis=0
    )

    vectors, normed_first, w_project, w_down, w_out, gate_up, start, tables = start_call(
        tokens[0], vector, project_weight, down_weight, output_weight, gate_weight, up_weight
    )

    def whole(row):
        pairs = vectors[:, row].reshape(16, 2, 128).astype(f32)
        return (pairs[:, 0] + pairs[:, 1]).reshape(-1)

    a_gain, f_gain, f_shift = whole(0), whole(2), whole(3)
    bias = vectors[:, 4:6].reshape(32, 256)[:, : 3 * shard].reshape(3, 8, local)
    bias = lax.dynamic_index_in_dim(bias, b, 1, False).reshape(1, -1).astype(f32)

    queries, keys, values, attended, log_total, attended_low, gate_up, w_out = attend_forward(
        normed_first, w_project, bias, start, tables, gate_up, w_out
    )
    w_out = w_out.reshape(width, width)
    inputs = tokens[0].astype(f32)
    resid_mid = inputs + dot(attended_low, w_out, ((1,), (0,)))
    unit_second, inverse_second = norm_stats(resid_mid)
    normed_second, w_gate_up, grad_out = second_gather(
        (unit_second * f_gain + f_shift).astype(bf), gate_up.reshape(8 * shard, 8 * hidden), cotangent[0]
    )
    both = dot(normed_second, w_gate_up, ((1,), (0,)))
    gate_value, up_value = both[:, : 4 * hidden], both[:, 4 * hidden :]
    gate_sigmoid = jax.nn.sigmoid(gate_value)
    silu = gate_value * gate_sigmoid
    hidden_low = (silu * up_value).astype(bf)
    grad_hidden = dot(grad_out, w_down, ((1,), (1,)))
    grad_gate = grad_hidden * up_value * gate_sigmoid * (1.0 + gate_value * (1.0 - gate_sigmoid))
    grad_both = jnp.concatenate([grad_gate.astype(bf), (grad_hidden * silu).astype(bf)], axis=1)
    grad_second = dot(grad_both, w_gate_up, ((1,), (1,))).astype(bf)
    down_partial = dot(hidden_low, grad_out, ((0,), (0,))).astype(bf)
    out_partial = dot(hidden_low, w_down, ((1,), (0,))).astype(bf)
    grad_second, output, gate_up_grad = feed_reduce(grad_second, out_partial, normed_second, grad_both)
    output = (resid_mid + output).astype(bf)

    mid_part, f_gain_part, f_shift_part = norm_back(grad_second, unit_second, inverse_second, f_gain)
    grad_mid = cotangent[0].astype(f32) + mid_part
    grad_mid_low = grad_mid.astype(bf)
    grad_attended = dot(grad_mid_low, w_out, ((1,), (1,))).astype(bf)
    out_partial = dot(attended_low, grad_mid_low, ((0,), (0,))).astype(bf)
    grad_mixed, out_part, gate_grad, up_grad = attend_backward(
        grad_attended, queries, keys, values, attended, log_total, start, tables,
        out_partial.reshape(4, 4, 2, shard, width), gate_up_grad.reshape(8, shard, 8 * hidden),
    )
    grad_first = dot(grad_mixed, w_project, ((1,), (1,))).astype(bf)

    bias_part = jnp.sum(grad_mixed.astype(f32), axis=0).reshape(3, 1, local)
    bias_part = jnp.where(jnp.arange(8)[None, :, None] == b, bias_part, 0.0)
    bias_part = jnp.pad(bias_part.reshape(32, 3 * shard), ((0, 0), (0, 64)))
    bias_part = bias_part.reshape(4, 8, 2, 128).transpose(1, 0, 2, 3)
    grad_tokens, project_grad, down_grad, out_grad, vector = finish(
        grad_first, normed_first, grad_mixed, down_partial, out_part, tokens[0], a_gain[None], grad_mid,
        jnp.stack([f_gain_part, f_shift_part]), bias_part,
    )
    gains = jnp.where(b % 2 == 0, vector[:4, :shard], vector[:4, shard:])
    return (
        output[None], grad_tokens[None], gains[0], gains[1], project_grad,
        vector[4:6].reshape(-1)[: 3 * shard], out_grad, gains[2], gains[3], gate_grad, up_grad, down_grad,
    )


def solution(mesh):
    tokens = P("rows", "blk", None)
    vector, matrix = P(BOTH), P(BOTH, None)
    in_specs = (
        tokens, P("rows", "blk"), tokens, vector, vector, matrix, vector, matrix, vector, vector,
        matrix, matrix, matrix,
    )
    out_specs = (
        tokens, tokens, vector, vector, matrix, vector, matrix, vector, vector, matrix, matrix, matrix,
    )
    if (mesh.shape["rows"], mesh.shape["blk"]) == (4, 8):
        body = fast_body
    else:
        body = make_body(mesh.shape["rows"], mesh.shape["blk"])
    return jax.shard_map(body, mesh=mesh, in_specs=in_specs, out_specs=out_specs, check_vma=False)
```

```python
import functools
import math

import jax
import jax.numpy as jnp
from jax import lax
from jax.experimental import pallas as pl
from jax.experimental.pallas import tpu as pltpu
from jax.sharding import PartitionSpec as P

HEADS = 32
ROT = 16
BOTH = ("rows", "blk")

epsilon = 1e-05
rotary_base = 10000.0
masked_value = -1e30


def dot(left, right, contract):
    return lax.dot_general(
        left, right, (contract, ((), ())), preferred_element_type=jnp.float32
    )


def norm_stats(inputs):
    row_mean = jnp.mean(inputs, axis=-1, keepdims=True)
    centered = inputs - row_mean
    variance = jnp.mean(centered * centered, axis=-1, keepdims=True)
    inverse = lax.rsqrt(variance + epsilon)
    return centered * inverse, inverse


def norm_back(incoming, unit, inverse, gain):
    gain_part = jnp.sum(incoming * unit, axis=0)
    shift_part = jnp.sum(incoming, axis=0)
    unit_grad = incoming * gain
    grad = inverse * (
        unit_grad
        - jnp.mean(unit_grad, axis=-1, keepdims=True)
        - unit * jnp.mean(unit_grad * unit, axis=-1, keepdims=True)
    )
    return grad, gain_part, shift_part


def rotate(columns, cosine, sine, head_width):
    half = cosine.shape[1]
    heads = columns.reshape(columns.shape[0], -1, head_width)
    cosine, sine = cosine[:, None, :], sine[:, None, :]
    first, second, rest = heads[..., :half], heads[..., half : 2 * half], heads[..., 2 * half :]
    return jnp.concatenate(
        [first * cosine - second * sine, second * cosine + first * sine, rest], axis=-1
    ).reshape(columns.shape)


def gather_blk(rows):
    return lax.all_gather(rows, "blk", axis=0, tiled=True)


def scatter_blk(partial):
    return lax.psum_scatter(
        partial.astype(jnp.bfloat16), "blk", scatter_dimension=0, tiled=True
    ).astype(jnp.float32)


def gather_rows(shard):
    return lax.all_gather(shard, "rows", axis=0, tiled=True)


def scatter_rows(partial):
    return lax.psum_scatter(
        partial.astype(jnp.bfloat16), "rows", scatter_dimension=0, tiled=True
    )


def exchange_blk(pieces):
    return lax.all_to_all(pieces, "blk", split_axis=0, concat_axis=0, tiled=True)


def make_body(group, ranks):
    def columns_of(shard, parts, inner):
        depth = shard.shape[0]
        pieces = shard.reshape(depth, parts, ranks, inner).transpose(2, 0, 1, 3)
        pieces = exchange_blk(pieces.reshape(ranks, depth, parts * inner))
        return gather_rows(pieces.reshape(ranks * depth, parts * inner))

    def columns_back(grad, parts, inner):
        owned = scatter_rows(grad)
        depth = owned.shape[0] // ranks
        pieces = exchange_blk(owned.reshape(ranks, depth, parts * inner))
        pieces = pieces.reshape(ranks, depth, parts, inner).transpose(1, 2, 0, 3)
        return pieces.reshape(depth, parts * ranks * inner).astype(jnp.float32)

    def body(
        tokens,
        segments,
        cotangent,
        attend_gain,
        attend_shift,
        project_weight,
        project_bias,
        output_weight,
        feed_gain,
        feed_shift,
        gate_weight,
        up_weight,
        down_weight,
    ):
        own_rows, width = tokens.shape[1], tokens.shape[2]
        length = own_rows * ranks
        head_width = width // HEADS
        local_heads = HEADS // ranks
        local_width = local_heads * head_width
        score_scale = 1.0 / math.sqrt(head_width)
        hidden_shard = down_weight.shape[0]
        shard = attend_gain.shape[0]
        me = lax.axis_index("blk")

        packed = jnp.concatenate(
            [
                attend_gain,
                attend_shift,
                feed_gain,
                feed_shift,
                project_bias,
                segments[0].astype(jnp.bfloat16),
            ]
        )
        packed = lax.all_gather(packed, BOTH, axis=0, tiled=False)
        a_gain = packed[:, :shard].reshape(-1).astype(jnp.float32)
        a_shift = packed[:, shard : 2 * shard].reshape(-1).astype(jnp.float32)
        f_gain = packed[:, 2 * shard : 3 * shard].reshape(-1).astype(jnp.float32)
        f_shift = packed[:, 3 * shard : 4 * shard].reshape(-1).astype(jnp.float32)
        bias = packed[:, 4 * shard : 7 * shard].reshape(3, ranks, local_width)
        bias = lax.dynamic_index_in_dim(bias, me, 1, False).reshape(-1).astype(jnp.float32)
        doc = packed[:, 7 * shard :].reshape(group, ranks * own_rows)
        doc = lax.dynamic_index_in_dim(doc, lax.axis_index("rows"), 0, False)

        w_project = columns_of(project_weight, 3, local_width)
        w_gate = columns_of(gate_weight, group, hidden_shard)
        w_up = columns_of(up_weight, group, hidden_shard)
        w_down = gather_rows(down_weight)
        w_out = lax.all_gather(output_weight, BOTH, axis=0, tiled=True)

        doc = doc.astype(jnp.int32)
        index = jnp.arange(length, dtype=jnp.int32)
        places = index - jnp.sum((doc[None, :] < doc[:, None]).astype(jnp.int32), axis=1)
        half = ROT // 2
        frequency = jnp.power(
            rotary_base, -jnp.arange(half, dtype=jnp.int32).astype(jnp.float32) / half
        )
        angles = places.astype(jnp.float32)[:, None] * frequency
        cosine, sine = jnp.cos(angles), jnp.sin(angles)
        mask = ((index[None, :] <= index[:, None]) & (doc[None, :] == doc[:, None]))[None]

        inputs = tokens[0].astype(jnp.float32)
        unit_first, inverse_first = norm_stats(inputs)
        normed_first = gather_blk((unit_first * a_gain + a_shift).astype(jnp.bfloat16))
        grad_out = gather_blk(cotangent[0])
        mixed = dot(normed_first, w_project, ((1,), (0,))) + bias
        queries = rotate(mixed[:, :local_width], cosine, sine, head_width).astype(jnp.bfloat16)
        keys = rotate(mixed[:, local_width : 2 * local_width], cosine, sine, head_width)
        keys = keys.astype(jnp.bfloat16)
        values = mixed[:, 2 * local_width :].astype(jnp.bfloat16)
        q_heads = queries.reshape(length, local_heads, head_width)
        k_heads = keys.reshape(length, local_heads, head_width)
        v_heads = values.reshape(length, local_heads, head_width)
        scores = jnp.einsum("qhd,khd->hqk", q_heads, k_heads, preferred_element_type=jnp.float32)
        scores = jnp.where(mask, scores * score_scale, masked_value)
        top = jnp.max(scores, axis=2, keepdims=True)
        weights = jnp.where(mask, jnp.exp(scores - top), 0.0)
        total = jnp.sum(weights, axis=2, keepdims=True)
        attended = jnp.einsum(
            "hqk,khd->qhd",
            weights.astype(jnp.bfloat16),
            v_heads,
            preferred_element_type=jnp.float32,
        ) / jnp.transpose(total[:, :, 0])[:, :, None]
        log_total = top + jnp.log(total)
        attended_flat = attended.reshape(length, local_width)
        attended_low = exchange_blk(
            attended_flat.astype(jnp.bfloat16).reshape(ranks, own_rows, local_width)
        )
        attended_low = attended_low.transpose(1, 0, 2).reshape(own_rows, width)
        resid_mid = inputs + dot(attended_low, w_out, ((1,), (0,)))

        unit_second, inverse_second = norm_stats(resid_mid)
        normed_second = gather_blk((unit_second * f_gain + f_shift).astype(jnp.bfloat16))
        gate_value = dot(normed_second, w_gate, ((1,), (0,)))
        up_value = dot(normed_second, w_up, ((1,), (0,)))
        gate_sigmoid = jax.nn.sigmoid(gate_value)
        silu = gate_value * gate_sigmoid
        hidden = (silu * up_value).astype(jnp.bfloat16)
        output = (resid_mid + scatter_blk(dot(hidden, w_down, ((1,), (0,))))).astype(jnp.bfloat16)

        grad_hidden = dot(grad_out, w_down, ((1,), (1,)))
        grad_gate = (
            grad_hidden * up_value * gate_sigmoid * (1.0 + gate_value * (1.0 - gate_sigmoid))
        ).astype(jnp.bfloat16)
        grad_up = (grad_hidden * silu).astype(jnp.bfloat16)
        grad_second = scatter_blk(
            dot(grad_gate, w_gate, ((1,), (1,))) + dot(grad_up, w_up, ((1,), (1,)))
        )
        down_grad = scatter_rows(dot(hidden, grad_out, ((0,), (0,)))).astype(jnp.float32)
        gate_grad = columns_back(dot(normed_second, grad_gate, ((0,), (0,))), group, hidden_shard)
        up_grad = columns_back(dot(normed_second, grad_up, ((0,), (0,))), group, hidden_shard)
        mid_part, f_gain_part, f_shift_part = norm_back(
            grad_second, unit_second, inverse_second, f_gain
        )
        grad_mid = cotangent[0].astype(jnp.float32) + mid_part
        grad_mid_low = grad_mid.astype(jnp.bfloat16)
        grad_attended = dot(grad_mid_low, w_out, ((1,), (1,))).astype(jnp.bfloat16)
        grad_attended = exchange_blk(
            grad_attended.reshape(own_rows, ranks, local_width).transpose(1, 0, 2)
        ).reshape(length, local_width)
        out_grad = lax.psum_scatter(
            dot(attended_low, grad_mid_low, ((0,), (0,))).astype(jnp.bfloat16),
            BOTH,
            scatter_dimension=0,
            tiled=True,
        ).astype(jnp.float32)

        g_heads = grad_attended.reshape(length, local_heads, head_width)
        delta = jnp.transpose(jnp.sum(g_heads.astype(jnp.float32) * attended, axis=2))
        probs = jnp.where(mask, jnp.exp(scores - log_total), 0.0)
        values_grad = jnp.einsum(
            "hqk,qhd->khd", probs.astype(jnp.bfloat16), g_heads, preferred_element_type=jnp.float32
        )
        grad_probs = jnp.einsum("qhd,khd->hqk", g_heads, v_heads, preferred_element_type=jnp.float32)
        grad_scores = (probs * (grad_probs - delta[:, :, None]) * score_scale).astype(jnp.bfloat16)
        grad_queries = jnp.einsum(
            "hqk,khd->qhd", grad_scores, k_heads, preferred_element_type=jnp.float32
        )
        keys_grad = jnp.einsum(
            "hqk,qhd->khd", grad_scores, q_heads, preferred_element_type=jnp.float32
        )
        grad_mixed = jnp.concatenate(
            [
                rotate(grad_queries.reshape(length, local_width), cosine, -sine, head_width),
                rotate(keys_grad.reshape(length, local_width), cosine, -sine, head_width),
                values_grad.reshape(length, local_width),
            ],
            axis=1,
        ).astype(jnp.bfloat16)
        grad_first = scatter_blk(dot(grad_mixed, w_project, ((1,), (1,))))
        project_grad = columns_back(
            dot(normed_first, grad_mixed, ((0,), (0,))), 3, local_width
        )
        bias_part = jnp.sum(grad_mixed.astype(jnp.float32), axis=0).reshape(3, 1, local_width)
        bias_part = jnp.where(jnp.arange(ranks)[None, :, None] == me, bias_part, 0.0)
        input_part, a_gain_part, a_shift_part = norm_back(
            grad_first, unit_first, inverse_first, a_gain
        )
        grad_tokens = grad_mid + input_part
        vectors = jnp.concatenate(
            [
                a_gain_part.reshape(-1, shard),
                a_shift_part.reshape(-1, shard),
                f_gain_part.reshape(-1, shard),
                f_shift_part.reshape(-1, shard),
                bias_part.reshape(-1, 3 * shard),
            ],
            axis=1,
        )
        vectors = lax.psum_scatter(vectors, BOTH, scatter_dimension=0, tiled=True)[0]
        return (
            output[None],
            grad_tokens[None],
            vectors[:shard],
            vectors[shard : 2 * shard],
            project_grad,
            vectors[4 * shard :],
            out_grad,
            vectors[2 * shard : 3 * shard],
            vectors[3 * shard : 4 * shard],
            gate_grad,
            up_grad,
            down_grad,
        )

    return body


MESH_ID = pl.DeviceIdType.MESH
DMA = pltpu.SemaphoreType.DMA
HBM = pl.ANY
VMEM = pltpu.VMEM
LIMIT = 60 * 1024 * 1024


class Place:
    def __init__(self):
        self.r = lax.axis_index("rows")
        self.b = lax.axis_index("blk")
        self.z = self.b // 2
        self.c = lax.rem(self.b, 2)
        self.sibling = 2 * self.z + 1 - self.c
        self.rx = self.r + 1 - 2 * lax.rem(self.r, 2)
        self.ry = lax.rem(self.r + 2, 4)
        self.rd = 3 - self.r

    def barrier(self, diagonal=False):
        sem = pltpu.get_barrier_semaphore()
        peers = [(self.r, lax.rem(self.b + k, 8)) for k in range(1, 8)]
        peers += [(self.rx, self.b), (self.ry, self.b)]
        if diagonal:
            peers.append((self.rd, self.b))
        for peer in peers:
            pl.semaphore_signal(sem, inc=1, device_id=peer, device_id_type=MESH_ID)
        pl.semaphore_wait(sem, len(peers))


def remote(src, dst, send, recv, r, b):
    return pltpu.make_async_remote_copy(
        src_ref=src, dst_ref=dst, send_sem=send, recv_sem=recv, device_id=(r, b), device_id_type=MESH_ID
    )


def drive(*jobs):
    active = list(jobs)
    while active:
        for job in list(active):
            try:
                next(job)
            except StopIteration:
                active.remove(job)


def later(job, count):
    for _ in range(count):
        yield
    yield from job


def steps(job, count):
    for _ in range(count):
        next(job, None)


CHUNKS = 2


def line_gather_sems():
    return [DMA((4, CHUNKS))] * 4 + [DMA((7, CHUNKS))] * 2 + [DMA((CHUNKS,))]


def line_gather(at, own, spot, sems, paired=True):
    up_send, down_send, up_recv, down_recv, pair_send, pair_recv, local_sem = sems

    def up(d, k, src):
        return remote(
            src, spot(at.z - d, at.c, k), up_send.at[d, k], up_recv.at[d, k], at.r, at.b + 2
        )

    def down(d, k, src):
        return remote(
            src, spot(at.z + d, at.c, k), down_send.at[d, k], down_recv.at[d, k], at.r, at.b - 2
        )

    def up_in(d, k):
        piece = spot(at.z - d - 1, at.c, k)
        return remote(piece, piece, up_send.at[d, k], up_recv.at[d, k], at.r, at.b + 2)

    def down_in(d, k):
        piece = spot(at.z + d + 1, at.c, k)
        return remote(piece, piece, down_send.at[d, k], down_recv.at[d, k], at.r, at.b - 2)

    def pair(i, k, z, src):
        return remote(
            src, spot(z, at.c, k), pair_send.at[i, k], pair_recv.at[i, k], at.r, at.sibling
        )

    def pair_in(i, k, z):
        piece = spot(z, 1 - at.c, k)
        return remote(piece, piece, pair_send.at[i, k], pair_recv.at[i, k], at.r, at.sibling)

    locals_ = [
        pltpu.make_async_copy(own(k), spot(at.z, at.c, k), local_sem.at[k]) for k in range(CHUNKS)
    ]
    for k in range(CHUNKS):
        locals_[k].start()
        pl.when(at.z < 3)(lambda: up(0, k, own(k)).start())
        pl.when(at.z > 0)(lambda: down(0, k, own(k)).start())
        if paired:
            pair(0, k, at.z, own(k)).start()
    yield
    for d in range(3):
        for k in range(CHUNKS):

            @pl.when(at.z - 1 - d >= 0)
            def _():
                z = at.z - 1 - d
                up_in(d, k).wait_recv()
                if d < 2:
                    pl.when(at.z < 3)(lambda: up(d + 1, k, spot(z, at.c, k)).start())
                if paired:
                    pair(1 + d, k, z, spot(z, at.c, k)).start()

            @pl.when(at.z + 1 + d <= 3)
            def _():
                z = at.z + 1 + d
                down_in(d, k).wait_recv()
                if d < 2:
                    pl.when(at.z > 0)(lambda: down(d + 1, k, spot(z, at.c, k)).start())
                if paired:
                    pair(4 + d, k, z, spot(z, at.c, k)).start()

            if d == 0:
                locals_[k].wait()
                if paired:
                    pair_in(0, k, at.z).wait_recv()
            if k == CHUNKS - 1 and paired:
                for part in range(CHUNKS):
                    pl.when(at.z - 1 - d >= 0)(
                        lambda: pair_in(1 + d, part, at.z - 1 - d).wait_recv()
                    )
                    pl.when(at.z + 1 + d <= 3)(
                        lambda: pair_in(4 + d, part, at.z + 1 + d).wait_recv()
                    )
            yield
    for k in range(CHUNKS):
        if paired:
            pair(0, k, at.z, own(k)).wait_send()
        pl.when(at.z < 3)(lambda: up(0, k, own(k)).wait_send())
        pl.when(at.z > 0)(lambda: down(0, k, own(k)).wait_send())
        for d in range(3):

            @pl.when(at.z - 1 - d >= 0)
            def _():
                z = at.z - 1 - d
                if paired:
                    pair(1 + d, k, z, spot(z, at.c, k)).wait_send()
                if d < 2:
                    pl.when(at.z < 3)(lambda: up(d + 1, k, spot(z, at.c, k)).wait_send())

            @pl.when(at.z + 1 + d <= 3)
            def _():
                z = at.z + 1 + d
                if paired:
                    pair(4 + d, k, z, spot(z, at.c, k)).wait_send()
                if d < 2:
                    pl.when(at.z > 0)(lambda: down(d + 1, k, spot(z, at.c, k)).wait_send())


def rows_of(ref, count):
    size = count // CHUNKS
    return lambda z, c, k: ref.at[pl.ds(pl.multiple_of((2 * z + c) * count + k * size, size), size)]


def cuts_of(ref):
    size = ref.shape[0] // CHUNKS
    return lambda k: ref.at[pl.ds(k * size, size)]


def line_scatter_scratch(count, width):
    block = VMEM((4, count, width), jnp.bfloat16)
    arrive = VMEM((3, count, width), jnp.bfloat16)
    return [block, arrive, arrive] + [DMA((4, CHUNKS))] * 2 + [DMA((3, CHUNKS))] * 4


def line_scatter(at, block, result, scratch, paired=True, prepare=None):
    held, from_below, from_above, pair_send, pair_recv, up_send, up_recv, down_send, down_recv = scratch
    count = held.shape[1]
    size = count // CHUNKS

    def cut(k):
        return pl.ds(k * size, size)

    def pair(z, k):
        return remote(
            block(z, 1 - at.c, k),
            held.at[z, cut(k)],
            pair_send.at[z, k],
            pair_recv.at[z, k],
            at.r,
            at.sibling,
        )

    def up(z, k):
        return remote(
            held.at[z, cut(k)],
            from_below.at[z - 1, cut(k)],
            up_send.at[z - 1, k],
            up_recv.at[z - 1, k],
            at.r,
            at.b + 2,
        )

    def down(z, k):
        return remote(
            held.at[z, cut(k)],
            from_above.at[z, cut(k)],
            down_send.at[z, k],
            down_recv.at[z, k],
            at.r,
            at.b - 2,
        )

    def wide(ref):
        return ref[...].astype(jnp.float32)

    def own(z, k):
        mine = wide(block(z, at.c, k))
        return mine + wide(held.at[z, cut(k)]) if paired else mine

    if paired:
        for z in (3, 0, 2, 1):
            if prepare:
                prepare(z)
            for k in range(CHUNKS):
                pair(z, k).start()
    yield
    for step in range(3):
        for k in range(CHUNKS):
            far, near = 3 - step, step

            @pl.when(at.z < far)
            def _():
                if paired:
                    pair(far, k).wait_recv()

                @pl.when(at.z == 0)
                def _():
                    held[far, cut(k)] = own(far, k).astype(jnp.bfloat16)

                @pl.when(at.z > 0)
                def _():
                    up(far, k).wait_recv()
                    held[far, cut(k)] = (
                        own(far, k) + wide(from_below.at[far - 1, cut(k)])
                    ).astype(jnp.bfloat16)

                up(far, k).start()

            @pl.when(at.z > near)
            def _():
                if paired:
                    pair(near, k).wait_recv()

                @pl.when(at.z == 3)
                def _():
                    held[near, cut(k)] = own(near, k).astype(jnp.bfloat16)

                @pl.when(at.z < 3)
                def _():
                    down(near, k).wait_recv()
                    held[near, cut(k)] = (
                        own(near, k) + wide(from_above.at[near, cut(k)])
                    ).astype(jnp.bfloat16)

                down(near, k).start()

            yield
    for z in range(4):
        for k in range(CHUNKS):

            @pl.when(at.z == z)
            def _():
                if paired:
                    pair(z, k).wait_recv()
                total = own(z, k)
                if z > 0:
                    up(z, k).wait_recv()
                    total += wide(from_below.at[z - 1, cut(k)])
                if z < 3:
                    down(z, k).wait_recv()
                    total += wide(from_above.at[z, cut(k)])
                result[cut(k)] = total.astype(result.dtype)

    for z in range(4):
        for k in range(CHUNKS):
            if paired:
                pair(z, k).wait_send()
            if z > 0:
                pl.when(at.z < z)(lambda: up(z, k).wait_send())
            if z < 3:
                pl.when(at.z > z)(lambda: down(z, k).wait_send())


def half_of(ref, axis, which):
    size = ref.shape[axis] // 2
    return ref.at[pl.ds(which * size, size)] if axis == 0 else ref.at[:, pl.ds(which * size, size)]


def row_halves(ref, axis=0):
    count = ref.shape[0] // 4
    return lambda r, which: half_of(
        ref.at[pl.ds(pl.multiple_of(r * count, count), count)], axis, which
    )


def square_gather_sems():
    return [DMA((6,)), DMA((6,)), DMA((2,))]


def square_gather(at, own, spot, sems, arrived=None):
    send, recv, local_sem = sems

    def copy(i, src, r_of, which, to):
        return remote(src, spot(r_of, which), send.at[i], recv.at[i], to, at.b)

    outs = [
        copy(0, own(0), at.r, 0, at.rx),
        copy(1, own(1), at.r, 1, at.ry),
        copy(2, own(1), at.r, 1, at.rx),
        copy(3, own(0), at.r, 0, at.ry),
    ]
    ins = [
        copy(0, spot(at.rx, 0), at.rx, 0, at.rx),
        copy(1, spot(at.ry, 1), at.ry, 1, at.ry),
        copy(2, spot(at.rx, 1), at.rx, 1, at.rx),
        copy(3, spot(at.ry, 0), at.ry, 0, at.ry),
        copy(4, spot(at.rd, 0), at.rd, 0, at.ry),
        copy(5, spot(at.rd, 1), at.rd, 1, at.rx),
    ]
    locals_ = [pltpu.make_async_copy(own(h), spot(at.r, h), local_sem.at[h]) for h in range(2)]
    for copy_ in outs + locals_:
        copy_.start()
    yield
    ins[0].wait_recv()
    outs.append(copy(4, spot(at.rx, 0), at.rx, 0, at.ry))
    outs[4].start()
    yield
    ins[1].wait_recv()
    outs.append(copy(5, spot(at.ry, 1), at.ry, 1, at.rx))
    outs[5].start()
    yield
    for copy_ in locals_:
        copy_.wait()
    for pair, r in (((2,), at.rx), ((3,), at.ry), ((4, 5), at.rd)):
        for i in pair:
            ins[i].wait_recv()
        if arrived:
            arrived(r)
    for out in outs:
        out.wait_send()


def square_scatter_scratch(count, width, axis=0):
    half = (count // 2, width) if axis == 0 else (count, width // 2)
    piece = VMEM((count, width), jnp.bfloat16)
    part = VMEM(half, jnp.bfloat16)
    return [piece, piece, part, part, part, part, DMA((6,)), DMA((6,))]


def square_scatter(at, part, result, scratch, axis=0, prepare=None):
    from_x, from_y, far_x, far_y, out_x, out_y, send, recv = scratch
    prepare = prepare or (lambda r: None)

    def wide(ref):
        return ref[...].astype(jnp.float32)

    copies = [
        remote(part(at.rd, 0), far_x, send.at[0], recv.at[0], at.rx, at.b),
        remote(part(at.rd, 1), far_y, send.at[1], recv.at[1], at.ry, at.b),
        remote(part(at.rx, 0), half_of(from_x, axis, 0), send.at[2], recv.at[2], at.rx, at.b),
        remote(part(at.ry, 1), half_of(from_y, axis, 1), send.at[3], recv.at[3], at.ry, at.b),
        remote(out_y, half_of(from_y, axis, 0), send.at[4], recv.at[4], at.ry, at.b),
        remote(out_x, half_of(from_x, axis, 1), send.at[5], recv.at[5], at.rx, at.b),
    ]
    prepare(at.rd)
    copies[0].start()
    copies[1].start()
    yield
    prepare(at.rx)
    copies[2].start()
    yield
    prepare(at.ry)
    copies[3].start()
    yield
    copies[0].wait_recv()
    out_y[...] = (wide(part(at.ry, 0)) + wide(far_x)).astype(jnp.bfloat16)
    copies[4].start()
    copies[1].wait_recv()
    out_x[...] = (wide(part(at.rx, 1)) + wide(far_y)).astype(jnp.bfloat16)
    copies[5].start()
    yield
    prepare(at.r)
    yield
    for i in (2, 3, 4, 5):
        copies[i].wait_recv()
    for which in range(2):
        total = (
            wide(part(at.r, which)) + wide(half_of(from_x, axis, which)) + wide(half_of(from_y, axis, which))
        )
        spot = half_of(result, axis, which)
        spot[...] = total.astype(result.dtype)
    for copy in copies:
        copy.wait_send()


def exchange_sems(parts=1):
    return [DMA((7, parts)), DMA((7, parts)), DMA((parts,))]


def exchange(at, take, put, sems, parts=1):
    send, recv, local_sem = sems
    locals_ = [
        pltpu.make_async_copy(take(at.b, p), put(at.b, p), local_sem.at[p]) for p in range(parts)
    ]
    outs, ins = [], []
    for k in (4, 3, 5, 2, 6, 1, 7):
        to, source = lax.rem(at.b + k, 8), lax.rem(at.b + 8 - k, 8)
        for p in range(parts):
            pair = (send.at[k - 1, p], recv.at[k - 1, p])
            outs.append(remote(take(to, p), put(at.b, p), *pair, at.r, to))
            ins.append(remote(put(source, p), put(source, p), *pair, at.r, source))
    for copy in locals_ + outs:
        copy.start()
    yield
    for copy in ins:
        copy.wait_recv()
    for copy in locals_:
        copy.wait()
    for copy in outs:
        copy.wait_send()


def call(kernel, ins, outs, scratch, number, *args):
    return pl.pallas_call(
        kernel,
        out_shape=[jax.ShapeDtypeStruct(shape, kind) for shape, kind, _ in outs],
        in_specs=[pl.BlockSpec(memory_space=space) for space in ins],
        out_specs=[pl.BlockSpec(memory_space=space) for _, _, space in outs],
        scratch_shapes=scratch,
        compiler_params=pltpu.CompilerParams(
            collective_id=number, has_side_effects=True, vmem_limit_bytes=LIMIT
        ),
    )(*args)


def vector_gather(at, own, full, sems):
    send, recv, local_sem = sems
    mine = 8 * at.r + at.b
    outs, ins = [], []
    for k in range(1, 8):
        to, source = lax.rem(at.b + k, 8), lax.rem(at.b + 8 - k, 8)
        outs.append(remote(own, full.at[mine], send.at[k - 1], recv.at[k - 1], at.r, to))
        piece = full.at[8 * at.r + source]
        ins.append(remote(piece, piece, send.at[k - 1], recv.at[k - 1], at.r, source))
    local = pltpu.make_async_copy(own, full.at[mine], local_sem)
    local.start()
    for out in outs:
        out.start()
    yield
    for copy in ins:
        copy.wait_recv()
    local.wait()
    group = full.at[pl.ds(8 * at.r, 8)]
    later = []
    for i, row in enumerate((at.rx, at.ry, at.rd)):
        outs.append(remote(group, group, send.at[7 + i], recv.at[7 + i], row, at.b))
        outs[-1].start()
        theirs = full.at[pl.ds(8 * row, 8)]
        later.append(remote(theirs, theirs, send.at[7 + i], recv.at[7 + i], row, at.b))
    yield
    for copy in later:
        copy.wait_recv()
    for out in outs:
        out.wait_send()


def make_tables(at, vectors, start, cosine, minus, plus):
    docs = jnp.concatenate(
        [vectors[8 * at.r + j, 6:7].astype(jnp.float32) for j in range(8)], axis=0
    )
    begins = jnp.zeros_like(docs)
    for doc in range(1, 5):
        before = jnp.sum((docs < doc).astype(jnp.float32), axis=(0, 1), keepdims=True)
        begins = jnp.where(docs == doc, before, begins)
    index = lax.broadcasted_iota(jnp.int32, docs.shape, 0) * 128
    index = (index + lax.broadcasted_iota(jnp.int32, docs.shape, 1)).astype(jnp.float32)
    places = index - begins
    half = ROT // 2
    row = lax.broadcasted_iota(jnp.int32, (half, 128), 0)
    frequency = jnp.zeros((half, 128), jnp.float32)
    for j in range(half):
        frequency = jnp.where(row == j, rotary_base ** (-j / half), frequency)
    eight = jnp.zeros((half, 128), jnp.float32)
    gap = jnp.zeros((48, 128), jnp.float32)
    for j in range(8):
        rows = slice(j * 128, j * 128 + 128)
        angles = frequency * places[j : j + 1]
        cos, sin = jnp.cos(angles), jnp.sin(angles)

        def table(first, second, rest):
            return jnp.transpose(jnp.concatenate([first, second, rest] * 2, axis=0))

        cosine[rows] = table(cos, cos, gap + 1.0)
        minus[rows] = table(-sin, eight, gap)
        plus[rows] = table(eight, sin, gap)
        start[rows] = jnp.transpose(jnp.broadcast_to(begins[j : j + 1], (128, 128))).astype(jnp.int32)
        yield


def start_kernel(
    x_ref, vector_ref, project_ref, down_ref, out_ref, gate_ref, up_ref,
    vectors, normed, pieces, w_project, w_down, w_out, gate_up, start, cosine, minus, plus,
    unit, own, vector_sems, exchange_sem, square_sem, down_sem, line_sems, out_sems,
):
    at = Place()
    at.barrier(diagonal=True)
    width = x_ref.shape[1]
    vector_job = vector_gather(at, vector_ref, vectors, vector_sems)
    next(vector_job)
    inner = w_project.shape[1] // 3
    depth = project_ref.shape[0]
    project_job = exchange(
        at,
        lambda b, p: project_ref.at[:, pl.ds(pl.multiple_of(p * width + b * inner, inner), inner)],
        lambda b, p: pieces.at[
            pl.ds(pl.multiple_of(b * depth, depth), depth), pl.ds(p * inner, inner)
        ],
        exchange_sem,
        3,
    )
    next(project_job)
    size = depth // CHUNKS
    out_job = line_gather(
        at, cuts_of(out_ref), lambda z, c, k: w_out.at[z, pl.ds(k * size, size)], out_sems, False
    )
    next(out_job)
    down_job = square_gather(
        at, lambda half: half_of(down_ref, 1, half), row_halves(w_down, 1), down_sem
    )
    next(down_job)
    x = x_ref[...].astype(jnp.float32)
    centered = x - jnp.mean(x, axis=1, keepdims=True)
    unit[...] = centered * lax.rsqrt(jnp.mean(centered * centered, axis=1, keepdims=True) + epsilon)
    drive(vector_job)
    for tile in range(width // 128):
        lanes = slice(tile * 128, tile * 128 + 128)
        both = vectors[2 * tile].astype(jnp.float32) + vectors[2 * tile + 1].astype(jnp.float32)
        own[:, lanes] = (unit[:, lanes] * both[0:1] + both[1:2]).astype(jnp.bfloat16)
    line_job = line_gather(at, cuts_of(own), rows_of(normed, own.shape[0]), line_sems)
    next(line_job)
    hidden = down_ref.shape[0]

    def reorder():
        for b in range(8):
            for r in range(4):
                source = slice((8 * r + b) * hidden, (8 * r + b + 1) * hidden)
                gate_up[b, :, r * hidden : (r + 1) * hidden] = gate_ref[:, source]
                gate_up[b, :, (4 + r) * hidden : (5 + r) * hidden] = up_ref[:, source]
            yield

    def project_work():
        yield from project_job
        yield from square_gather(
            at, lambda half: half_of(pieces, 0, half), row_halves(w_project), square_sem
        )

    table_job, order_job = make_tables(at, vectors, start, cosine, minus, plus), reorder()
    steps(table_job, 4)
    steps(order_job, 4)
    drive(out_job, line_job, project_work(), table_job, order_job, down_job)


def pack_sems(groups):
    flat, spans = [], []
    for group in groups:
        spans.append((len(flat), len(flat) + len(group)))
        flat += group
    return flat, spans


def grouped(kernel, lead, spans):
    def run(*refs):
        rest = refs[lead:]
        return kernel(*refs[:lead], *[rest[a:b] for a, b in spans])

    return run


def start_call(x, vector, project, down, out_weight, gate, up):
    rows, width = x.shape
    depth = project.shape[0]
    inner = project.shape[1] // 8
    bf, f32 = jnp.bfloat16, jnp.float32
    groups = [
        [DMA((10,)), DMA((10,)), DMA], exchange_sems(3), square_gather_sems(), square_gather_sems(),
        line_gather_sems(), line_gather_sems(),
    ]
    flat, spans = pack_sems(groups)
    outs = [
        ((32, 16, 128), bf, VMEM), ((8 * rows, width), bf, HBM), ((8 * depth, inner), bf, HBM),
        ((32 * depth, inner), bf, HBM), ((4 * down.shape[0], width), bf, HBM),
        ((4, depth, width), bf, HBM), ((8, depth, 8 * down.shape[0]), bf, VMEM),
        ((8 * rows, 128), jnp.int32, VMEM),
    ] + [((8 * rows, 128), f32, VMEM)] * 3
    scratch = [VMEM((rows, width), f32), VMEM((rows, width), bf)] + flat
    vectors, normed, _, w_project, w_down, w_out, gate_up, start, *tables = call(
        grouped(start_kernel, 20, spans), [VMEM, VMEM, HBM, HBM, HBM, VMEM, VMEM], outs, scratch, 0,
        x, vector, project, down, out_weight, gate, up,
    )
    return vectors, normed, w_project, w_down, w_out, gate_up, start, tables


def turned(columns, cosine, minus, plus):
    half = ROT // 2
    return (
        columns * cosine
        + pltpu.roll(columns, 128 - half, 1) * minus
        + pltpu.roll(columns, half, 1) * plus
    )


def score_mask(first_row, rows, keys, start):
    row = lax.broadcasted_iota(jnp.int32, (rows, keys), 0) + first_row
    col = lax.broadcasted_iota(jnp.int32, (rows, keys), 1)
    return (col <= row) & (col >= start)


QROWS = 256


def attend_forward_kernel(
    x_ref, w_ref, bias, start, cosine, minus, plus, tokens, feed_set, gate_up, out_ref,
    queries, keys, values, attended, log_total, mixed_heads, resid_mid, normed, gate_up_all, w_out,
    low, own_sems, gate_up_sems, square_sems, pair_sems,
):
    at = Place()
    at.barrier()
    pair_send, pair_recv = pair_sems

    def pair(i, r, src):
        return remote(src, w_out.at[r, :, at.c], pair_send.at[i], pair_recv.at[i], at.r, at.sibling)

    pairs = [pair(0, at.r, out_ref)] + [
        pair(i, r, w_out.at[r, :, at.c]) for i, r in ((1, at.rx), (2, at.ry), (3, at.rd))
    ]
    pairs[0].start()
    handed = iter(pairs[1:])
    out_job = square_gather(
        at,
        lambda half: half_of(out_ref, 0, half),
        lambda r, half: w_out.at[r, pl.ds(2 * half, 2), at.c],
        square_sems,
        lambda r: next(handed).start(),
    )
    next(out_job)
    length, local = queries.shape
    depth = gate_up.shape[1]
    gate_up_job = exchange(
        at, lambda b, p: gate_up.at[b], lambda b, p: gate_up_all.at[b], gate_up_sems
    )
    next(gate_up_job)
    scale = 1.0 / math.sqrt(local * 8 // HEADS)
    blocks = length // QROWS

    @pl.loop(0, blocks)
    def _(i):
        rows = pl.ds(pl.multiple_of(i * QROWS, QROWS), QROWS)
        mixed = dot(x_ref[rows], w_ref[...], ((1,), (0,))) + bias[...]
        tables = (cosine[rows], minus[rows], plus[rows])
        for pair in range(local // 128):
            lanes = slice(pair * 128, pair * 128 + 128)
            queries[rows, lanes] = turned(mixed[:, lanes], *tables).astype(jnp.bfloat16)
            shifted = slice(local + pair * 128, local + pair * 128 + 128)
            keys[rows, lanes] = turned(mixed[:, shifted], *tables).astype(jnp.bfloat16)
        values[rows] = mixed[:, 2 * local :].astype(jnp.bfloat16)

    send, recv, local_sem = own_sems

    def deliver(to):
        rows = low.at[pl.ds(to * 128, 128)]
        spot = mixed_heads.at[:, pl.ds(pl.multiple_of(at.b * local, local), local)]
        return remote(rows, spot, send.at[to], recv.at[at.b], at.r, to)

    for i in range(blocks):
        rows = slice(i * QROWS, (i + 1) * QROWS)
        count = (i + 1) * QROWS

        @pl.loop(0, local // 128)
        def _(pair):
            lanes = pl.ds(pl.multiple_of(pair * 128, 128), 128)
            lane = lax.broadcasted_iota(jnp.int32, (QROWS, 128), 1)
            q, k, v = queries[rows, lanes], keys[:count, lanes], values[:count, lanes]
            allowed = score_mask(i * QROWS, QROWS, count, start[rows, 0:1])
            found = []
            for head in range(2):
                mine = (lane >= 64) if head else (lane < 64)
                scores = dot(jnp.where(mine, q, jnp.zeros_like(q)), k, ((1,), (1,))) * scale
                scores = jnp.where(allowed, scores, masked_value)
                top = jnp.max(scores, axis=1, keepdims=True)
                weights = jnp.exp(scores - top)
                total = jnp.sum(weights, axis=1, keepdims=True)
                found.append(
                    (dot(weights.astype(jnp.bfloat16), v, ((1,), (0,))) / total, top + jnp.log(total))
                )
            both = jnp.where(lane < 64, found[0][0], found[1][0])
            attended[rows, lanes] = both
            low[rows, lanes] = both.astype(jnp.bfloat16)
            log_total[rows, lanes] = jnp.where(lane < 64, found[0][1], found[1][1])

        next(out_job, None)
        for to in range(i * QROWS // 128, (i + 1) * QROWS // 128):
            pl.when(at.b != to)(lambda: deliver(to).start())

            @pl.when(at.b == to)
            def _():
                pltpu.make_async_copy(
                    low.at[pl.ds(to * 128, 128)],
                    mixed_heads.at[:, pl.ds(pl.multiple_of(at.b * local, local), local)],
                    local_sem,
                ).start()

    drive(out_job)
    for source in range(8):

        @pl.when(at.b != source)
        def _():
            spot = mixed_heads.at[:, pl.ds(source * local, local)]
            remote(spot, spot, send.at[source], recv.at[source], at.r, source).wait_recv()

        @pl.when(at.b == source)
        def _():
            pltpu.make_async_copy(
                low.at[pl.ds(source * 128, 128)],
                mixed_heads.at[:, pl.ds(source * local, local)],
                local_sem,
            ).wait()

    total = tokens[...].astype(jnp.float32)
    depth, width = w_out.shape[3:]
    for i, r in enumerate((at.r, at.rx, at.ry, at.rd)):
        theirs = w_out.at[r, :, 1 - at.c]
        remote(theirs, theirs, pair_send.at[i], pair_recv.at[i], at.r, at.sibling).wait_recv()
    for r in range(4):
        lanes = slice(r * 8 * depth, (r + 1) * 8 * depth)
        total += dot(mixed_heads[:, lanes], w_out[r].reshape(8 * depth, width), ((1,), (0,)))
    resid_mid[...] = total
    unit, _ = norm_stats(total)
    normed[...] = (unit * feed_set[0:1] + feed_set[1:2]).astype(jnp.bfloat16)
    drive(gate_up_job)
    for to in range(8):
        pl.when(at.b != to)(lambda: deliver(to).wait_send())
    for copy in pairs:
        copy.wait_send()


def attend_forward(x, w, bias, start, tables, tokens, feed_set, gate_up, w_out):
    length, local = x.shape[0], w.shape[1] // 3
    bf, f32 = jnp.bfloat16, jnp.float32
    flat, spans = pack_sems(
        [[DMA((8,)), DMA((8,)), DMA], exchange_sems(), square_gather_sems(), [DMA((4,)), DMA((4,))]]
    )
    outs = [((length, local), bf, VMEM)] * 3 + [((length, local), f32, VMEM)] * 2
    outs += [(tokens.shape, bf, VMEM), (tokens.shape, f32, VMEM), (tokens.shape, bf, VMEM)]
    outs += [(gate_up.shape, bf, HBM), ((4, 4, 2) + w_out.shape[1:], bf, VMEM)]
    return call(
        grouped(attend_forward_kernel, 22, spans), [VMEM] * 9 + [HBM, HBM], outs,
        [VMEM((length, local), bf)] + flat, 1,
        x, w, bias, start, *tables, tokens, feed_set, gate_up, w_out,
    )


def feed_kernel(
    own, gate_up, cotangent, w_down,
    grad_out, hidden_out, output_sum, result, weight_result,
    normed, w_gate_up, values, out_partial, partial, weight,
    line_sems, other_sems, square_sems, out_scratch, scatter_scratch, square_scratch,
):
    at = Place()
    at.barrier()
    count = own.shape[0]
    hidden = hidden_out.shape[1]
    line_job = line_gather(at, cuts_of(own), rows_of(normed, count), line_sems)
    square_job = square_gather(
        at, lambda half: half_of(gate_up, 0, half), row_halves(w_gate_up), square_sems
    )
    other_job = line_gather(at, cuts_of(cotangent), rows_of(grad_out, count), other_sems)

    def rows_at(z):
        return pl.ds(pl.multiple_of(z * 2 * count, 2 * count), 2 * count)

    def forward(z):
        rows = rows_at(z)
        both = dot(normed[rows], w_gate_up[...], ((1,), (0,)))
        gate_value, up_value = both[:, :hidden], both[:, hidden:]
        low = (gate_value / (1.0 + jnp.exp(-gate_value)) * up_value).astype(jnp.bfloat16)
        hidden_out[rows] = low
        values[rows] = both.astype(jnp.bfloat16)
        out_partial[rows] = dot(low, w_down[...], ((1,), (0,))).astype(jnp.bfloat16)

    def backward(z):
        rows = rows_at(z)
        both = values[rows].astype(jnp.float32)
        gate_value, up_value = both[:, :hidden], both[:, hidden:]
        grad_hidden = dot(grad_out[rows], w_down[...], ((1,), (1,)))
        gate_sigmoid = 1.0 / (1.0 + jnp.exp(-gate_value))
        silu = gate_value * gate_sigmoid
        grad_gate = grad_hidden * up_value * gate_sigmoid * (1.0 + gate_value * (1.0 - gate_sigmoid))
        grads = jnp.concatenate([grad_gate, grad_hidden * silu], axis=1).astype(jnp.bfloat16)
        values[rows] = grads
        partial[rows] = dot(grads, w_gate_up[...], ((1,), (1,))).astype(jnp.bfloat16)

    out_job = line_scatter(at, rows_of(out_partial, count), output_sum, out_scratch)
    next(line_job)
    next(square_job)
    next(other_job)
    for i in range(4):
        steps(line_job, 1)
        steps(square_job, 1)
        steps(other_job, 1)
    steps(line_job, 2)
    drive(square_job)
    pl.loop(0, 2)(forward)
    steps(other_job, 1)
    pl.loop(2, 4)(forward)
    next(out_job)
    steps(other_job, 1)
    for z in range(4):
        backward(z)
        steps(out_job, 1)

    depth = weight_result.shape[0]
    step = depth // 2

    def prepare(r):
        for half in range(2):
            spot = pl.ds(pl.multiple_of(r * depth + half * step, step), step)
            weight[spot] = dot(normed[:, spot], values[...], ((0,), (0,))).astype(jnp.bfloat16)

    scatter_job = line_scatter(at, rows_of(partial, count), result, scatter_scratch)
    weight_job = square_scatter(at, row_halves(weight), weight_result, square_scratch, 0, prepare)
    next(scatter_job)
    steps(weight_job, 3)
    drive(out_job, scatter_job, weight_job, line_job, other_job)


def feed(own, gate_up, cotangent, w_down):
    bf, f32 = jnp.bfloat16, jnp.float32
    rows, width = own.shape
    hidden = w_down.shape[0]
    owned = (width // 4, 2 * hidden)
    full = (8 * rows, width)
    flat, spans = pack_sems(
        [
            line_gather_sems(), line_gather_sems(), square_gather_sems(),
            line_scatter_scratch(rows, width), line_scatter_scratch(rows, width),
            square_scatter_scratch(*owned),
        ]
    )
    outs = [(full, bf, VMEM), ((8 * rows, hidden), bf, VMEM)]
    outs += [((rows, width), f32, VMEM)] * 2 + [(owned, bf, VMEM)]
    scratch = [
        VMEM(full, bf), VMEM((width, 2 * hidden), bf), VMEM((8 * rows, 2 * hidden), bf), VMEM(full, bf),
        VMEM(full, bf), VMEM((width, 2 * hidden), bf),
    ]
    return call(
        grouped(feed_kernel, 15, spans), [VMEM, HBM, VMEM, VMEM], outs, scratch + flat, 2,
        own, gate_up, cotangent, w_down,
    )


def attend_backward_kernel(
    grad_second, resid_mid, cotangent, feed_gain, queries, keys, values, attended, log_total,
    start, cosine, minus, plus, mixed_heads, gate_up, out_weight,
    grad_mixed, out_result, gate_result, up_result, grad_mid, feed_sums,
    grad_rows, w_out, grad, keys_sum, values_sum, pieces, halves, heads_pair, mid_pair, product_rows,
    own_sems, square_scratch, pair_sems, gate_up_sems, load_sems,
):
    at = Place()
    load = pltpu.make_async_copy(out_weight, w_out, load_sems[0])
    load.start()
    unit, inverse = norm_stats(resid_mid[...])
    incoming = grad_second[...]
    mid_part, gain_part, shift_part = norm_back(incoming, unit, inverse, feed_gain[...])
    total = cotangent[...].astype(jnp.float32) + mid_part
    grad_mid[...] = total
    mid_pair[:128] = total.astype(jnp.bfloat16)
    heads_pair[:128] = mixed_heads[...]
    feed_sums[0:1] = gain_part[None]
    feed_sums[1:2] = shift_part[None]
    at.barrier()
    pair_send, pair_recv = pair_sems
    pairs = [
        remote(ref.at[pl.ds(0, 128)], ref.at[pl.ds(128, 128)], pair_send.at[i], pair_recv.at[i], at.r, at.sibling)
        for i, ref in enumerate((heads_pair, mid_pair))
    ]
    for copy in pairs:
        copy.start()
    load.wait()
    grad_rows[...] = dot(mid_pair[:128], w_out[...], ((1,), (1,))).astype(jnp.bfloat16)
    length, local = queries.shape
    scale = 1.0 / math.sqrt(local * 8 // HEADS)
    blocks = length // QROWS
    own_job = exchange(
        at,
        lambda b, p: grad_rows.at[:, pl.ds(pl.multiple_of(b * local, local), local)],
        lambda b, p: grad.at[pl.ds(pl.multiple_of(b * 128, 128), 128)],
        own_sems,
    )
    next(own_job)
    keys_sum[...] = jnp.zeros_like(keys_sum)
    values_sum[...] = jnp.zeros_like(values_sum)
    for copy in pairs:
        copy.wait()
    depth = halves.shape[2]

    def prepare(r):
        for z in range(4):
            lanes = pl.ds(pl.multiple_of((r * 4 + z) * 2 * depth, 2 * depth), 2 * depth)
            product_rows[...] = dot(heads_pair[:, lanes], mid_pair[...], ((0,), (0,)))
            mine = product_rows[pl.ds(pl.multiple_of(at.c * depth, depth), depth)]
            halves[r, z] = mine.astype(jnp.bfloat16)

    out_job = square_scatter(
        at, lambda r, half: halves.at[r, pl.ds(2 * half, 2)], out_result, square_scratch, 0, prepare
    )
    next(out_job)
    drive(own_job)
    gate_up_job = exchange(at, lambda b, p: gate_up.at[b], lambda b, p: pieces.at[b], gate_up_sems)
    next(gate_up_job)
    for i in range(blocks):
        rows = slice(i * QROWS, (i + 1) * QROWS)
        count = (i + 1) * QROWS

        @pl.loop(0, local // 128)
        def _(pair):
            lanes = pl.ds(pl.multiple_of(pair * 128, 128), 128)
            lane = lax.broadcasted_iota(jnp.int32, (QROWS, 128), 1)
            q, g = queries[rows, lanes], grad[rows, lanes]
            k, v = keys[:count, lanes], values[:count, lanes]
            allowed = score_mask(i * QROWS, QROWS, count, start[rows, 0:1])
            product = g.astype(jnp.float32) * attended[rows, lanes]
            logs = log_total[rows, lanes]
            queries_part, keys_part, values_part = [], [], []
            for head in range(2):
                mine = (lane >= 64) if head else (lane < 64)
                q_head = jnp.where(mine, q, jnp.zeros_like(q))
                g_head = jnp.where(mine, g, jnp.zeros_like(g))
                delta = jnp.sum(jnp.where(mine, product, 0.0), axis=1, keepdims=True)
                log_head = jnp.max(jnp.where(mine, logs, masked_value), axis=1, keepdims=True)
                scores = dot(q_head, k, ((1,), (1,))) * scale
                probs = jnp.exp(jnp.where(allowed, scores - log_head, masked_value))
                grad_probs = dot(g_head, v, ((1,), (1,)))
                grad_scores = (probs * (grad_probs - delta) * scale).astype(jnp.bfloat16)
                queries_part.append(dot(grad_scores, k, ((1,), (0,))))
                keys_part.append(dot(grad_scores, q_head, ((0,), (0,))))
                values_part.append(dot(probs.astype(jnp.bfloat16), g_head, ((0,), (0,))))
            both = jnp.where(lane < 64, queries_part[0], queries_part[1])
            tables = (cosine[rows], -minus[rows], -plus[rows])
            grad_mixed[rows, lanes] = turned(both, *tables).astype(jnp.bfloat16)
            keys_sum[:count, lanes] += keys_part[0] + keys_part[1]
            values_sum[:count, lanes] += values_part[0] + values_part[1]

        next(out_job, None)

    @pl.loop(0, blocks)
    def _(i):
        rows = pl.ds(pl.multiple_of(i * QROWS, QROWS), QROWS)
        tables = (cosine[rows], -minus[rows], -plus[rows])
        for pair in range(local // 128):
            lanes = slice(pair * 128, pair * 128 + 128)
            shifted = slice(local + pair * 128, local + pair * 128 + 128)
            grad_mixed[rows, shifted] = turned(keys_sum[rows, lanes], *tables).astype(jnp.bfloat16)
        grad_mixed[rows, slice(2 * local, 3 * local)] = values_sum[rows].astype(jnp.bfloat16)

    drive(out_job)
    drive(gate_up_job)
    hidden = pieces.shape[2] // 8
    for b in range(8):
        for r in range(4):
            source = slice((8 * r + b) * hidden, (8 * r + b + 1) * hidden)
            gate_result[:, source] = pieces[b, :, r * hidden : (r + 1) * hidden].astype(jnp.float32)
            up_result[:, source] = pieces[b, :, (4 + r) * hidden : (5 + r) * hidden].astype(jnp.float32)


def attend_backward(
    grad_second, resid_mid, cotangent, feed_gain, queries, keys, values, attended, log_total,
    start, tables, mixed_heads, gate_up, w_out,
):
    length, local = queries.shape
    bf, f32 = jnp.bfloat16, jnp.float32
    depth = gate_up.shape[1]
    rows, width = mixed_heads.shape
    quarter = [VMEM((4, depth, width), bf)] * 2 + [VMEM((2, depth, width), bf)] * 4
    flat, spans = pack_sems(
        [
            exchange_sems(), quarter + [DMA((6,)), DMA((6,))], [DMA((2,)), DMA((2,))], exchange_sems(),
            [DMA],
        ]
    )
    shard = (depth, 4 * gate_up.shape[2])
    outs = [((length, 3 * local), bf, VMEM), ((4, depth, width), bf, VMEM)] + [(shard, f32, VMEM)] * 2
    outs += [((rows, width), f32, VMEM), ((2, width), f32, VMEM)]
    scratch = [VMEM((rows, width), bf), VMEM((width, width), bf)]
    scratch += [VMEM((length, local), bf), VMEM((length, local), f32), VMEM((length, local), f32)]
    scratch += [VMEM(gate_up.shape, bf), VMEM((4, 4, depth, width), bf)]
    scratch += [VMEM((2 * rows, width), bf)] * 2 + [VMEM((2 * depth, width), f32)]
    return call(
        grouped(attend_backward_kernel, 32, spans), [VMEM] * 14 + [HBM] * 2, outs, scratch + flat, 4,
        grad_second, resid_mid, cotangent, feed_gain, queries, keys, values, attended, log_total,
        start, *tables, mixed_heads, gate_up, w_out,
    )


def finish_kernel(
    w_project, normed, grad_mixed, hidden, grad_out, out_part, x_ref, gain, grad_mid, feed_sums, bias_sums,
    tokens_grad, project_grad, down_grad, out_grad, vector_out,
    weight, weight_result, pieces, first, sums, arrived, summed, rows_in, down_partial, partial,
    line_scratch, project_scratch, down_scratch, out_scratch, piece_sems, vector_sems, row_sems,
):
    at = Place()
    at.barrier(diagonal=True)
    rows, width = first.shape
    depth = weight_result.shape[0]

    def prepare(r):
        spot = pl.ds(pl.multiple_of(r * depth, depth), depth)
        weight[spot] = dot(normed[:, spot], grad_mixed[...], ((0,), (0,))).astype(jnp.bfloat16)

    def prepare_down(r):
        count = down_grad.shape[0]
        for i in range(4):
            pl.when(r == i)(lambda: down_quarter(i, count))

    def down_quarter(i, count):
        rows_ = slice(i * count, (i + 1) * count)
        down_partial[rows_] = dot(hidden[:, rows_], grad_out[...], ((0,), (0,))).astype(jnp.bfloat16)

    shard = depth // 8
    size = shard // CHUNKS

    def prepare_rows(z):
        spot = slice(z * 2 * rows, (z + 1) * 2 * rows)
        partial[spot] = dot(grad_mixed[spot], w_project[...], ((1,), (1,))).astype(jnp.bfloat16)

    line_job = line_scatter(at, rows_of(partial, rows), first, line_scratch, True, prepare_rows)
    next(line_job)
    out_job = line_scatter(
        at, lambda z, c, k: out_part.at[z, pl.ds(k * size, size)], out_grad, out_scratch, False
    )

    def project_work():
        yield from square_scatter(at, row_halves(weight), weight_result, project_scratch, 0, prepare)
        yield from exchange(
            at,
            lambda b, p: weight_result.at[pl.ds(pl.multiple_of(b * shard, shard), shard)],
            lambda b, p: pieces.at[b],
            piece_sems,
        )

    project_job = project_work()
    down_job = square_scatter(
        at, row_halves(down_partial, 1), down_grad, down_scratch, 1, prepare_down
    )

    def vector_work():
        x = x_ref[...].astype(jnp.float32)
        centered = x - jnp.mean(x, axis=1, keepdims=True)
        inverse = lax.rsqrt(jnp.mean(centered * centered, axis=1, keepdims=True) + epsilon)
        unit = centered * inverse
        incoming = first[...]
        product = incoming * unit
        parts = jnp.concatenate(
            [
                jnp.sum(product, axis=0, keepdims=True),
                jnp.sum(incoming, axis=0, keepdims=True),
                feed_sums[...],
            ],
            axis=0,
        )
        for b in range(8):
            for r in range(4):
                lanes = slice((4 * r + b // 2) * 128, (4 * r + b // 2 + 1) * 128)
                sums[b, r, 0:4] = parts[:, lanes]
                sums[b, r, 4:6] = bias_sums[b, r]
                sums[b, r, 6:8] = jnp.zeros((2, 128), jnp.float32)
        spread = exchange(at, lambda b, p: sums.at[b], lambda b, p: arrived.at[b], vector_sems)
        next(spread)
        unit_grad = incoming * gain[...]
        tokens_grad[...] = grad_mid[...] + inverse * (
            unit_grad
            - jnp.mean(unit_grad, axis=1, keepdims=True)
            - unit * jnp.mean(unit_grad * unit, axis=1, keepdims=True)
        )
        drive(spread)
        summed[...] = jnp.sum(arrived[...], axis=0)
        send, recv = row_sems
        copies = [
            remote(summed.at[row], rows_in.at[i], send.at[i], recv.at[i], row, at.b)
            for i, row in enumerate((at.rx, at.ry, at.rd))
        ]
        for copy in copies:
            copy.start()
        for copy in copies:
            copy.wait()
        vector_out[...] = summed[at.r] + rows_in[0] + rows_in[1] + rows_in[2]

    steps(project_job, 3)
    steps(line_job, 2)
    next(project_job)
    steps(line_job, 1)
    next(project_job)
    steps(line_job, 1)
    next(project_job)
    next(out_job)
    next(down_job)
    drive(line_job, out_job, limited(down_job, 3))
    vector_work()
    drive(down_job, project_job)
    inner = pieces.shape[2] // 3
    for b in range(8):
        for p in range(3):
            lanes = slice(p * width + b * inner, p * width + (b + 1) * inner)
            project_grad[:, lanes] = pieces[b, :, p * inner : (p + 1) * inner].astype(jnp.float32)


def limited(job, count):
    for _ in range(count):
        next(job)
        yield


def finish(
    w_project, normed, grad_mixed, hidden, grad_out, out_part, x, gain, grad_mid, feed_sums, bias_sums
):
    bf, f32 = jnp.bfloat16, jnp.float32
    rows, width = x.shape
    inner = grad_mixed.shape[1]
    depth = width // 4
    shard = depth // 8
    down_owned = (hidden.shape[1] // 4, width)
    flat, spans = pack_sems(
        [
            line_scatter_scratch(rows, width),
            square_scatter_scratch(depth, inner),
            square_scatter_scratch(*down_owned, 1),
            line_scatter_scratch(shard, width),
            exchange_sems(), exchange_sems(), [DMA((3,)), DMA((3,))],
        ]
    )
    outs = [
        ((rows, width), f32, VMEM), ((shard, 8 * inner), f32, VMEM), (down_owned, f32, VMEM),
        ((shard, width), f32, VMEM), ((8, 128), f32, VMEM),
    ]
    scratch = [
        VMEM((width, inner), bf), VMEM((depth, inner), bf), VMEM((8, shard, inner), bf),
        VMEM((rows, width), f32), VMEM((8, 4, 8, 128), f32), VMEM((8, 4, 8, 128), f32),
        VMEM((4, 8, 128), f32), VMEM((3, 8, 128), f32),
        VMEM((hidden.shape[1], width), bf), VMEM((8 * rows, width), bf),
    ]
    return call(
        grouped(finish_kernel, 26, spans), [VMEM] * 11, outs, scratch + flat, 5,
        w_project, normed, grad_mixed, hidden, grad_out, out_part, x, gain, grad_mid, feed_sums, bias_sums,
    )


def fast_body(
    tokens, segments, cotangent, attend_gain, attend_shift, project_weight, project_bias,
    output_weight, feed_gain, feed_shift, gate_weight, up_weight, down_weight,
):
    bf, f32 = jnp.bfloat16, jnp.float32
    own_rows, width = tokens.shape[1], tokens.shape[2]
    length = own_rows * 8
    head_width = width // HEADS
    local = width // 8
    hidden = down_weight.shape[0]
    shard = attend_gain.shape[0]
    b = lax.axis_index("blk")

    small = jnp.stack([attend_gain, attend_shift, feed_gain, feed_shift])
    zeros = jnp.zeros_like(small)
    small = jnp.where(
        b % 2 == 0, jnp.concatenate([small, zeros], 1), jnp.concatenate([zeros, small], 1)
    )
    rest = jnp.pad(project_bias, (0, 64)).reshape(2, 128)
    vector = jnp.concatenate(
        [small, rest, segments.astype(bf), jnp.zeros((9, 128), bf)], axis=0
    )

    vectors, normed_first, w_project, w_down, w_out, gate_up, start, tables = start_call(
        tokens[0], vector, project_weight, down_weight, output_weight, gate_weight, up_weight
    )

    def whole(row):
        pairs = vectors[:, row].reshape(16, 2, 128).astype(f32)
        return (pairs[:, 0] + pairs[:, 1]).reshape(-1)

    a_gain, f_gain, f_shift = whole(0), whole(2), whole(3)
    bias = vectors[:, 4:6].reshape(32, 256)[:, : 3 * shard].reshape(3, 8, local)
    bias = lax.dynamic_index_in_dim(bias, b, 1, False).reshape(1, -1).astype(f32)

    (
        queries, keys, values, attended, log_total, attended_low, resid_mid, normed_second, gate_up, w_out
    ) = attend_forward(
        normed_first, w_project, bias, start, tables, tokens[0], jnp.stack([f_gain, f_shift]), gate_up, w_out
    )
    grad_out, hidden_low, output, grad_second, gate_up_grad = feed(
        normed_second, gate_up.reshape(8 * shard, 8 * hidden), cotangent[0], w_down
    )
    output = (resid_mid + output).astype(bf)
    grad_mixed, out_part, gate_grad, up_grad, grad_mid, feed_sums = attend_backward(
        grad_second, resid_mid, cotangent[0], f_gain[None], queries, keys, values, attended, log_total,
        start, tables, attended_low, gate_up_grad.reshape(8, shard, 8 * hidden), w_out.reshape(width, width),
    )

    bias_part = jnp.sum(grad_mixed.astype(f32), axis=0).reshape(3, 1, local)
    bias_part = jnp.where(jnp.arange(8)[None, :, None] == b, bias_part, 0.0)
    bias_part = jnp.pad(bias_part.reshape(32, 3 * shard), ((0, 0), (0, 64)))
    bias_part = bias_part.reshape(4, 8, 2, 128).transpose(1, 0, 2, 3)
    grad_tokens, project_grad, down_grad, out_grad, vector = finish(
        w_project, normed_first, grad_mixed, hidden_low, grad_out, out_part, tokens[0], a_gain[None],
        grad_mid, feed_sums, bias_part,
    )
    gains = jnp.where(b % 2 == 0, vector[:4, :shard], vector[:4, shard:])
    return (
        output[None], grad_tokens[None], gains[0], gains[1], project_grad,
        vector[4:6].reshape(-1)[: 3 * shard], out_grad, gains[2], gains[3], gate_grad, up_grad, down_grad,
    )


def solution(mesh):
    tokens = P("rows", "blk", None)
    vector, matrix = P(BOTH), P(BOTH, None)
    in_specs = (
        tokens, P("rows", "blk"), tokens, vector, vector, matrix, vector, matrix, vector, vector,
        matrix, matrix, matrix,
    )
    out_specs = (
        tokens, tokens, vector, vector, matrix, vector, matrix, vector, vector, matrix, matrix, matrix,
    )
    if (mesh.shape["rows"], mesh.shape["blk"]) == (4, 8):
        body = fast_body
    else:
        body = make_body(mesh.shape["rows"], mesh.shape["blk"])
    return jax.shard_map(body, mesh=mesh, in_specs=in_specs, out_specs=out_specs, check_vma=False)
```

```python
import functools
import math

import jax
import jax.numpy as jnp
from jax import lax
from jax.experimental import pallas as pl
from jax.experimental.pallas import tpu as pltpu
from jax.sharding import PartitionSpec as P

HEADS = 32
ROT = 16
BOTH = ("rows", "blk")

epsilon = 1e-05
rotary_base = 10000.0
masked_value = -1e30


def dot(left, right, contract):
    return lax.dot_general(
        left, right, (contract, ((), ())), preferred_element_type=jnp.float32
    )


def norm_stats(inputs):
    row_mean = jnp.mean(inputs, axis=-1, keepdims=True)
    centered = inputs - row_mean
    variance = jnp.mean(centered * centered, axis=-1, keepdims=True)
    inverse = lax.rsqrt(variance + epsilon)
    return centered * inverse, inverse


def norm_back(incoming, unit, inverse, gain):
    gain_part = jnp.sum(incoming * unit, axis=0)
    shift_part = jnp.sum(incoming, axis=0)
    unit_grad = incoming * gain
    grad = inverse * (
        unit_grad
        - jnp.mean(unit_grad, axis=-1, keepdims=True)
        - unit * jnp.mean(unit_grad * unit, axis=-1, keepdims=True)
    )
    return grad, gain_part, shift_part


def rotate(columns, cosine, sine, head_width):
    half = cosine.shape[1]
    heads = columns.reshape(columns.shape[0], -1, head_width)
    cosine, sine = cosine[:, None, :], sine[:, None, :]
    first, second, rest = heads[..., :half], heads[..., half : 2 * half], heads[..., 2 * half :]
    return jnp.concatenate(
        [first * cosine - second * sine, second * cosine + first * sine, rest], axis=-1
    ).reshape(columns.shape)


def gather_blk(rows):
    return lax.all_gather(rows, "blk", axis=0, tiled=True)


def scatter_blk(partial):
    return lax.psum_scatter(
        partial.astype(jnp.bfloat16), "blk", scatter_dimension=0, tiled=True
    ).astype(jnp.float32)


def gather_rows(shard):
    return lax.all_gather(shard, "rows", axis=0, tiled=True)


def scatter_rows(partial):
    return lax.psum_scatter(
        partial.astype(jnp.bfloat16), "rows", scatter_dimension=0, tiled=True
    )


def exchange_blk(pieces):
    return lax.all_to_all(pieces, "blk", split_axis=0, concat_axis=0, tiled=True)


def make_body(group, ranks):
    def columns_of(shard, parts, inner):
        depth = shard.shape[0]
        pieces = shard.reshape(depth, parts, ranks, inner).transpose(2, 0, 1, 3)
        pieces = exchange_blk(pieces.reshape(ranks, depth, parts * inner))
        return gather_rows(pieces.reshape(ranks * depth, parts * inner))

    def columns_back(grad, parts, inner):
        owned = scatter_rows(grad)
        depth = owned.shape[0] // ranks
        pieces = exchange_blk(owned.reshape(ranks, depth, parts * inner))
        pieces = pieces.reshape(ranks, depth, parts, inner).transpose(1, 2, 0, 3)
        return pieces.reshape(depth, parts * ranks * inner).astype(jnp.float32)

    def body(
        tokens,
        segments,
        cotangent,
        attend_gain,
        attend_shift,
        project_weight,
        project_bias,
        output_weight,
        feed_gain,
        feed_shift,
        gate_weight,
        up_weight,
        down_weight,
    ):
        own_rows, width = tokens.shape[1], tokens.shape[2]
        length = own_rows * ranks
        head_width = width // HEADS
        local_heads = HEADS // ranks
        local_width = local_heads * head_width
        score_scale = 1.0 / math.sqrt(head_width)
        hidden_shard = down_weight.shape[0]
        shard = attend_gain.shape[0]
        me = lax.axis_index("blk")

        packed = jnp.concatenate(
            [
                attend_gain,
                attend_shift,
                feed_gain,
                feed_shift,
                project_bias,
                segments[0].astype(jnp.bfloat16),
            ]
        )
        packed = lax.all_gather(packed, BOTH, axis=0, tiled=False)
        a_gain = packed[:, :shard].reshape(-1).astype(jnp.float32)
        a_shift = packed[:, shard : 2 * shard].reshape(-1).astype(jnp.float32)
        f_gain = packed[:, 2 * shard : 3 * shard].reshape(-1).astype(jnp.float32)
        f_shift = packed[:, 3 * shard : 4 * shard].reshape(-1).astype(jnp.float32)
        bias = packed[:, 4 * shard : 7 * shard].reshape(3, ranks, local_width)
        bias = lax.dynamic_index_in_dim(bias, me, 1, False).reshape(-1).astype(jnp.float32)
        doc = packed[:, 7 * shard :].reshape(group, ranks * own_rows)
        doc = lax.dynamic_index_in_dim(doc, lax.axis_index("rows"), 0, False)

        w_project = columns_of(project_weight, 3, local_width)
        w_gate = columns_of(gate_weight, group, hidden_shard)
        w_up = columns_of(up_weight, group, hidden_shard)
        w_down = gather_rows(down_weight)
        w_out = lax.all_gather(output_weight, BOTH, axis=0, tiled=True)

        doc = doc.astype(jnp.int32)
        index = jnp.arange(length, dtype=jnp.int32)
        places = index - jnp.sum((doc[None, :] < doc[:, None]).astype(jnp.int32), axis=1)
        half = ROT // 2
        frequency = jnp.power(
            rotary_base, -jnp.arange(half, dtype=jnp.int32).astype(jnp.float32) / half
        )
        angles = places.astype(jnp.float32)[:, None] * frequency
        cosine, sine = jnp.cos(angles), jnp.sin(angles)
        mask = ((index[None, :] <= index[:, None]) & (doc[None, :] == doc[:, None]))[None]

        inputs = tokens[0].astype(jnp.float32)
        unit_first, inverse_first = norm_stats(inputs)
        normed_first = gather_blk((unit_first * a_gain + a_shift).astype(jnp.bfloat16))
        grad_out = gather_blk(cotangent[0])
        mixed = dot(normed_first, w_project, ((1,), (0,))) + bias
        queries = rotate(mixed[:, :local_width], cosine, sine, head_width).astype(jnp.bfloat16)
        keys = rotate(mixed[:, local_width : 2 * local_width], cosine, sine, head_width)
        keys = keys.astype(jnp.bfloat16)
        values = mixed[:, 2 * local_width :].astype(jnp.bfloat16)
        q_heads = queries.reshape(length, local_heads, head_width)
        k_heads = keys.reshape(length, local_heads, head_width)
        v_heads = values.reshape(length, local_heads, head_width)
        scores = jnp.einsum("qhd,khd->hqk", q_heads, k_heads, preferred_element_type=jnp.float32)
        scores = jnp.where(mask, scores * score_scale, masked_value)
        top = jnp.max(scores, axis=2, keepdims=True)
        weights = jnp.where(mask, jnp.exp(scores - top), 0.0)
        total = jnp.sum(weights, axis=2, keepdims=True)
        attended = jnp.einsum(
            "hqk,khd->qhd",
            weights.astype(jnp.bfloat16),
            v_heads,
            preferred_element_type=jnp.float32,
        ) / jnp.transpose(total[:, :, 0])[:, :, None]
        log_total = top + jnp.log(total)
        attended_flat = attended.reshape(length, local_width)
        attended_low = exchange_blk(
            attended_flat.astype(jnp.bfloat16).reshape(ranks, own_rows, local_width)
        )
        attended_low = attended_low.transpose(1, 0, 2).reshape(own_rows, width)
        resid_mid = inputs + dot(attended_low, w_out, ((1,), (0,)))

        unit_second, inverse_second = norm_stats(resid_mid)
        normed_second = gather_blk((unit_second * f_gain + f_shift).astype(jnp.bfloat16))
        gate_value = dot(normed_second, w_gate, ((1,), (0,)))
        up_value = dot(normed_second, w_up, ((1,), (0,)))
        gate_sigmoid = jax.nn.sigmoid(gate_value)
        silu = gate_value * gate_sigmoid
        hidden = (silu * up_value).astype(jnp.bfloat16)
        output = (resid_mid + scatter_blk(dot(hidden, w_down, ((1,), (0,))))).astype(jnp.bfloat16)

        grad_hidden = dot(grad_out, w_down, ((1,), (1,)))
        grad_gate = (
            grad_hidden * up_value * gate_sigmoid * (1.0 + gate_value * (1.0 - gate_sigmoid))
        ).astype(jnp.bfloat16)
        grad_up = (grad_hidden * silu).astype(jnp.bfloat16)
        grad_second = scatter_blk(
            dot(grad_gate, w_gate, ((1,), (1,))) + dot(grad_up, w_up, ((1,), (1,)))
        )
        down_grad = scatter_rows(dot(hidden, grad_out, ((0,), (0,)))).astype(jnp.float32)
        gate_grad = columns_back(dot(normed_second, grad_gate, ((0,), (0,))), group, hidden_shard)
        up_grad = columns_back(dot(normed_second, grad_up, ((0,), (0,))), group, hidden_shard)
        mid_part, f_gain_part, f_shift_part = norm_back(
            grad_second, unit_second, inverse_second, f_gain
        )
        grad_mid = cotangent[0].astype(jnp.float32) + mid_part
        grad_mid_low = grad_mid.astype(jnp.bfloat16)
        grad_attended = dot(grad_mid_low, w_out, ((1,), (1,))).astype(jnp.bfloat16)
        grad_attended = exchange_blk(
            grad_attended.reshape(own_rows, ranks, local_width).transpose(1, 0, 2)
        ).reshape(length, local_width)
        out_grad = lax.psum_scatter(
            dot(attended_low, grad_mid_low, ((0,), (0,))).astype(jnp.bfloat16),
            BOTH,
            scatter_dimension=0,
            tiled=True,
        ).astype(jnp.float32)

        g_heads = grad_attended.reshape(length, local_heads, head_width)
        delta = jnp.transpose(jnp.sum(g_heads.astype(jnp.float32) * attended, axis=2))
        probs = jnp.where(mask, jnp.exp(scores - log_total), 0.0)
        values_grad = jnp.einsum(
            "hqk,qhd->khd", probs.astype(jnp.bfloat16), g_heads, preferred_element_type=jnp.float32
        )
        grad_probs = jnp.einsum("qhd,khd->hqk", g_heads, v_heads, preferred_element_type=jnp.float32)
        grad_scores = (probs * (grad_probs - delta[:, :, None]) * score_scale).astype(jnp.bfloat16)
        grad_queries = jnp.einsum(
            "hqk,khd->qhd", grad_scores, k_heads, preferred_element_type=jnp.float32
        )
        keys_grad = jnp.einsum(
            "hqk,qhd->khd", grad_scores, q_heads, preferred_element_type=jnp.float32
        )
        grad_mixed = jnp.concatenate(
            [
                rotate(grad_queries.reshape(length, local_width), cosine, -sine, head_width),
                rotate(keys_grad.reshape(length, local_width), cosine, -sine, head_width),
                values_grad.reshape(length, local_width),
            ],
            axis=1,
        ).astype(jnp.bfloat16)
        grad_first = scatter_blk(dot(grad_mixed, w_project, ((1,), (1,))))
        project_grad = columns_back(
            dot(normed_first, grad_mixed, ((0,), (0,))), 3, local_width
        )
        bias_part = jnp.sum(grad_mixed.astype(jnp.float32), axis=0).reshape(3, 1, local_width)
        bias_part = jnp.where(jnp.arange(ranks)[None, :, None] == me, bias_part, 0.0)
        input_part, a_gain_part, a_shift_part = norm_back(
            grad_first, unit_first, inverse_first, a_gain
        )
        grad_tokens = grad_mid + input_part
        vectors = jnp.concatenate(
            [
                a_gain_part.reshape(-1, shard),
                a_shift_part.reshape(-1, shard),
                f_gain_part.reshape(-1, shard),
                f_shift_part.reshape(-1, shard),
                bias_part.reshape(-1, 3 * shard),
            ],
            axis=1,
        )
        vectors = lax.psum_scatter(vectors, BOTH, scatter_dimension=0, tiled=True)[0]
        return (
            output[None],
            grad_tokens[None],
            vectors[:shard],
            vectors[shard : 2 * shard],
            project_grad,
            vectors[4 * shard :],
            out_grad,
            vectors[2 * shard : 3 * shard],
            vectors[3 * shard : 4 * shard],
            gate_grad,
            up_grad,
            down_grad,
        )

    return body


MESH_ID = pl.DeviceIdType.MESH
DMA = pltpu.SemaphoreType.DMA
HBM = pl.ANY
VMEM = pltpu.VMEM
LIMIT = 60 * 1024 * 1024


class Place:
    def __init__(self):
        self.r = lax.axis_index("rows")
        self.b = lax.axis_index("blk")
        self.z = self.b // 2
        self.c = lax.rem(self.b, 2)
        self.sibling = 2 * self.z + 1 - self.c
        self.rx = self.r + 1 - 2 * lax.rem(self.r, 2)
        self.ry = lax.rem(self.r + 2, 4)
        self.rd = 3 - self.r

    def barrier(self, diagonal=False):
        sem = pltpu.get_barrier_semaphore()
        peers = [(self.r, lax.rem(self.b + k, 8)) for k in range(1, 8)]
        peers += [(self.rx, self.b), (self.ry, self.b)]
        if diagonal:
            peers.append((self.rd, self.b))
        for peer in peers:
            pl.semaphore_signal(sem, inc=1, device_id=peer, device_id_type=MESH_ID)
        pl.semaphore_wait(sem, len(peers))


def remote(src, dst, send, recv, r, b):
    return pltpu.make_async_remote_copy(
        src_ref=src, dst_ref=dst, send_sem=send, recv_sem=recv, device_id=(r, b), device_id_type=MESH_ID
    )


def drive(*jobs):
    active = list(jobs)
    while active:
        for job in list(active):
            try:
                next(job)
            except StopIteration:
                active.remove(job)


def later(job, count):
    for _ in range(count):
        yield
    yield from job


def steps(job, count):
    for _ in range(count):
        next(job, None)


CHUNKS = 2


def line_gather_sems():
    return [DMA((4, CHUNKS))] * 4 + [DMA((7, CHUNKS))] * 2 + [DMA((CHUNKS,))]


def line_gather(at, own, spot, sems, paired=True):
    up_send, down_send, up_recv, down_recv, pair_send, pair_recv, local_sem = sems

    def up(d, k, src):
        return remote(
            src, spot(at.z - d, at.c, k), up_send.at[d, k], up_recv.at[d, k], at.r, at.b + 2
        )

    def down(d, k, src):
        return remote(
            src, spot(at.z + d, at.c, k), down_send.at[d, k], down_recv.at[d, k], at.r, at.b - 2
        )

    def up_in(d, k):
        piece = spot(at.z - d - 1, at.c, k)
        return remote(piece, piece, up_send.at[d, k], up_recv.at[d, k], at.r, at.b + 2)

    def down_in(d, k):
        piece = spot(at.z + d + 1, at.c, k)
        return remote(piece, piece, down_send.at[d, k], down_recv.at[d, k], at.r, at.b - 2)

    def pair(i, k, z, src):
        return remote(
            src, spot(z, at.c, k), pair_send.at[i, k], pair_recv.at[i, k], at.r, at.sibling
        )

    def pair_in(i, k, z):
        piece = spot(z, 1 - at.c, k)
        return remote(piece, piece, pair_send.at[i, k], pair_recv.at[i, k], at.r, at.sibling)

    locals_ = [
        pltpu.make_async_copy(own(k), spot(at.z, at.c, k), local_sem.at[k]) for k in range(CHUNKS)
    ]
    for k in range(CHUNKS):
        locals_[k].start()
        pl.when(at.z < 3)(lambda: up(0, k, own(k)).start())
        pl.when(at.z > 0)(lambda: down(0, k, own(k)).start())
        if paired:
            pair(0, k, at.z, own(k)).start()
    yield
    for d in range(3):
        for k in range(CHUNKS):

            @pl.when(at.z - 1 - d >= 0)
            def _():
                z = at.z - 1 - d
                up_in(d, k).wait_recv()
                if d < 2:
                    pl.when(at.z < 3)(lambda: up(d + 1, k, spot(z, at.c, k)).start())
                if paired:
                    pair(1 + d, k, z, spot(z, at.c, k)).start()

            @pl.when(at.z + 1 + d <= 3)
            def _():
                z = at.z + 1 + d
                down_in(d, k).wait_recv()
                if d < 2:
                    pl.when(at.z > 0)(lambda: down(d + 1, k, spot(z, at.c, k)).start())
                if paired:
                    pair(4 + d, k, z, spot(z, at.c, k)).start()

            if d == 0:
                locals_[k].wait()
                if paired:
                    pair_in(0, k, at.z).wait_recv()
            if k == CHUNKS - 1 and paired:
                for part in range(CHUNKS):
                    pl.when(at.z - 1 - d >= 0)(
                        lambda: pair_in(1 + d, part, at.z - 1 - d).wait_recv()
                    )
                    pl.when(at.z + 1 + d <= 3)(
                        lambda: pair_in(4 + d, part, at.z + 1 + d).wait_recv()
                    )
            yield
    for k in range(CHUNKS):
        if paired:
            pair(0, k, at.z, own(k)).wait_send()
        pl.when(at.z < 3)(lambda: up(0, k, own(k)).wait_send())
        pl.when(at.z > 0)(lambda: down(0, k, own(k)).wait_send())
        for d in range(3):

            @pl.when(at.z - 1 - d >= 0)
            def _():
                z = at.z - 1 - d
                if paired:
                    pair(1 + d, k, z, spot(z, at.c, k)).wait_send()
                if d < 2:
                    pl.when(at.z < 3)(lambda: up(d + 1, k, spot(z, at.c, k)).wait_send())

            @pl.when(at.z + 1 + d <= 3)
            def _():
                z = at.z + 1 + d
                if paired:
                    pair(4 + d, k, z, spot(z, at.c, k)).wait_send()
                if d < 2:
                    pl.when(at.z > 0)(lambda: down(d + 1, k, spot(z, at.c, k)).wait_send())


def rows_of(ref, count):
    size = count // CHUNKS
    return lambda z, c, k: ref.at[pl.ds(pl.multiple_of((2 * z + c) * count + k * size, size), size)]


def cuts_of(ref):
    size = ref.shape[0] // CHUNKS
    return lambda k: ref.at[pl.ds(k * size, size)]


def line_scatter_scratch(count, width):
    block = VMEM((4, count, width), jnp.bfloat16)
    arrive = VMEM((3, count, width), jnp.bfloat16)
    return [block, arrive, arrive] + [DMA((4, CHUNKS))] * 2 + [DMA((3, CHUNKS))] * 4


def line_scatter(at, block, result, scratch, paired=True, prepare=None):
    held, from_below, from_above, pair_send, pair_recv, up_send, up_recv, down_send, down_recv = scratch
    count = held.shape[1]
    size = count // CHUNKS

    def cut(k):
        return pl.ds(k * size, size)

    def pair(z, k):
        return remote(
            block(z, 1 - at.c, k),
            held.at[z, cut(k)],
            pair_send.at[z, k],
            pair_recv.at[z, k],
            at.r,
            at.sibling,
        )

    def up(z, k):
        return remote(
            held.at[z, cut(k)],
            from_below.at[z - 1, cut(k)],
            up_send.at[z - 1, k],
            up_recv.at[z - 1, k],
            at.r,
            at.b + 2,
        )

    def down(z, k):
        return remote(
            held.at[z, cut(k)],
            from_above.at[z, cut(k)],
            down_send.at[z, k],
            down_recv.at[z, k],
            at.r,
            at.b - 2,
        )

    def wide(ref):
        return ref[...].astype(jnp.float32)

    def own(z, k):
        mine = wide(block(z, at.c, k))
        return mine + wide(held.at[z, cut(k)]) if paired else mine

    if paired:
        for z in (3, 0, 2, 1):
            if prepare:
                prepare(z)
            for k in range(CHUNKS):
                pair(z, k).start()
    yield
    for step in range(3):
        for k in range(CHUNKS):
            far, near = 3 - step, step

            @pl.when(at.z < far)
            def _():
                if paired:
                    pair(far, k).wait_recv()

                @pl.when(at.z == 0)
                def _():
                    held[far, cut(k)] = own(far, k).astype(jnp.bfloat16)

                @pl.when(at.z > 0)
                def _():
                    up(far, k).wait_recv()
                    held[far, cut(k)] = (
                        own(far, k) + wide(from_below.at[far - 1, cut(k)])
                    ).astype(jnp.bfloat16)

                up(far, k).start()

            @pl.when(at.z > near)
            def _():
                if paired:
                    pair(near, k).wait_recv()

                @pl.when(at.z == 3)
                def _():
                    held[near, cut(k)] = own(near, k).astype(jnp.bfloat16)

                @pl.when(at.z < 3)
                def _():
                    down(near, k).wait_recv()
                    held[near, cut(k)] = (
                        own(near, k) + wide(from_above.at[near, cut(k)])
                    ).astype(jnp.bfloat16)

                down(near, k).start()

            yield
    for z in range(4):
        for k in range(CHUNKS):

            @pl.when(at.z == z)
            def _():
                if paired:
                    pair(z, k).wait_recv()
                total = own(z, k)
                if z > 0:
                    up(z, k).wait_recv()
                    total += wide(from_below.at[z - 1, cut(k)])
                if z < 3:
                    down(z, k).wait_recv()
                    total += wide(from_above.at[z, cut(k)])
                result[cut(k)] = total.astype(result.dtype)

    for z in range(4):
        for k in range(CHUNKS):
            if paired:
                pair(z, k).wait_send()
            if z > 0:
                pl.when(at.z < z)(lambda: up(z, k).wait_send())
            if z < 3:
                pl.when(at.z > z)(lambda: down(z, k).wait_send())


def half_of(ref, axis, which):
    size = ref.shape[axis] // 2
    return ref.at[pl.ds(which * size, size)] if axis == 0 else ref.at[:, pl.ds(which * size, size)]


def row_halves(ref, axis=0):
    count = ref.shape[0] // 4
    return lambda r, which: half_of(
        ref.at[pl.ds(pl.multiple_of(r * count, count), count)], axis, which
    )


def square_gather_sems():
    return [DMA((6,)), DMA((6,)), DMA((2,))]


def square_gather(at, own, spot, sems, arrived=None):
    send, recv, local_sem = sems

    def copy(i, src, r_of, which, to):
        return remote(src, spot(r_of, which), send.at[i], recv.at[i], to, at.b)

    outs = [
        copy(0, own(0), at.r, 0, at.rx),
        copy(1, own(1), at.r, 1, at.ry),
        copy(2, own(1), at.r, 1, at.rx),
        copy(3, own(0), at.r, 0, at.ry),
    ]
    ins = [
        copy(0, spot(at.rx, 0), at.rx, 0, at.rx),
        copy(1, spot(at.ry, 1), at.ry, 1, at.ry),
        copy(2, spot(at.rx, 1), at.rx, 1, at.rx),
        copy(3, spot(at.ry, 0), at.ry, 0, at.ry),
        copy(4, spot(at.rd, 0), at.rd, 0, at.ry),
        copy(5, spot(at.rd, 1), at.rd, 1, at.rx),
    ]
    locals_ = [pltpu.make_async_copy(own(h), spot(at.r, h), local_sem.at[h]) for h in range(2)]
    for copy_ in outs + locals_:
        copy_.start()
    yield
    ins[0].wait_recv()
    outs.append(copy(4, spot(at.rx, 0), at.rx, 0, at.ry))
    outs[4].start()
    yield
    ins[1].wait_recv()
    outs.append(copy(5, spot(at.ry, 1), at.ry, 1, at.rx))
    outs[5].start()
    yield
    for copy_ in locals_:
        copy_.wait()
    for pair, r in (((2,), at.rx), ((3,), at.ry), ((4, 5), at.rd)):
        for i in pair:
            ins[i].wait_recv()
        if arrived:
            arrived(r)
    for out in outs:
        out.wait_send()


def square_scatter_scratch(count, width, axis=0):
    half = (count // 2, width) if axis == 0 else (count, width // 2)
    piece = VMEM((count, width), jnp.bfloat16)
    part = VMEM(half, jnp.bfloat16)
    return [piece, piece, part, part, part, part, DMA((6,)), DMA((6,))]


def square_scatter(at, part, result, scratch, axis=0, prepare=None):
    from_x, from_y, far_x, far_y, out_x, out_y, send, recv = scratch
    prepare = prepare or (lambda r: None)

    def wide(ref):
        return ref[...].astype(jnp.float32)

    copies = [
        remote(part(at.rd, 0), far_x, send.at[0], recv.at[0], at.rx, at.b),
        remote(part(at.rd, 1), far_y, send.at[1], recv.at[1], at.ry, at.b),
        remote(part(at.rx, 0), half_of(from_x, axis, 0), send.at[2], recv.at[2], at.rx, at.b),
        remote(part(at.ry, 1), half_of(from_y, axis, 1), send.at[3], recv.at[3], at.ry, at.b),
        remote(out_y, half_of(from_y, axis, 0), send.at[4], recv.at[4], at.ry, at.b),
        remote(out_x, half_of(from_x, axis, 1), send.at[5], recv.at[5], at.rx, at.b),
    ]
    prepare(at.rd)
    copies[0].start()
    copies[1].start()
    yield
    prepare(at.rx)
    copies[2].start()
    yield
    prepare(at.ry)
    copies[3].start()
    yield
    copies[0].wait_recv()
    out_y[...] = (wide(part(at.ry, 0)) + wide(far_x)).astype(jnp.bfloat16)
    copies[4].start()
    copies[1].wait_recv()
    out_x[...] = (wide(part(at.rx, 1)) + wide(far_y)).astype(jnp.bfloat16)
    copies[5].start()
    yield
    prepare(at.r)
    yield
    for i in (2, 3, 4, 5):
        copies[i].wait_recv()
    for which in range(2):
        total = (
            wide(part(at.r, which)) + wide(half_of(from_x, axis, which)) + wide(half_of(from_y, axis, which))
        )
        spot = half_of(result, axis, which)
        spot[...] = total.astype(result.dtype)
    for copy in copies:
        copy.wait_send()


def exchange_sems(parts=1):
    return [DMA((7, parts)), DMA((7, parts)), DMA((parts,))]


def exchange(at, take, put, sems, parts=1):
    send, recv, local_sem = sems
    locals_ = [
        pltpu.make_async_copy(take(at.b, p), put(at.b, p), local_sem.at[p]) for p in range(parts)
    ]
    outs, ins = [], []
    for k in (4, 3, 5, 2, 6, 1, 7):
        to, source = lax.rem(at.b + k, 8), lax.rem(at.b + 8 - k, 8)
        for p in range(parts):
            pair = (send.at[k - 1, p], recv.at[k - 1, p])
            outs.append(remote(take(to, p), put(at.b, p), *pair, at.r, to))
            ins.append(remote(put(source, p), put(source, p), *pair, at.r, source))
    for copy in locals_ + outs:
        copy.start()
    yield
    for copy in ins:
        copy.wait_recv()
    for copy in locals_:
        copy.wait()
    for copy in outs:
        copy.wait_send()


def call(kernel, ins, outs, scratch, number, *args):
    return pl.pallas_call(
        kernel,
        out_shape=[jax.ShapeDtypeStruct(shape, kind) for shape, kind, _ in outs],
        in_specs=[pl.BlockSpec(memory_space=space) for space in ins],
        out_specs=[pl.BlockSpec(memory_space=space) for _, _, space in outs],
        scratch_shapes=scratch,
        compiler_params=pltpu.CompilerParams(
            collective_id=number, has_side_effects=True, vmem_limit_bytes=LIMIT
        ),
    )(*args)


def vector_gather(at, own, full, sems):
    send, recv, local_sem = sems
    mine = 8 * at.r + at.b
    outs, ins = [], []
    for k in range(1, 8):
        to, source = lax.rem(at.b + k, 8), lax.rem(at.b + 8 - k, 8)
        outs.append(remote(own, full.at[mine], send.at[k - 1], recv.at[k - 1], at.r, to))
        piece = full.at[8 * at.r + source]
        ins.append(remote(piece, piece, send.at[k - 1], recv.at[k - 1], at.r, source))
    local = pltpu.make_async_copy(own, full.at[mine], local_sem)
    local.start()
    for out in outs:
        out.start()
    yield
    for copy in ins:
        copy.wait_recv()
    local.wait()
    group = full.at[pl.ds(8 * at.r, 8)]
    later = []
    for i, row in enumerate((at.rx, at.ry, at.rd)):
        outs.append(remote(group, group, send.at[7 + i], recv.at[7 + i], row, at.b))
        outs[-1].start()
        theirs = full.at[pl.ds(8 * row, 8)]
        later.append(remote(theirs, theirs, send.at[7 + i], recv.at[7 + i], row, at.b))
    yield
    for copy in later:
        copy.wait_recv()
    for out in outs:
        out.wait_send()


def make_tables(at, vectors, start, cosine, minus, plus):
    docs = jnp.concatenate(
        [vectors[8 * at.r + j, 6:7].astype(jnp.float32) for j in range(8)], axis=0
    )
    begins = jnp.zeros_like(docs)
    for doc in range(1, 5):
        before = jnp.sum((docs < doc).astype(jnp.float32), axis=(0, 1), keepdims=True)
        begins = jnp.where(docs == doc, before, begins)
    index = lax.broadcasted_iota(jnp.int32, docs.shape, 0) * 128
    index = (index + lax.broadcasted_iota(jnp.int32, docs.shape, 1)).astype(jnp.float32)
    places = index - begins
    half = ROT // 2
    row = lax.broadcasted_iota(jnp.int32, (half, 128), 0)
    frequency = jnp.zeros((half, 128), jnp.float32)
    for j in range(half):
        frequency = jnp.where(row == j, rotary_base ** (-j / half), frequency)
    eight = jnp.zeros((half, 128), jnp.float32)
    gap = jnp.zeros((48, 128), jnp.float32)
    for j in range(8):
        rows = slice(j * 128, j * 128 + 128)
        angles = frequency * places[j : j + 1]
        cos, sin = jnp.cos(angles), jnp.sin(angles)

        def table(first, second, rest):
            return jnp.transpose(jnp.concatenate([first, second, rest] * 2, axis=0))

        cosine[rows] = table(cos, cos, gap + 1.0)
        minus[rows] = table(-sin, eight, gap)
        plus[rows] = table(eight, sin, gap)
        start[rows] = jnp.transpose(jnp.broadcast_to(begins[j : j + 1], (128, 128))).astype(jnp.int32)
        yield


def start_kernel(
    x_ref, vector_ref, project_ref, down_ref, out_ref, gate_ref, up_ref,
    vectors, normed, pieces, w_project, w_down, w_out, gate_up, start, cosine, minus, plus,
    unit, own, vector_sems, exchange_sem, square_sem, down_sem, line_sems, out_sems,
):
    at = Place()
    at.barrier(diagonal=True)
    width = x_ref.shape[1]
    vector_job = vector_gather(at, vector_ref, vectors, vector_sems)
    next(vector_job)
    inner = w_project.shape[1] // 3
    depth = project_ref.shape[0]
    project_job = exchange(
        at,
        lambda b, p: project_ref.at[:, pl.ds(pl.multiple_of(p * width + b * inner, inner), inner)],
        lambda b, p: pieces.at[
            pl.ds(pl.multiple_of(b * depth, depth), depth), pl.ds(p * inner, inner)
        ],
        exchange_sem,
        3,
    )
    next(project_job)
    size = depth // CHUNKS
    out_job = line_gather(
        at, cuts_of(out_ref), lambda z, c, k: w_out.at[z, pl.ds(k * size, size)], out_sems, False
    )
    next(out_job)
    down_job = square_gather(
        at, lambda half: half_of(down_ref, 1, half), row_halves(w_down, 1), down_sem
    )
    next(down_job)
    x = x_ref[...].astype(jnp.float32)
    centered = x - jnp.mean(x, axis=1, keepdims=True)
    unit[...] = centered * lax.rsqrt(jnp.mean(centered * centered, axis=1, keepdims=True) + epsilon)
    drive(vector_job)
    for tile in range(width // 128):
        lanes = slice(tile * 128, tile * 128 + 128)
        both = vectors[2 * tile].astype(jnp.float32) + vectors[2 * tile + 1].astype(jnp.float32)
        own[:, lanes] = (unit[:, lanes] * both[0:1] + both[1:2]).astype(jnp.bfloat16)
    line_job = line_gather(at, cuts_of(own), rows_of(normed, own.shape[0]), line_sems)
    next(line_job)
    hidden = down_ref.shape[0]

    def reorder():
        for b in range(8):
            for r in range(4):
                source = slice((8 * r + b) * hidden, (8 * r + b + 1) * hidden)
                gate_up[b, :, r * hidden : (r + 1) * hidden] = gate_ref[:, source]
                gate_up[b, :, (4 + r) * hidden : (5 + r) * hidden] = up_ref[:, source]
            yield

    def project_work():
        yield from project_job
        yield from square_gather(
            at, lambda half: half_of(pieces, 0, half), row_halves(w_project), square_sem
        )

    table_job, order_job = make_tables(at, vectors, start, cosine, minus, plus), reorder()
    steps(table_job, 4)
    steps(order_job, 4)
    drive(out_job, line_job, project_work(), table_job, order_job, down_job)


def pack_sems(groups):
    flat, spans = [], []
    for group in groups:
        spans.append((len(flat), len(flat) + len(group)))
        flat += group
    return flat, spans


def grouped(kernel, lead, spans):
    def run(*refs):
        rest = refs[lead:]
        return kernel(*refs[:lead], *[rest[a:b] for a, b in spans])

    return run


def start_call(x, vector, project, down, out_weight, gate, up):
    rows, width = x.shape
    depth = project.shape[0]
    inner = project.shape[1] // 8
    bf, f32 = jnp.bfloat16, jnp.float32
    groups = [
        [DMA((10,)), DMA((10,)), DMA], exchange_sems(3), square_gather_sems(), square_gather_sems(),
        line_gather_sems(), line_gather_sems(),
    ]
    flat, spans = pack_sems(groups)
    outs = [
        ((32, 16, 128), bf, VMEM), ((8 * rows, width), bf, HBM), ((8 * depth, inner), bf, HBM),
        ((32 * depth, inner), bf, HBM), ((4 * down.shape[0], width), bf, HBM),
        ((4, depth, width), bf, HBM), ((8, depth, 8 * down.shape[0]), bf, VMEM),
        ((8 * rows, 128), jnp.int32, VMEM),
    ] + [((8 * rows, 128), f32, VMEM)] * 3
    scratch = [VMEM((rows, width), f32), VMEM((rows, width), bf)] + flat
    vectors, normed, _, w_project, w_down, w_out, gate_up, start, *tables = call(
        grouped(start_kernel, 20, spans), [VMEM, VMEM, HBM, HBM, HBM, VMEM, VMEM], outs, scratch, 0,
        x, vector, project, down, out_weight, gate, up,
    )
    return vectors, normed, w_project, w_down, w_out, gate_up, start, tables


def turned(columns, cosine, minus, plus):
    half = ROT // 2
    return (
        columns * cosine
        + pltpu.roll(columns, 128 - half, 1) * minus
        + pltpu.roll(columns, half, 1) * plus
    )


def score_mask(first_row, rows, keys, start):
    row = lax.broadcasted_iota(jnp.int32, (rows, keys), 0) + first_row
    col = lax.broadcasted_iota(jnp.int32, (rows, keys), 1)
    return (col <= row) & (col >= start)


QROWS = 256


def attend_forward_kernel(
    x_ref, w_ref, bias, start, cosine, minus, plus, tokens, feed_set, gate_up, out_ref,
    queries, keys, values, attended, log_total, mixed_heads, resid_mid, normed, gate_up_all, w_out,
    low, own_sems, gate_up_sems, square_sems, pair_sems,
):
    at = Place()
    at.barrier()
    pair_send, pair_recv = pair_sems

    def pair(i, r, src):
        return remote(src, w_out.at[r, :, at.c], pair_send.at[i], pair_recv.at[i], at.r, at.sibling)

    pairs = [pair(0, at.r, out_ref)] + [
        pair(i, r, w_out.at[r, :, at.c]) for i, r in ((1, at.rx), (2, at.ry), (3, at.rd))
    ]
    pairs[0].start()
    handed = iter(pairs[1:])
    out_job = square_gather(
        at,
        lambda half: half_of(out_ref, 0, half),
        lambda r, half: w_out.at[r, pl.ds(2 * half, 2), at.c],
        square_sems,
        lambda r: next(handed).start(),
    )
    next(out_job)
    length, local = queries.shape
    depth = gate_up.shape[1]
    gate_up_job = exchange(
        at, lambda b, p: gate_up.at[b], lambda b, p: gate_up_all.at[b], gate_up_sems
    )
    next(gate_up_job)
    scale = 1.0 / math.sqrt(local * 8 // HEADS)
    blocks = length // QROWS

    @pl.loop(0, blocks)
    def _(i):
        rows = pl.ds(pl.multiple_of(i * QROWS, QROWS), QROWS)
        mixed = dot(x_ref[rows], w_ref[...], ((1,), (0,))) + bias[...]
        tables = (cosine[rows], minus[rows], plus[rows])
        for pair in range(local // 128):
            lanes = slice(pair * 128, pair * 128 + 128)
            queries[rows, lanes] = turned(mixed[:, lanes], *tables).astype(jnp.bfloat16)
            shifted = slice(local + pair * 128, local + pair * 128 + 128)
            keys[rows, lanes] = turned(mixed[:, shifted], *tables).astype(jnp.bfloat16)
        values[rows] = mixed[:, 2 * local :].astype(jnp.bfloat16)

    send, recv, local_sem = own_sems

    def deliver(to):
        rows = low.at[pl.ds(to * 128, 128)]
        spot = mixed_heads.at[:, pl.ds(pl.multiple_of(at.b * local, local), local)]
        return remote(rows, spot, send.at[to], recv.at[at.b], at.r, to)

    for i in range(blocks):
        rows = slice(i * QROWS, (i + 1) * QROWS)
        count = (i + 1) * QROWS

        @pl.loop(0, local // 128)
        def _(pair):
            lanes = pl.ds(pl.multiple_of(pair * 128, 128), 128)
            lane = lax.broadcasted_iota(jnp.int32, (QROWS, 128), 1)
            q, k, v = queries[rows, lanes], keys[:count, lanes], values[:count, lanes]
            allowed = score_mask(i * QROWS, QROWS, count, start[rows, 0:1])
            found = []
            for head in range(2):
                mine = (lane >= 64) if head else (lane < 64)
                scores = dot(jnp.where(mine, q, jnp.zeros_like(q)), k, ((1,), (1,))) * scale
                scores = jnp.where(allowed, scores, masked_value)
                top = jnp.max(scores, axis=1, keepdims=True)
                weights = jnp.exp(scores - top)
                total = jnp.sum(weights, axis=1, keepdims=True)
                found.append(
                    (dot(weights.astype(jnp.bfloat16), v, ((1,), (0,))) / total, top + jnp.log(total))
                )
            both = jnp.where(lane < 64, found[0][0], found[1][0])
            attended[rows, lanes] = both
            low[rows, lanes] = both.astype(jnp.bfloat16)
            log_total[rows, lanes] = jnp.where(lane < 64, found[0][1], found[1][1])

        next(out_job, None)
        for to in range(i * QROWS // 128, (i + 1) * QROWS // 128):
            pl.when(at.b != to)(lambda: deliver(to).start())

            @pl.when(at.b == to)
            def _():
                pltpu.make_async_copy(
                    low.at[pl.ds(to * 128, 128)],
                    mixed_heads.at[:, pl.ds(pl.multiple_of(at.b * local, local), local)],
                    local_sem,
                ).start()

    drive(out_job)
    for source in range(8):

        @pl.when(at.b != source)
        def _():
            spot = mixed_heads.at[:, pl.ds(source * local, local)]
            remote(spot, spot, send.at[source], recv.at[source], at.r, source).wait_recv()

        @pl.when(at.b == source)
        def _():
            pltpu.make_async_copy(
                low.at[pl.ds(source * 128, 128)],
                mixed_heads.at[:, pl.ds(source * local, local)],
                local_sem,
            ).wait()

    total = tokens[...].astype(jnp.float32)
    depth, width = w_out.shape[3:]
    for i, r in enumerate((at.r, at.rx, at.ry, at.rd)):
        theirs = w_out.at[r, :, 1 - at.c]
        remote(theirs, theirs, pair_send.at[i], pair_recv.at[i], at.r, at.sibling).wait_recv()
    for r in range(4):
        lanes = slice(r * 8 * depth, (r + 1) * 8 * depth)
        total += dot(mixed_heads[:, lanes], w_out[r].reshape(8 * depth, width), ((1,), (0,)))
    resid_mid[...] = total
    unit, _ = norm_stats(total)
    normed[...] = (unit * feed_set[0:1] + feed_set[1:2]).astype(jnp.bfloat16)
    drive(gate_up_job)
    for to in range(8):
        pl.when(at.b != to)(lambda: deliver(to).wait_send())
    for copy in pairs:
        copy.wait_send()


def attend_forward(x, w, bias, start, tables, tokens, feed_set, gate_up, w_out):
    length, local = x.shape[0], w.shape[1] // 3
    bf, f32 = jnp.bfloat16, jnp.float32
    flat, spans = pack_sems(
        [[DMA((8,)), DMA((8,)), DMA], exchange_sems(), square_gather_sems(), [DMA((4,)), DMA((4,))]]
    )
    outs = [((length, local), bf, VMEM)] * 3 + [((length, local), f32, VMEM)] * 2
    outs += [(tokens.shape, bf, VMEM), (tokens.shape, f32, VMEM), (tokens.shape, bf, VMEM)]
    outs += [(gate_up.shape, bf, HBM), ((4, 4, 2) + w_out.shape[1:], bf, VMEM)]
    return call(
        grouped(attend_forward_kernel, 22, spans), [VMEM] * 9 + [HBM, HBM], outs,
        [VMEM((length, local), bf)] + flat, 1,
        x, w, bias, start, *tables, tokens, feed_set, gate_up, w_out,
    )


def feed_kernel(
    own, gate_up, cotangent, w_down, resid_mid, feed_gain, out_weight,
    grad_out, hidden_out, output, weight_result, grad_mid, feed_sums, grad,
    normed, w_gate_up, values, out_partial, partial, output_sum, result, grad_rows,
    line_sems, other_sems, square_sems, out_scratch, scatter_scratch, square_scratch, own_sems, load_sems,
):
    at = Place()
    at.barrier()
    count = own.shape[0]
    hidden = hidden_out.shape[1]
    line_job = line_gather(at, cuts_of(own), rows_of(normed, count), line_sems)
    square_job = square_gather(
        at, lambda half: half_of(gate_up, 0, half), row_halves(w_gate_up), square_sems
    )
    other_job = line_gather(at, cuts_of(cotangent), rows_of(grad_out, count), other_sems)

    def rows_at(z):
        return pl.ds(pl.multiple_of(z * 2 * count, 2 * count), 2 * count)

    def hidden_back(z):
        rows = rows_at(z)
        partial[rows, :hidden] = dot(grad_out[rows], w_down[...], ((1,), (1,))).astype(jnp.bfloat16)

    def forward(z):
        rows = rows_at(z)
        both = dot(normed[rows], w_gate_up[...], ((1,), (0,)))
        gate_value, up_value = both[:, :hidden], both[:, hidden:]
        low = (gate_value / (1.0 + jnp.exp(-gate_value)) * up_value).astype(jnp.bfloat16)
        hidden_out[rows] = low
        values[rows] = both.astype(jnp.bfloat16)
        out_partial[rows] = dot(low, w_down[...], ((1,), (0,))).astype(jnp.bfloat16)

    def backward(z):
        rows = rows_at(z)
        both = values[rows].astype(jnp.float32)
        gate_value, up_value = both[:, :hidden], both[:, hidden:]
        grad_hidden = partial[rows, :hidden].astype(jnp.float32)
        gate_sigmoid = 1.0 / (1.0 + jnp.exp(-gate_value))
        silu = gate_value * gate_sigmoid
        grad_gate = grad_hidden * up_value * gate_sigmoid * (1.0 + gate_value * (1.0 - gate_sigmoid))
        grads = jnp.concatenate([grad_gate, grad_hidden * silu], axis=1).astype(jnp.bfloat16)
        values[rows] = grads
        partial[rows] = dot(grads, w_gate_up[...], ((1,), (1,))).astype(jnp.bfloat16)

    def near(i):
        return at.z + (i + 1) // 2 * (1 - 2 * lax.rem(i, 2))

    def far(i):
        return at.z + 3 * (2 * i - 1)

    def each(count, place, work):
        @pl.loop(0, count)
        def _(i):
            z = place(i)
            pl.when((z >= 0) & (z <= 3))(lambda: work(z))

    out_job = line_scatter(at, rows_of(out_partial, count), output_sum, out_scratch)
    next(line_job)
    next(square_job)
    next(other_job)
    for i in range(4):
        steps(line_job, 1)
        steps(square_job, 1)
        steps(other_job, 1)
    each(5, near, hidden_back)
    drive(square_job)
    each(5, near, forward)
    steps(line_job, 2)
    each(2, far, forward)
    next(out_job)
    steps(other_job, 2)
    each(2, far, hidden_back)
    for z in range(4):
        backward(z)
        steps(out_job, 1)

    depth = weight_result.shape[0]
    step = depth // 2

    def prepare(r):
        for half in range(2):
            spot = pl.ds(pl.multiple_of(r * depth + half * step, step), step)
            w_gate_up[spot] = dot(normed[:, spot], values[...], ((0,), (0,))).astype(jnp.bfloat16)

    scatter_job = line_scatter(at, rows_of(partial, count), result, scatter_scratch)
    weight_job = square_scatter(at, row_halves(w_gate_up), weight_result, square_scratch, 0, prepare)
    next(scatter_job)
    steps(weight_job, 3)
    drive(scatter_job, limited(weight_job, 2), line_job)
    half = out_partial.shape[0]
    loads = [
        pltpu.make_async_copy(out_weight.at[pl.ds(i * half, half)], place, load_sems[0].at[i])
        for i, place in enumerate((normed, partial))
    ]
    for load in loads:
        load.start()
    unit, inverse = norm_stats(resid_mid[...])
    mid_part, gain_part, shift_part = norm_back(result[...], unit, inverse, feed_gain[...])
    total = cotangent[...].astype(jnp.float32) + mid_part
    grad_mid[...] = total
    low = total.astype(jnp.bfloat16)
    feed_sums[0:1] = gain_part[None]
    feed_sums[1:2] = shift_part[None]
    for i, place in enumerate((normed, partial)):
        loads[i].wait()
        grad_rows[:, i * half : (i + 1) * half] = dot(low, place[...], ((1,), (1,))).astype(jnp.bfloat16)
    local = grad.shape[1]
    own_job = exchange(
        at,
        lambda b, p: grad_rows.at[:, pl.ds(pl.multiple_of(b * local, local), local)],
        lambda b, p: grad.at[pl.ds(pl.multiple_of(b * count, count), count)],
        own_sems,
    )
    next(own_job)
    drive(out_job, weight_job, other_job)
    output[...] = (resid_mid[...] + output_sum[...]).astype(jnp.bfloat16)
    drive(own_job)


def feed(own, gate_up, cotangent, w_down, resid_mid, feed_gain, w_out):
    bf, f32 = jnp.bfloat16, jnp.float32
    rows, width = own.shape
    hidden = w_down.shape[0]
    owned = (width // 4, 2 * hidden)
    full, mine = (8 * rows, width), (rows, width)
    flat, spans = pack_sems(
        [
            line_gather_sems(), line_gather_sems(), square_gather_sems(),
            line_scatter_scratch(rows, width), line_scatter_scratch(rows, width),
            square_scatter_scratch(*owned), exchange_sems(), [DMA((2,))],
        ]
    )
    outs = [(full, bf, VMEM), ((8 * rows, hidden), bf, VMEM), (mine, bf, VMEM), (owned, bf, VMEM)]
    outs += [(mine, f32, VMEM), ((2, width), f32, VMEM), ((8 * rows, width // 8), bf, VMEM)]
    scratch = [
        VMEM(full, bf), VMEM((width, 2 * hidden), bf), VMEM((8 * rows, 2 * hidden), bf), VMEM(full, bf),
        VMEM(full, bf), VMEM(mine, f32), VMEM(mine, f32), VMEM(mine, bf),
    ]
    return call(
        grouped(feed_kernel, 22, spans), [VMEM, HBM, VMEM, VMEM, VMEM, VMEM, HBM], outs, scratch + flat, 2,
        own, gate_up, cotangent, w_down, resid_mid, feed_gain, w_out,
    )


def limited(job, count):
    for _ in range(count):
        next(job)
        yield


def attend_backward_kernel(
    grad, grad_mid, queries, keys, values, attended, log_total,
    start, cosine, minus, plus, mixed_heads, gate_up,
    grad_mixed, out_result, gate_result, up_result,
    keys_sum, values_sum, pieces, halves, heads_pair, mid_pair, product_rows,
    square_scratch, pair_sems, gate_up_sems,
):
    at = Place()
    at.barrier()
    gate_up_job = exchange(at, lambda b, p: gate_up.at[b], lambda b, p: pieces.at[b], gate_up_sems)
    next(gate_up_job)
    mid_pair[:128] = grad_mid[...].astype(jnp.bfloat16)
    heads_pair[:128] = mixed_heads[...]
    pair_send, pair_recv = pair_sems
    pairs = [
        remote(ref.at[pl.ds(0, 128)], ref.at[pl.ds(128, 128)], pair_send.at[i], pair_recv.at[i], at.r, at.sibling)
        for i, ref in enumerate((heads_pair, mid_pair))
    ]
    for copy in pairs:
        copy.start()
    length, local = queries.shape
    scale = 1.0 / math.sqrt(local * 8 // HEADS)
    blocks = length // QROWS
    keys_sum[...] = jnp.zeros_like(keys_sum)
    values_sum[...] = jnp.zeros_like(values_sum)
    for copy in pairs:
        copy.wait()
    depth = halves.shape[2]

    def prepare(r):
        for z in range(4):
            lanes = pl.ds(pl.multiple_of((r * 4 + z) * 2 * depth, 2 * depth), 2 * depth)
            product_rows[...] = dot(heads_pair[:, lanes], mid_pair[...], ((0,), (0,)))
            mine = product_rows[pl.ds(pl.multiple_of(at.c * depth, depth), depth)]
            halves[r, z] = mine.astype(jnp.bfloat16)

    out_job = square_scatter(
        at, lambda r, half: halves.at[r, pl.ds(2 * half, 2)], out_result, square_scratch, 0, prepare
    )
    steps(out_job, 3)
    for i in range(blocks):
        rows = slice(i * QROWS, (i + 1) * QROWS)
        count = (i + 1) * QROWS

        @pl.loop(0, local // 128)
        def _(pair):
            lanes = pl.ds(pl.multiple_of(pair * 128, 128), 128)
            lane = lax.broadcasted_iota(jnp.int32, (QROWS, 128), 1)
            q, g = queries[rows, lanes], grad[rows, lanes]
            k, v = keys[:count, lanes], values[:count, lanes]
            allowed = score_mask(i * QROWS, QROWS, count, start[rows, 0:1])
            product = g.astype(jnp.float32) * attended[rows, lanes]
            logs = log_total[rows, lanes]
            queries_part, keys_part, values_part = [], [], []
            for head in range(2):
                mine = (lane >= 64) if head else (lane < 64)
                q_head = jnp.where(mine, q, jnp.zeros_like(q))
                g_head = jnp.where(mine, g, jnp.zeros_like(g))
                delta = jnp.sum(jnp.where(mine, product, 0.0), axis=1, keepdims=True)
                log_head = jnp.max(jnp.where(mine, logs, masked_value), axis=1, keepdims=True)
                scores = dot(q_head, k, ((1,), (1,))) * scale
                probs = jnp.exp(jnp.where(allowed, scores - log_head, masked_value))
                grad_probs = dot(g_head, v, ((1,), (1,)))
                grad_scores = (probs * (grad_probs - delta) * scale).astype(jnp.bfloat16)
                queries_part.append(dot(grad_scores, k, ((1,), (0,))))
                keys_part.append(dot(grad_scores, q_head, ((0,), (0,))))
                values_part.append(dot(probs.astype(jnp.bfloat16), g_head, ((0,), (0,))))
            both = jnp.where(lane < 64, queries_part[0], queries_part[1])
            tables = (cosine[rows], -minus[rows], -plus[rows])
            grad_mixed[rows, lanes] = turned(both, *tables).astype(jnp.bfloat16)
            keys_sum[:count, lanes] += keys_part[0] + keys_part[1]
            values_sum[:count, lanes] += values_part[0] + values_part[1]

        next(out_job, None)

    @pl.loop(0, blocks)
    def _(i):
        rows = pl.ds(pl.multiple_of(i * QROWS, QROWS), QROWS)
        tables = (cosine[rows], -minus[rows], -plus[rows])
        for pair in range(local // 128):
            lanes = slice(pair * 128, pair * 128 + 128)
            shifted = slice(local + pair * 128, local + pair * 128 + 128)
            grad_mixed[rows, shifted] = turned(keys_sum[rows, lanes], *tables).astype(jnp.bfloat16)
        grad_mixed[rows, slice(2 * local, 3 * local)] = values_sum[rows].astype(jnp.bfloat16)

    drive(out_job)
    drive(gate_up_job)
    hidden = pieces.shape[2] // 8
    for b in range(8):
        for r in range(4):
            source = slice((8 * r + b) * hidden, (8 * r + b + 1) * hidden)
            gate_result[:, source] = pieces[b, :, r * hidden : (r + 1) * hidden]
            up_result[:, source] = pieces[b, :, (4 + r) * hidden : (5 + r) * hidden]


def attend_backward(
    grad, grad_mid, queries, keys, values, attended, log_total, start, tables, mixed_heads, gate_up
):
    length, local = queries.shape
    bf, f32 = jnp.bfloat16, jnp.float32
    depth = gate_up.shape[1]
    rows, width = mixed_heads.shape
    quarter = [VMEM((4, depth, width), bf)] * 2 + [VMEM((2, depth, width), bf)] * 4
    flat, spans = pack_sems(
        [quarter + [DMA((6,)), DMA((6,))], [DMA((2,)), DMA((2,))], exchange_sems()]
    )
    shard = (depth, 4 * gate_up.shape[2])
    outs = [((length, 3 * local), bf, VMEM), ((4, depth, width), bf, VMEM)] + [(shard, bf, VMEM)] * 2
    scratch = [VMEM((length, local), f32), VMEM((length, local), f32)]
    scratch += [VMEM(gate_up.shape, bf), VMEM((4, 4, depth, width), bf)]
    scratch += [VMEM((2 * rows, width), bf)] * 2 + [VMEM((2 * depth, width), f32)]
    return call(
        grouped(attend_backward_kernel, 24, spans), [VMEM] * 12 + [HBM], outs, scratch + flat, 4,
        grad, grad_mid, queries, keys, values, attended, log_total, start, *tables, mixed_heads, gate_up,
    )


def finish_kernel(
    w_project, grad_mixed, out_part, x_ref, gain, feed_sums, bias_sums, normed_all, hidden_all,
    grad_out_all, tokens_part, project_grad, down_grad, out_grad, vector_out,
    weight, weight_result, pieces, first, sums, arrived, summed, rows_in, down_partial, partial, overlap,
    normed, hidden, grad_out,
    line_scratch, project_scratch, down_scratch, out_scratch, piece_sems, vector_sems, row_sems, load_sems,
):
    at = Place()
    loads = [
        pltpu.make_async_copy(*pair, load_sems[0].at[i])
        for i, pair in enumerate(((normed_all, normed), (hidden_all, hidden), (grad_out_all, grad_out)))
    ]
    for load in loads:
        load.start()
    at.barrier(diagonal=True)
    rows, width = first.shape
    depth = weight_result.shape[0]

    def prepare(r):
        spot = pl.ds(pl.multiple_of(r * depth, depth), depth)
        product = dot(normed[:, spot], grad_mixed[...], ((0,), (0,)))
        weight[spot] = product.astype(jnp.bfloat16)
        found = jnp.sum(product * w_project[spot].astype(jnp.float32), axis=1, keepdims=True)
        overlap[spot] = jnp.broadcast_to(found, (depth, 128))

    def prepare_down(r):
        count = down_grad.shape[0]
        for i in range(4):
            pl.when(r == i)(lambda: down_quarter(i, count))

    def down_quarter(i, count):
        rows_ = slice(i * count, (i + 1) * count)
        down_partial[rows_] = dot(hidden[:, rows_], grad_out[...], ((0,), (0,))).astype(jnp.bfloat16)

    shard = depth // 8
    size = shard // CHUNKS

    def prepare_rows(z):
        spot = slice(z * 2 * rows, (z + 1) * 2 * rows)
        partial[spot] = dot(grad_mixed[spot], w_project[...], ((1,), (1,))).astype(jnp.bfloat16)

    line_job = line_scatter(at, rows_of(partial, rows), first, line_scratch, True, prepare_rows)
    out_job = line_scatter(
        at, lambda z, c, k: out_part.at[z, pl.ds(k * size, size)], out_grad, out_scratch, False
    )

    def project_work():
        yield from square_scatter(at, row_halves(weight), weight_result, project_scratch, 0, prepare)
        yield from exchange(
            at,
            lambda b, p: weight_result.at[pl.ds(pl.multiple_of(b * shard, shard), shard)],
            lambda b, p: pieces.at[b],
            piece_sems,
        )

    project_job = project_work()
    down_job = square_scatter(
        at, row_halves(down_partial, 1), down_grad, down_scratch, 1, prepare_down
    )

    def vector_work():
        column = jnp.sum(grad_mixed[...].astype(jnp.float32), axis=0, keepdims=True)
        high = column.astype(jnp.bfloat16)
        low = (column - high.astype(jnp.float32)).astype(jnp.bfloat16)
        row = lax.broadcasted_iota(jnp.int32, (16, column.shape[1]), 0)
        both = jnp.where(row == 0, high, jnp.where(row == 1, low, jnp.zeros_like(low)))
        plain = dot(both, w_project[...], ((1,), (1,)))
        times = jnp.concatenate(
            [jnp.transpose(overlap[t * 128 : t * 128 + 128])[0:1] for t in range(width // 128)], axis=1
        )
        parts = jnp.concatenate([times, plain[0:1] + plain[1:2], feed_sums[...]], axis=0)
        for b in range(8):
            for r in range(4):
                lanes = slice((4 * r + b // 2) * 128, (4 * r + b // 2 + 1) * 128)
                sums[b, r, 0:4] = parts[:, lanes]
                sums[b, r, 4:6] = bias_sums[b, r]
                sums[b, r, 6:8] = jnp.zeros((2, 128), jnp.float32)
        spread = exchange(at, lambda b, p: sums.at[b], lambda b, p: arrived.at[b], vector_sems)
        next(spread)
        yield
        drive(spread)
        summed[...] = jnp.sum(arrived[...], axis=0)
        send, recv = row_sems
        copies = [
            remote(summed.at[row], rows_in.at[i], send.at[i], recv.at[i], row, at.b)
            for i, row in enumerate((at.rx, at.ry, at.rd))
        ]
        for copy in copies:
            copy.start()
        yield
        for copy in copies:
            copy.wait()
        vector_out[...] = summed[at.r] + rows_in[0] + rows_in[1] + rows_in[2]

    def tokens_work():
        unit, inverse = norm_stats(x_ref[...].astype(jnp.float32))
        part, _, _ = norm_back(first[...], unit, inverse, gain[...])
        tokens_part[...] = part

    vector_job = vector_work()
    next(out_job)
    next(out_job)
    next(line_job)
    next(out_job)
    loads[0].wait()
    steps(project_job, 3)
    next(out_job)
    next(line_job)
    next(out_job)
    next(line_job)
    next(project_job)
    loads[1].wait()
    loads[2].wait()
    steps(down_job, 3)
    next(out_job)
    next(line_job)
    next(project_job)
    next(vector_job)
    next(line_job)
    next(project_job)
    next(out_job)
    next(vector_job)
    next(line_job)
    next(down_job)
    next(line_job)
    drive(out_job)
    drive(vector_job)
    drive(line_job)
    tokens_work()
    drive(down_job)
    drive(project_job)
    inner = pieces.shape[2] // 3
    for b in range(8):
        for p in range(3):
            lanes = slice(p * width + b * inner, p * width + (b + 1) * inner)
            project_grad[:, lanes] = pieces[b, :, p * inner : (p + 1) * inner]


def finish(
    w_project, normed, grad_mixed, hidden, grad_out, out_part, x, gain, feed_sums, bias_sums
):
    bf, f32 = jnp.bfloat16, jnp.float32
    rows, width = x.shape
    inner = grad_mixed.shape[1]
    depth = width // 4
    shard = depth // 8
    down_owned = (hidden.shape[1] // 4, width)
    flat, spans = pack_sems(
        [
            line_scatter_scratch(rows, width),
            square_scatter_scratch(depth, inner),
            square_scatter_scratch(*down_owned, 1),
            line_scatter_scratch(shard, width),
            exchange_sems(), exchange_sems(), [DMA((3,)), DMA((3,))], [DMA((3,))],
        ]
    )
    outs = [
        ((rows, width), f32, VMEM), ((shard, 8 * inner), bf, VMEM), (down_owned, bf, VMEM),
        ((shard, width), bf, VMEM), ((8, 128), f32, VMEM),
    ]
    scratch = [
        VMEM((width, inner), bf), VMEM((depth, inner), bf), VMEM((8, shard, inner), bf),
        VMEM((rows, width), f32), VMEM((8, 4, 8, 128), f32), VMEM((8, 4, 8, 128), f32),
        VMEM((4, 8, 128), f32), VMEM((3, 8, 128), f32),
        VMEM((hidden.shape[1], width), bf), VMEM((8 * rows, width), bf),
        VMEM((width, 128), f32), VMEM(normed.shape, bf), VMEM(hidden.shape, bf), VMEM(grad_out.shape, bf),
    ]
    return call(
        grouped(finish_kernel, 29, spans), [VMEM] * 7 + [HBM] * 3, outs, scratch + flat, 5,
        w_project, grad_mixed, out_part, x, gain, feed_sums, bias_sums, normed, hidden, grad_out,
    )


def widen_kernel(part, base, *refs):
    count = len(refs) // 2
    sources, total, results = refs[:count], refs[count], refs[count + 1 :]
    total[...] = part[...] + base[...]
    for source, result in zip(sources, results):
        result[...] = source[...].astype(jnp.float32)


def widen(part, base, *arrays):
    kinds = [jax.ShapeDtypeStruct(array.shape, jnp.float32) for array in (part,) + arrays]
    return pl.pallas_call(
        widen_kernel,
        out_shape=kinds,
        in_specs=[pl.BlockSpec(memory_space=VMEM)] * (2 + len(arrays)),
        out_specs=[pl.BlockSpec(memory_space=VMEM)] * len(kinds),
        compiler_params=pltpu.CompilerParams(vmem_limit_bytes=LIMIT),
    )(part, base, *arrays)


def fast_body(
    tokens, segments, cotangent, attend_gain, attend_shift, project_weight, project_bias,
    output_weight, feed_gain, feed_shift, gate_weight, up_weight, down_weight,
):
    bf, f32 = jnp.bfloat16, jnp.float32
    own_rows, width = tokens.shape[1], tokens.shape[2]
    length = own_rows * 8
    head_width = width // HEADS
    local = width // 8
    hidden = down_weight.shape[0]
    shard = attend_gain.shape[0]
    b = lax.axis_index("blk")

    small = jnp.stack([attend_gain, attend_shift, feed_gain, feed_shift])
    zeros = jnp.zeros_like(small)
    small = jnp.where(
        b % 2 == 0, jnp.concatenate([small, zeros], 1), jnp.concatenate([zeros, small], 1)
    )
    rest = jnp.pad(project_bias, (0, 64)).reshape(2, 128)
    vector = jnp.concatenate(
        [small, rest, segments.astype(bf), jnp.zeros((9, 128), bf)], axis=0
    )

    vectors, normed_first, w_project, w_down, w_out, gate_up, start, tables = start_call(
        tokens[0], vector, project_weight, down_weight, output_weight, gate_weight, up_weight
    )

    def whole(row):
        pairs = vectors[:, row].reshape(16, 2, 128).astype(f32)
        return (pairs[:, 0] + pairs[:, 1]).reshape(-1)

    a_gain, f_gain, f_shift = whole(0), whole(2), whole(3)
    bias = vectors[:, 4:6].reshape(32, 256)[:, : 3 * shard].reshape(3, 8, local)
    bias = lax.dynamic_index_in_dim(bias, b, 1, False).reshape(1, -1).astype(f32)

    (
        queries, keys, values, attended, log_total, attended_low, resid_mid, normed_second, gate_up, w_out
    ) = attend_forward(
        normed_first, w_project, bias, start, tables, tokens[0], jnp.stack([f_gain, f_shift]), gate_up, w_out
    )
    grad_out, hidden_low, output, gate_up_grad, grad_mid, feed_sums, grad = feed(
        normed_second, gate_up.reshape(8 * shard, 8 * hidden), cotangent[0], w_down, resid_mid, f_gain[None],
        w_out.reshape(width, width),
    )
    grad_mixed, out_part, gate_grad, up_grad = attend_backward(
        grad, grad_mid, queries, keys, values, attended, log_total, start, tables, attended_low,
        gate_up_grad.reshape(8, shard, 8 * hidden),
    )

    bias_part = jnp.sum(grad_mixed.astype(f32), axis=0).reshape(3, 1, local)
    bias_part = jnp.where(jnp.arange(8)[None, :, None] == b, bias_part, 0.0)
    bias_part = jnp.pad(bias_part.reshape(32, 3 * shard), ((0, 0), (0, 64)))
    bias_part = bias_part.reshape(4, 8, 2, 128).transpose(1, 0, 2, 3)
    tokens_part, project_grad, down_grad, out_grad, vector = finish(
        w_project, normed_first, grad_mixed, hidden_low, grad_out, out_part, tokens[0], a_gain[None],
        feed_sums, bias_part,
    )
    grad_tokens, project_grad, down_grad, out_grad, gate_grad, up_grad = widen(
        tokens_part, grad_mid, project_grad, down_grad, out_grad, gate_grad, up_grad
    )
    gains = jnp.where(b % 2 == 0, vector[:4, :shard], vector[:4, shard:])
    gain_grad = (gains[0] - attend_shift.astype(f32) * gains[1]) / attend_gain.astype(f32)
    return (
        output[None], grad_tokens[None], gain_grad, gains[1], project_grad,
        vector[4:6].reshape(-1)[: 3 * shard], out_grad, gains[2], gains[3], gate_grad, up_grad, down_grad,
    )


def solution(mesh):
    tokens = P("rows", "blk", None)
    vector, matrix = P(BOTH), P(BOTH, None)
    in_specs = (
        tokens, P("rows", "blk"), tokens, vector, vector, matrix, vector, matrix, vector, vector,
        matrix, matrix, matrix,
    )
    out_specs = (
        tokens, tokens, vector, vector, matrix, vector, matrix, vector, vector, matrix, matrix, matrix,
    )
    if (mesh.shape["rows"], mesh.shape["blk"]) == (4, 8):
        body = fast_body
    else:
        body = make_body(mesh.shape["rows"], mesh.shape["blk"])
    return jax.shard_map(body, mesh=mesh, in_specs=in_specs, out_specs=out_specs, check_vma=False)
```

```python
import functools
import math

import jax
import jax.numpy as jnp
from jax import lax
from jax.experimental import pallas as pl
from jax.experimental.pallas import tpu as pltpu
from jax.sharding import PartitionSpec as P

HEADS = 32
ROT = 16
BOTH = ("rows", "blk")

epsilon = 1e-05
rotary_base = 10000.0
masked_value = -1e30


def dot(left, right, contract):
    return lax.dot_general(
        left, right, (contract, ((), ())), preferred_element_type=jnp.float32
    )


def norm_stats(inputs):
    row_mean = jnp.mean(inputs, axis=-1, keepdims=True)
    centered = inputs - row_mean
    variance = jnp.mean(centered * centered, axis=-1, keepdims=True)
    inverse = lax.rsqrt(variance + epsilon)
    return centered * inverse, inverse


def norm_back(incoming, unit, inverse, gain):
    gain_part = jnp.sum(incoming * unit, axis=0)
    shift_part = jnp.sum(incoming, axis=0)
    unit_grad = incoming * gain
    grad = inverse * (
        unit_grad
        - jnp.mean(unit_grad, axis=-1, keepdims=True)
        - unit * jnp.mean(unit_grad * unit, axis=-1, keepdims=True)
    )
    return grad, gain_part, shift_part


def rotate(columns, cosine, sine, head_width):
    half = cosine.shape[1]
    heads = columns.reshape(columns.shape[0], -1, head_width)
    cosine, sine = cosine[:, None, :], sine[:, None, :]
    first, second, rest = heads[..., :half], heads[..., half : 2 * half], heads[..., 2 * half :]
    return jnp.concatenate(
        [first * cosine - second * sine, second * cosine + first * sine, rest], axis=-1
    ).reshape(columns.shape)


def gather_blk(rows):
    return lax.all_gather(rows, "blk", axis=0, tiled=True)


def scatter_blk(partial):
    return lax.psum_scatter(
        partial.astype(jnp.bfloat16), "blk", scatter_dimension=0, tiled=True
    ).astype(jnp.float32)


def gather_rows(shard):
    return lax.all_gather(shard, "rows", axis=0, tiled=True)


def scatter_rows(partial):
    return lax.psum_scatter(
        partial.astype(jnp.bfloat16), "rows", scatter_dimension=0, tiled=True
    )


def exchange_blk(pieces):
    return lax.all_to_all(pieces, "blk", split_axis=0, concat_axis=0, tiled=True)


def make_body(group, ranks):
    def columns_of(shard, parts, inner):
        depth = shard.shape[0]
        pieces = shard.reshape(depth, parts, ranks, inner).transpose(2, 0, 1, 3)
        pieces = exchange_blk(pieces.reshape(ranks, depth, parts * inner))
        return gather_rows(pieces.reshape(ranks * depth, parts * inner))

    def columns_back(grad, parts, inner):
        owned = scatter_rows(grad)
        depth = owned.shape[0] // ranks
        pieces = exchange_blk(owned.reshape(ranks, depth, parts * inner))
        pieces = pieces.reshape(ranks, depth, parts, inner).transpose(1, 2, 0, 3)
        return pieces.reshape(depth, parts * ranks * inner).astype(jnp.float32)

    def body(
        tokens,
        segments,
        cotangent,
        attend_gain,
        attend_shift,
        project_weight,
        project_bias,
        output_weight,
        feed_gain,
        feed_shift,
        gate_weight,
        up_weight,
        down_weight,
    ):
        own_rows, width = tokens.shape[1], tokens.shape[2]
        length = own_rows * ranks
        head_width = width // HEADS
        local_heads = HEADS // ranks
        local_width = local_heads * head_width
        score_scale = 1.0 / math.sqrt(head_width)
        hidden_shard = down_weight.shape[0]
        shard = attend_gain.shape[0]
        me = lax.axis_index("blk")

        packed = jnp.concatenate(
            [
                attend_gain,
                attend_shift,
                feed_gain,
                feed_shift,
                project_bias,
                segments[0].astype(jnp.bfloat16),
            ]
        )
        packed = lax.all_gather(packed, BOTH, axis=0, tiled=False)
        a_gain = packed[:, :shard].reshape(-1).astype(jnp.float32)
        a_shift = packed[:, shard : 2 * shard].reshape(-1).astype(jnp.float32)
        f_gain = packed[:, 2 * shard : 3 * shard].reshape(-1).astype(jnp.float32)
        f_shift = packed[:, 3 * shard : 4 * shard].reshape(-1).astype(jnp.float32)
        bias = packed[:, 4 * shard : 7 * shard].reshape(3, ranks, local_width)
        bias = lax.dynamic_index_in_dim(bias, me, 1, False).reshape(-1).astype(jnp.float32)
        doc = packed[:, 7 * shard :].reshape(group, ranks * own_rows)
        doc = lax.dynamic_index_in_dim(doc, lax.axis_index("rows"), 0, False)

        w_project = columns_of(project_weight, 3, local_width)
        w_gate = columns_of(gate_weight, group, hidden_shard)
        w_up = columns_of(up_weight, group, hidden_shard)
        w_down = gather_rows(down_weight)
        w_out = lax.all_gather(output_weight, BOTH, axis=0, tiled=True)

        doc = doc.astype(jnp.int32)
        index = jnp.arange(length, dtype=jnp.int32)
        places = index - jnp.sum((doc[None, :] < doc[:, None]).astype(jnp.int32), axis=1)
        half = ROT // 2
        frequency = jnp.power(
            rotary_base, -jnp.arange(half, dtype=jnp.int32).astype(jnp.float32) / half
        )
        angles = places.astype(jnp.float32)[:, None] * frequency
        cosine, sine = jnp.cos(angles), jnp.sin(angles)
        mask = ((index[None, :] <= index[:, None]) & (doc[None, :] == doc[:, None]))[None]

        inputs = tokens[0].astype(jnp.float32)
        unit_first, inverse_first = norm_stats(inputs)
        normed_first = gather_blk((unit_first * a_gain + a_shift).astype(jnp.bfloat16))
        grad_out = gather_blk(cotangent[0])
        mixed = dot(normed_first, w_project, ((1,), (0,))) + bias
        queries = rotate(mixed[:, :local_width], cosine, sine, head_width).astype(jnp.bfloat16)
        keys = rotate(mixed[:, local_width : 2 * local_width], cosine, sine, head_width)
        keys = keys.astype(jnp.bfloat16)
        values = mixed[:, 2 * local_width :].astype(jnp.bfloat16)
        q_heads = queries.reshape(length, local_heads, head_width)
        k_heads = keys.reshape(length, local_heads, head_width)
        v_heads = values.reshape(length, local_heads, head_width)
        scores = jnp.einsum("qhd,khd->hqk", q_heads, k_heads, preferred_element_type=jnp.float32)
        scores = jnp.where(mask, scores * score_scale, masked_value)
        top = jnp.max(scores, axis=2, keepdims=True)
        weights = jnp.where(mask, jnp.exp(scores - top), 0.0)
        total = jnp.sum(weights, axis=2, keepdims=True)
        attended = jnp.einsum(
            "hqk,khd->qhd",
            weights.astype(jnp.bfloat16),
            v_heads,
            preferred_element_type=jnp.float32,
        ) / jnp.transpose(total[:, :, 0])[:, :, None]
        log_total = top + jnp.log(total)
        attended_flat = attended.reshape(length, local_width)
        attended_low = exchange_blk(
            attended_flat.astype(jnp.bfloat16).reshape(ranks, own_rows, local_width)
        )
        attended_low = attended_low.transpose(1, 0, 2).reshape(own_rows, width)
        resid_mid = inputs + dot(attended_low, w_out, ((1,), (0,)))

        unit_second, inverse_second = norm_stats(resid_mid)
        normed_second = gather_blk((unit_second * f_gain + f_shift).astype(jnp.bfloat16))
        gate_value = dot(normed_second, w_gate, ((1,), (0,)))
        up_value = dot(normed_second, w_up, ((1,), (0,)))
        gate_sigmoid = jax.nn.sigmoid(gate_value)
        silu = gate_value * gate_sigmoid
        hidden = (silu * up_value).astype(jnp.bfloat16)
        output = (resid_mid + scatter_blk(dot(hidden, w_down, ((1,), (0,))))).astype(jnp.bfloat16)

        grad_hidden = dot(grad_out, w_down, ((1,), (1,)))
        grad_gate = (
            grad_hidden * up_value * gate_sigmoid * (1.0 + gate_value * (1.0 - gate_sigmoid))
        ).astype(jnp.bfloat16)
        grad_up = (grad_hidden * silu).astype(jnp.bfloat16)
        grad_second = scatter_blk(
            dot(grad_gate, w_gate, ((1,), (1,))) + dot(grad_up, w_up, ((1,), (1,)))
        )
        down_grad = scatter_rows(dot(hidden, grad_out, ((0,), (0,)))).astype(jnp.float32)
        gate_grad = columns_back(dot(normed_second, grad_gate, ((0,), (0,))), group, hidden_shard)
        up_grad = columns_back(dot(normed_second, grad_up, ((0,), (0,))), group, hidden_shard)
        mid_part, f_gain_part, f_shift_part = norm_back(
            grad_second, unit_second, inverse_second, f_gain
        )
        grad_mid = cotangent[0].astype(jnp.float32) + mid_part
        grad_mid_low = grad_mid.astype(jnp.bfloat16)
        grad_attended = dot(grad_mid_low, w_out, ((1,), (1,))).astype(jnp.bfloat16)
        grad_attended = exchange_blk(
            grad_attended.reshape(own_rows, ranks, local_width).transpose(1, 0, 2)
        ).reshape(length, local_width)
        out_grad = lax.psum_scatter(
            dot(attended_low, grad_mid_low, ((0,), (0,))).astype(jnp.bfloat16),
            BOTH,
            scatter_dimension=0,
            tiled=True,
        ).astype(jnp.float32)

        g_heads = grad_attended.reshape(length, local_heads, head_width)
        delta = jnp.transpose(jnp.sum(g_heads.astype(jnp.float32) * attended, axis=2))
        probs = jnp.where(mask, jnp.exp(scores - log_total), 0.0)
        values_grad = jnp.einsum(
            "hqk,qhd->khd", probs.astype(jnp.bfloat16), g_heads, preferred_element_type=jnp.float32
        )
        grad_probs = jnp.einsum("qhd,khd->hqk", g_heads, v_heads, preferred_element_type=jnp.float32)
        grad_scores = (probs * (grad_probs - delta[:, :, None]) * score_scale).astype(jnp.bfloat16)
        grad_queries = jnp.einsum(
            "hqk,khd->qhd", grad_scores, k_heads, preferred_element_type=jnp.float32
        )
        keys_grad = jnp.einsum(
            "hqk,qhd->khd", grad_scores, q_heads, preferred_element_type=jnp.float32
        )
        grad_mixed = jnp.concatenate(
            [
                rotate(grad_queries.reshape(length, local_width), cosine, -sine, head_width),
                rotate(keys_grad.reshape(length, local_width), cosine, -sine, head_width),
                values_grad.reshape(length, local_width),
            ],
            axis=1,
        ).astype(jnp.bfloat16)
        grad_first = scatter_blk(dot(grad_mixed, w_project, ((1,), (1,))))
        project_grad = columns_back(
            dot(normed_first, grad_mixed, ((0,), (0,))), 3, local_width
        )
        bias_part = jnp.sum(grad_mixed.astype(jnp.float32), axis=0).reshape(3, 1, local_width)
        bias_part = jnp.where(jnp.arange(ranks)[None, :, None] == me, bias_part, 0.0)
        input_part, a_gain_part, a_shift_part = norm_back(
            grad_first, unit_first, inverse_first, a_gain
        )
        grad_tokens = grad_mid + input_part
        vectors = jnp.concatenate(
            [
                a_gain_part.reshape(-1, shard),
                a_shift_part.reshape(-1, shard),
                f_gain_part.reshape(-1, shard),
                f_shift_part.reshape(-1, shard),
                bias_part.reshape(-1, 3 * shard),
            ],
            axis=1,
        )
        vectors = lax.psum_scatter(vectors, BOTH, scatter_dimension=0, tiled=True)[0]
        return (
            output[None],
            grad_tokens[None],
            vectors[:shard],
            vectors[shard : 2 * shard],
            project_grad,
            vectors[4 * shard :],
            out_grad,
            vectors[2 * shard : 3 * shard],
            vectors[3 * shard : 4 * shard],
            gate_grad,
            up_grad,
            down_grad,
        )

    return body


MESH_ID = pl.DeviceIdType.MESH
DMA = pltpu.SemaphoreType.DMA
HBM = pl.ANY
VMEM = pltpu.VMEM
LIMIT = 60 * 1024 * 1024


class Place:
    def __init__(self):
        self.r = lax.axis_index("rows")
        self.b = lax.axis_index("blk")
        self.z = self.b // 2
        self.c = lax.rem(self.b, 2)
        self.sibling = 2 * self.z + 1 - self.c
        self.rx = self.r + 1 - 2 * lax.rem(self.r, 2)
        self.ry = lax.rem(self.r + 2, 4)
        self.rd = 3 - self.r

    def barrier(self, diagonal=False):
        sem = pltpu.get_barrier_semaphore()
        peers = [(self.r, lax.rem(self.b + k, 8)) for k in range(1, 8)]
        peers += [(self.rx, self.b), (self.ry, self.b)]
        if diagonal:
            peers.append((self.rd, self.b))
        for peer in peers:
            pl.semaphore_signal(sem, inc=1, device_id=peer, device_id_type=MESH_ID)
        pl.semaphore_wait(sem, len(peers))


def remote(src, dst, send, recv, r, b):
    return pltpu.make_async_remote_copy(
        src_ref=src, dst_ref=dst, send_sem=send, recv_sem=recv, device_id=(r, b), device_id_type=MESH_ID
    )


def drive(*jobs):
    active = list(jobs)
    while active:
        for job in list(active):
            try:
                next(job)
            except StopIteration:
                active.remove(job)


def later(job, count):
    for _ in range(count):
        yield
    yield from job


def steps(job, count):
    for _ in range(count):
        next(job, None)


CHUNKS = 2


def line_gather_sems():
    return [DMA((4, CHUNKS))] * 4 + [DMA((7, CHUNKS))] * 2 + [DMA((CHUNKS,))]


def line_gather(at, own, spot, sems, paired=True):
    up_send, down_send, up_recv, down_recv, pair_send, pair_recv, local_sem = sems

    def up(d, k, src):
        return remote(
            src, spot(at.z - d, at.c, k), up_send.at[d, k], up_recv.at[d, k], at.r, at.b + 2
        )

    def down(d, k, src):
        return remote(
            src, spot(at.z + d, at.c, k), down_send.at[d, k], down_recv.at[d, k], at.r, at.b - 2
        )

    def up_in(d, k):
        piece = spot(at.z - d - 1, at.c, k)
        return remote(piece, piece, up_send.at[d, k], up_recv.at[d, k], at.r, at.b + 2)

    def down_in(d, k):
        piece = spot(at.z + d + 1, at.c, k)
        return remote(piece, piece, down_send.at[d, k], down_recv.at[d, k], at.r, at.b - 2)

    def pair(i, k, z, src):
        return remote(
            src, spot(z, at.c, k), pair_send.at[i, k], pair_recv.at[i, k], at.r, at.sibling
        )

    def pair_in(i, k, z):
        piece = spot(z, 1 - at.c, k)
        return remote(piece, piece, pair_send.at[i, k], pair_recv.at[i, k], at.r, at.sibling)

    locals_ = [
        pltpu.make_async_copy(own(k), spot(at.z, at.c, k), local_sem.at[k]) for k in range(CHUNKS)
    ]
    for k in range(CHUNKS):
        locals_[k].start()
        pl.when(at.z < 3)(lambda: up(0, k, own(k)).start())
        pl.when(at.z > 0)(lambda: down(0, k, own(k)).start())
        if paired:
            pair(0, k, at.z, own(k)).start()
    yield
    for d in range(3):
        for k in range(CHUNKS):

            @pl.when(at.z - 1 - d >= 0)
            def _():
                z = at.z - 1 - d
                up_in(d, k).wait_recv()
                if d < 2:
                    pl.when(at.z < 3)(lambda: up(d + 1, k, spot(z, at.c, k)).start())
                if paired:
                    pair(1 + d, k, z, spot(z, at.c, k)).start()

            @pl.when(at.z + 1 + d <= 3)
            def _():
                z = at.z + 1 + d
                down_in(d, k).wait_recv()
                if d < 2:
                    pl.when(at.z > 0)(lambda: down(d + 1, k, spot(z, at.c, k)).start())
                if paired:
                    pair(4 + d, k, z, spot(z, at.c, k)).start()

            if d == 0:
                locals_[k].wait()
                if paired:
                    pair_in(0, k, at.z).wait_recv()
            if k == CHUNKS - 1 and paired:
                for part in range(CHUNKS):
                    pl.when(at.z - 1 - d >= 0)(
                        lambda: pair_in(1 + d, part, at.z - 1 - d).wait_recv()
                    )
                    pl.when(at.z + 1 + d <= 3)(
                        lambda: pair_in(4 + d, part, at.z + 1 + d).wait_recv()
                    )
            yield
    for k in range(CHUNKS):
        if paired:
            pair(0, k, at.z, own(k)).wait_send()
        pl.when(at.z < 3)(lambda: up(0, k, own(k)).wait_send())
        pl.when(at.z > 0)(lambda: down(0, k, own(k)).wait_send())
        for d in range(3):

            @pl.when(at.z - 1 - d >= 0)
            def _():
                z = at.z - 1 - d
                if paired:
                    pair(1 + d, k, z, spot(z, at.c, k)).wait_send()
                if d < 2:
                    pl.when(at.z < 3)(lambda: up(d + 1, k, spot(z, at.c, k)).wait_send())

            @pl.when(at.z + 1 + d <= 3)
            def _():
                z = at.z + 1 + d
                if paired:
                    pair(4 + d, k, z, spot(z, at.c, k)).wait_send()
                if d < 2:
                    pl.when(at.z > 0)(lambda: down(d + 1, k, spot(z, at.c, k)).wait_send())


def rows_of(ref, count):
    size = count // CHUNKS
    return lambda z, c, k: ref.at[pl.ds(pl.multiple_of((2 * z + c) * count + k * size, size), size)]


def cuts_of(ref):
    size = ref.shape[0] // CHUNKS
    return lambda k: ref.at[pl.ds(k * size, size)]


def line_scatter_scratch(count, width):
    block = VMEM((4, count, width), jnp.bfloat16)
    arrive = VMEM((3, count, width), jnp.bfloat16)
    return [block, arrive, arrive] + [DMA((4, CHUNKS))] * 2 + [DMA((3, CHUNKS))] * 4


def line_scatter(at, block, result, scratch, paired=True, prepare=None):
    held, from_below, from_above, pair_send, pair_recv, up_send, up_recv, down_send, down_recv = scratch
    count = held.shape[1]
    size = count // CHUNKS

    def cut(k):
        return pl.ds(k * size, size)

    def pair(z, k):
        return remote(
            block(z, 1 - at.c, k),
            held.at[z, cut(k)],
            pair_send.at[z, k],
            pair_recv.at[z, k],
            at.r,
            at.sibling,
        )

    def up(z, k):
        return remote(
            held.at[z, cut(k)],
            from_below.at[z - 1, cut(k)],
            up_send.at[z - 1, k],
            up_recv.at[z - 1, k],
            at.r,
            at.b + 2,
        )

    def down(z, k):
        return remote(
            held.at[z, cut(k)],
            from_above.at[z, cut(k)],
            down_send.at[z, k],
            down_recv.at[z, k],
            at.r,
            at.b - 2,
        )

    def wide(ref):
        return ref[...].astype(jnp.float32)

    def own(z, k):
        mine = wide(block(z, at.c, k))
        return mine + wide(held.at[z, cut(k)]) if paired else mine

    if paired:
        for z in (3, 0, 2, 1):
            if prepare:
                prepare(z)
            for k in range(CHUNKS):
                pair(z, k).start()
    yield
    for step in range(3):
        for k in range(CHUNKS):
            far, near = 3 - step, step

            @pl.when(at.z < far)
            def _():
                if paired:
                    pair(far, k).wait_recv()

                @pl.when(at.z == 0)
                def _():
                    held[far, cut(k)] = own(far, k).astype(jnp.bfloat16)

                @pl.when(at.z > 0)
                def _():
                    up(far, k).wait_recv()
                    held[far, cut(k)] = (
                        own(far, k) + wide(from_below.at[far - 1, cut(k)])
                    ).astype(jnp.bfloat16)

                up(far, k).start()

            @pl.when(at.z > near)
            def _():
                if paired:
                    pair(near, k).wait_recv()

                @pl.when(at.z == 3)
                def _():
                    held[near, cut(k)] = own(near, k).astype(jnp.bfloat16)

                @pl.when(at.z < 3)
                def _():
                    down(near, k).wait_recv()
                    held[near, cut(k)] = (
                        own(near, k) + wide(from_above.at[near, cut(k)])
                    ).astype(jnp.bfloat16)

                down(near, k).start()

            yield
    for z in range(4):
        for k in range(CHUNKS):

            @pl.when(at.z == z)
            def _():
                if paired:
                    pair(z, k).wait_recv()
                total = own(z, k)
                if z > 0:
                    up(z, k).wait_recv()
                    total += wide(from_below.at[z - 1, cut(k)])
                if z < 3:
                    down(z, k).wait_recv()
                    total += wide(from_above.at[z, cut(k)])
                result[cut(k)] = total.astype(result.dtype)

    for z in range(4):
        for k in range(CHUNKS):
            if paired:
                pair(z, k).wait_send()
            if z > 0:
                pl.when(at.z < z)(lambda: up(z, k).wait_send())
            if z < 3:
                pl.when(at.z > z)(lambda: down(z, k).wait_send())


def half_of(ref, axis, which):
    size = ref.shape[axis] // 2
    return ref.at[pl.ds(which * size, size)] if axis == 0 else ref.at[:, pl.ds(which * size, size)]


def row_halves(ref, axis=0):
    count = ref.shape[0] // 4
    return lambda r, which: half_of(
        ref.at[pl.ds(pl.multiple_of(r * count, count), count)], axis, which
    )


def square_gather_sems():
    return [DMA((6,)), DMA((6,)), DMA((2,))]


def square_gather(at, own, spot, sems, arrived=None):
    send, recv, local_sem = sems

    def copy(i, src, r_of, which, to):
        return remote(src, spot(r_of, which), send.at[i], recv.at[i], to, at.b)

    outs = [
        copy(0, own(0), at.r, 0, at.rx),
        copy(1, own(1), at.r, 1, at.ry),
        copy(2, own(1), at.r, 1, at.rx),
        copy(3, own(0), at.r, 0, at.ry),
    ]
    ins = [
        copy(0, spot(at.rx, 0), at.rx, 0, at.rx),
        copy(1, spot(at.ry, 1), at.ry, 1, at.ry),
        copy(2, spot(at.rx, 1), at.rx, 1, at.rx),
        copy(3, spot(at.ry, 0), at.ry, 0, at.ry),
        copy(4, spot(at.rd, 0), at.rd, 0, at.ry),
        copy(5, spot(at.rd, 1), at.rd, 1, at.rx),
    ]
    locals_ = [pltpu.make_async_copy(own(h), spot(at.r, h), local_sem.at[h]) for h in range(2)]
    for copy_ in outs + locals_:
        copy_.start()
    yield
    ins[0].wait_recv()
    outs.append(copy(4, spot(at.rx, 0), at.rx, 0, at.ry))
    outs[4].start()
    yield
    ins[1].wait_recv()
    outs.append(copy(5, spot(at.ry, 1), at.ry, 1, at.rx))
    outs[5].start()
    yield
    for copy_ in locals_:
        copy_.wait()
    for pair, r in (((2,), at.rx), ((3,), at.ry), ((4, 5), at.rd)):
        for i in pair:
            ins[i].wait_recv()
        if arrived:
            arrived(r)
    for out in outs:
        out.wait_send()


def square_scatter_scratch(count, width, axis=0):
    half = (count // 2, width) if axis == 0 else (count, width // 2)
    piece = VMEM((count, width), jnp.bfloat16)
    part = VMEM(half, jnp.bfloat16)
    return [piece, piece, part, part, part, part, DMA((6,)), DMA((6,))]


def square_scatter(at, part, result, scratch, axis=0, prepare=None):
    from_x, from_y, far_x, far_y, out_x, out_y, send, recv = scratch
    prepare = prepare or (lambda r: None)

    def wide(ref):
        return ref[...].astype(jnp.float32)

    copies = [
        remote(part(at.rd, 0), far_x, send.at[0], recv.at[0], at.rx, at.b),
        remote(part(at.rd, 1), far_y, send.at[1], recv.at[1], at.ry, at.b),
        remote(part(at.rx, 0), half_of(from_x, axis, 0), send.at[2], recv.at[2], at.rx, at.b),
        remote(part(at.ry, 1), half_of(from_y, axis, 1), send.at[3], recv.at[3], at.ry, at.b),
        remote(out_y, half_of(from_y, axis, 0), send.at[4], recv.at[4], at.ry, at.b),
        remote(out_x, half_of(from_x, axis, 1), send.at[5], recv.at[5], at.rx, at.b),
    ]
    prepare(at.rd)
    copies[0].start()
    copies[1].start()
    yield
    prepare(at.rx)
    copies[2].start()
    yield
    prepare(at.ry)
    copies[3].start()
    yield
    copies[0].wait_recv()
    out_y[...] = (wide(part(at.ry, 0)) + wide(far_x)).astype(jnp.bfloat16)
    copies[4].start()
    copies[1].wait_recv()
    out_x[...] = (wide(part(at.rx, 1)) + wide(far_y)).astype(jnp.bfloat16)
    copies[5].start()
    yield
    prepare(at.r)
    yield
    for i in (2, 3, 4, 5):
        copies[i].wait_recv()
    for which in range(2):
        total = (
            wide(part(at.r, which)) + wide(half_of(from_x, axis, which)) + wide(half_of(from_y, axis, which))
        )
        spot = half_of(result, axis, which)
        spot[...] = total.astype(result.dtype)
    for copy in copies:
        copy.wait_send()


def exchange_sems(parts=1):
    return [DMA((7, parts)), DMA((7, parts)), DMA((parts,))]


def exchange(at, take, put, sems, parts=1):
    send, recv, local_sem = sems
    locals_ = [
        pltpu.make_async_copy(take(at.b, p), put(at.b, p), local_sem.at[p]) for p in range(parts)
    ]
    outs, ins = [], []
    for k in (4, 3, 5, 2, 6, 1, 7):
        to, source = lax.rem(at.b + k, 8), lax.rem(at.b + 8 - k, 8)
        for p in range(parts):
            pair = (send.at[k - 1, p], recv.at[k - 1, p])
            outs.append(remote(take(to, p), put(at.b, p), *pair, at.r, to))
            ins.append(remote(put(source, p), put(source, p), *pair, at.r, source))
    for copy in locals_ + outs:
        copy.start()
    yield
    for copy in ins:
        copy.wait_recv()
    for copy in locals_:
        copy.wait()
    for copy in outs:
        copy.wait_send()


def call(kernel, ins, outs, scratch, number, *args):
    return pl.pallas_call(
        kernel,
        out_shape=[jax.ShapeDtypeStruct(shape, kind) for shape, kind, _ in outs],
        in_specs=[pl.BlockSpec(memory_space=space) for space in ins],
        out_specs=[pl.BlockSpec(memory_space=space) for _, _, space in outs],
        scratch_shapes=scratch,
        compiler_params=pltpu.CompilerParams(
            collective_id=number, has_side_effects=True, vmem_limit_bytes=LIMIT
        ),
    )(*args)


def vector_gather(at, own, full, sems):
    send, recv, local_sem = sems
    mine = 8 * at.r + at.b
    outs, ins = [], []
    for k in range(1, 8):
        to, source = lax.rem(at.b + k, 8), lax.rem(at.b + 8 - k, 8)
        outs.append(remote(own, full.at[mine], send.at[k - 1], recv.at[k - 1], at.r, to))
        piece = full.at[8 * at.r + source]
        ins.append(remote(piece, piece, send.at[k - 1], recv.at[k - 1], at.r, source))
    local = pltpu.make_async_copy(own, full.at[mine], local_sem)
    local.start()
    for out in outs:
        out.start()
    yield
    for copy in ins:
        copy.wait_recv()
    local.wait()
    group = full.at[pl.ds(8 * at.r, 8)]
    later = []
    for i, row in enumerate((at.rx, at.ry, at.rd)):
        outs.append(remote(group, group, send.at[7 + i], recv.at[7 + i], row, at.b))
        outs[-1].start()
        theirs = full.at[pl.ds(8 * row, 8)]
        later.append(remote(theirs, theirs, send.at[7 + i], recv.at[7 + i], row, at.b))
    yield
    for copy in later:
        copy.wait_recv()
    for out in outs:
        out.wait_send()


def make_tables(at, vectors, start, cosine, minus, plus):
    docs = jnp.concatenate(
        [vectors[8 * at.r + j, 6:7].astype(jnp.float32) for j in range(8)], axis=0
    )
    begins = jnp.zeros_like(docs)
    for doc in range(1, 5):
        before = jnp.sum((docs < doc).astype(jnp.float32), axis=(0, 1), keepdims=True)
        begins = jnp.where(docs == doc, before, begins)
    index = lax.broadcasted_iota(jnp.int32, docs.shape, 0) * 128
    index = (index + lax.broadcasted_iota(jnp.int32, docs.shape, 1)).astype(jnp.float32)
    places = index - begins
    half = ROT // 2
    row = lax.broadcasted_iota(jnp.int32, (half, 128), 0)
    frequency = jnp.zeros((half, 128), jnp.float32)
    for j in range(half):
        frequency = jnp.where(row == j, rotary_base ** (-j / half), frequency)
    eight = jnp.zeros((half, 128), jnp.float32)
    gap = jnp.zeros((48, 128), jnp.float32)
    for j in range(8):
        rows = slice(j * 128, j * 128 + 128)
        angles = frequency * places[j : j + 1]
        cos, sin = jnp.cos(angles), jnp.sin(angles)

        def table(first, second, rest):
            return jnp.transpose(jnp.concatenate([first, second, rest] * 2, axis=0))

        cosine[rows] = table(cos, cos, gap + 1.0)
        minus[rows] = table(-sin, eight, gap)
        plus[rows] = table(eight, sin, gap)
        start[rows] = jnp.transpose(jnp.broadcast_to(begins[j : j + 1], (128, 128))).astype(jnp.int32)
        yield


def start_kernel(
    x_ref, vector_ref, project_ref, down_ref, out_ref, gate_ref, up_ref,
    vectors, normed, pieces, w_project, w_down, w_out, gate_up, start, cosine, minus, plus,
    unit, own, vector_sems, exchange_sem, square_sem, down_sem, line_sems, out_sems,
):
    at = Place()
    at.barrier(diagonal=True)
    width = x_ref.shape[1]
    vector_job = vector_gather(at, vector_ref, vectors, vector_sems)
    next(vector_job)
    inner = w_project.shape[1] // 3
    depth = project_ref.shape[0]
    project_job = exchange(
        at,
        lambda b, p: project_ref.at[:, pl.ds(pl.multiple_of(p * width + b * inner, inner), inner)],
        lambda b, p: pieces.at[
            pl.ds(pl.multiple_of(b * depth, depth), depth), pl.ds(p * inner, inner)
        ],
        exchange_sem,
        3,
    )
    next(project_job)
    size = depth // CHUNKS
    out_job = line_gather(
        at, cuts_of(out_ref), lambda z, c, k: w_out.at[z, pl.ds(k * size, size)], out_sems, False
    )
    next(out_job)
    down_job = square_gather(
        at, lambda half: half_of(down_ref, 1, half), row_halves(w_down, 1), down_sem
    )
    next(down_job)
    x = x_ref[...].astype(jnp.float32)
    centered = x - jnp.mean(x, axis=1, keepdims=True)
    unit[...] = centered * lax.rsqrt(jnp.mean(centered * centered, axis=1, keepdims=True) + epsilon)
    drive(vector_job)
    for tile in range(width // 128):
        lanes = slice(tile * 128, tile * 128 + 128)
        both = vectors[2 * tile].astype(jnp.float32) + vectors[2 * tile + 1].astype(jnp.float32)
        own[:, lanes] = (unit[:, lanes] * both[0:1] + both[1:2]).astype(jnp.bfloat16)
    line_job = line_gather(at, cuts_of(own), rows_of(normed, own.shape[0]), line_sems)
    next(line_job)
    hidden = down_ref.shape[0]

    def reorder():
        for b in range(8):
            for r in range(4):
                source = slice((8 * r + b) * hidden, (8 * r + b + 1) * hidden)
                gate_up[b, :, r * hidden : (r + 1) * hidden] = gate_ref[:, source]
                gate_up[b, :, (4 + r) * hidden : (5 + r) * hidden] = up_ref[:, source]
            yield

    def project_work():
        yield from project_job
        yield from square_gather(
            at, lambda half: half_of(pieces, 0, half), row_halves(w_project), square_sem
        )

    table_job, order_job = make_tables(at, vectors, start, cosine, minus, plus), reorder()
    steps(table_job, 4)
    steps(order_job, 4)
    drive(out_job, line_job, project_work(), table_job, order_job, down_job)


def pack_sems(groups):
    flat, spans = [], []
    for group in groups:
        spans.append((len(flat), len(flat) + len(group)))
        flat += group
    return flat, spans


def grouped(kernel, lead, spans):
    def run(*refs):
        rest = refs[lead:]
        return kernel(*refs[:lead], *[rest[a:b] for a, b in spans])

    return run


def start_call(x, vector, project, down, out_weight, gate, up):
    rows, width = x.shape
    depth = project.shape[0]
    inner = project.shape[1] // 8
    bf, f32 = jnp.bfloat16, jnp.float32
    groups = [
        [DMA((10,)), DMA((10,)), DMA], exchange_sems(3), square_gather_sems(), square_gather_sems(),
        line_gather_sems(), line_gather_sems(),
    ]
    flat, spans = pack_sems(groups)
    outs = [
        ((32, 16, 128), bf, VMEM), ((8 * rows, width), bf, HBM), ((8 * depth, inner), bf, HBM),
        ((32 * depth, inner), bf, HBM), ((4 * down.shape[0], width), bf, HBM),
        ((4, depth, width), bf, HBM), ((8, depth, 8 * down.shape[0]), bf, VMEM),
        ((8 * rows, 128), jnp.int32, VMEM),
    ] + [((8 * rows, 128), f32, VMEM)] * 3
    scratch = [VMEM((rows, width), f32), VMEM((rows, width), bf)] + flat
    vectors, normed, _, w_project, w_down, w_out, gate_up, start, *tables = call(
        grouped(start_kernel, 20, spans), [VMEM, VMEM, HBM, HBM, HBM, VMEM, VMEM], outs, scratch, 0,
        x, vector, project, down, out_weight, gate, up,
    )
    return vectors, normed, w_project, w_down, w_out, gate_up, start, tables


def turned(columns, cosine, minus, plus):
    half = ROT // 2
    return (
        columns * cosine
        + pltpu.roll(columns, 128 - half, 1) * minus
        + pltpu.roll(columns, half, 1) * plus
    )


def score_mask(first_row, rows, keys, start):
    row = lax.broadcasted_iota(jnp.int32, (rows, keys), 0) + first_row
    col = lax.broadcasted_iota(jnp.int32, (rows, keys), 1)
    return (col <= row) & (col >= start)


QROWS = 256


def attend_forward_kernel(
    x_all, w_all, bias, start, cosine, minus, plus, tokens, feed_set, gate_up, out_ref,
    queries, keys, values, attended, log_total, mixed_heads, resid_mid, normed, gate_up_all, w_out,
    low, x_ref, w_ref, own_sems, gate_up_sems, square_sems, pair_sems, load_sems,
):
    at = Place()
    loads = [
        pltpu.make_async_copy(*pair_, load_sems[0].at[i])
        for i, pair_ in enumerate(((x_all, x_ref), (w_all, w_ref)))
    ]
    for load in loads:
        load.start()
    at.barrier()
    pair_send, pair_recv = pair_sems

    def pair(i, r, src):
        return remote(src, w_out.at[r, :, at.c], pair_send.at[i], pair_recv.at[i], at.r, at.sibling)

    pairs = [pair(0, at.r, out_ref)] + [
        pair(i, r, w_out.at[r, :, at.c]) for i, r in ((1, at.rx), (2, at.ry), (3, at.rd))
    ]
    pairs[0].start()
    handed = iter(pairs[1:])
    out_job = square_gather(
        at,
        lambda half: half_of(out_ref, 0, half),
        lambda r, half: w_out.at[r, pl.ds(2 * half, 2), at.c],
        square_sems,
        lambda r: next(handed).start(),
    )
    next(out_job)
    length, local = queries.shape
    depth = gate_up.shape[1]
    gate_up_job = exchange(
        at, lambda b, p: gate_up.at[b], lambda b, p: gate_up_all.at[b], gate_up_sems
    )
    next(gate_up_job)
    scale = 1.0 / math.sqrt(local * 8 // HEADS)
    blocks = length // QROWS
    for load in loads:
        load.wait()

    @pl.loop(0, blocks)
    def _(i):
        rows = pl.ds(pl.multiple_of(i * QROWS, QROWS), QROWS)
        mixed = dot(x_ref[rows], w_ref[...], ((1,), (0,))) + bias[...]
        tables = (cosine[rows], minus[rows], plus[rows])
        for pair in range(local // 128):
            lanes = slice(pair * 128, pair * 128 + 128)
            queries[rows, lanes] = turned(mixed[:, lanes], *tables).astype(jnp.bfloat16)
            shifted = slice(local + pair * 128, local + pair * 128 + 128)
            keys[rows, lanes] = turned(mixed[:, shifted], *tables).astype(jnp.bfloat16)
        values[rows] = mixed[:, 2 * local :].astype(jnp.bfloat16)

    send, recv, local_sem = own_sems

    def deliver(to):
        rows = low.at[pl.ds(to * 128, 128)]
        spot = mixed_heads.at[:, pl.ds(pl.multiple_of(at.b * local, local), local)]
        return remote(rows, spot, send.at[to], recv.at[at.b], at.r, to)

    for i in range(blocks):
        rows = slice(i * QROWS, (i + 1) * QROWS)
        count = (i + 1) * QROWS

        @pl.loop(0, local // 128)
        def _(pair):
            lanes = pl.ds(pl.multiple_of(pair * 128, 128), 128)
            lane = lax.broadcasted_iota(jnp.int32, (QROWS, 128), 1)
            q, k, v = queries[rows, lanes], keys[:count, lanes], values[:count, lanes]
            allowed = score_mask(i * QROWS, QROWS, count, start[rows, 0:1])
            found = []
            for head in range(2):
                mine = (lane >= 64) if head else (lane < 64)
                scores = dot(jnp.where(mine, q, jnp.zeros_like(q)), k, ((1,), (1,))) * scale
                scores = jnp.where(allowed, scores, masked_value)
                top = jnp.max(scores, axis=1, keepdims=True)
                weights = jnp.exp(scores - top)
                total = jnp.sum(weights, axis=1, keepdims=True)
                found.append(
                    (dot(weights.astype(jnp.bfloat16), v, ((1,), (0,))) / total, top + jnp.log(total))
                )
            both = jnp.where(lane < 64, found[0][0], found[1][0])
            attended[rows, lanes] = both
            low[rows, lanes] = both.astype(jnp.bfloat16)
            log_total[rows, lanes] = jnp.where(lane < 64, found[0][1], found[1][1])

        next(out_job, None)
        for to in range(i * QROWS // 128, (i + 1) * QROWS // 128):
            pl.when(at.b != to)(lambda: deliver(to).start())

            @pl.when(at.b == to)
            def _():
                pltpu.make_async_copy(
                    low.at[pl.ds(to * 128, 128)],
                    mixed_heads.at[:, pl.ds(pl.multiple_of(at.b * local, local), local)],
                    local_sem,
                ).start()

    drive(out_job)
    for source in range(8):

        @pl.when(at.b != source)
        def _():
            spot = mixed_heads.at[:, pl.ds(source * local, local)]
            remote(spot, spot, send.at[source], recv.at[source], at.r, source).wait_recv()

        @pl.when(at.b == source)
        def _():
            pltpu.make_async_copy(
                low.at[pl.ds(source * 128, 128)],
                mixed_heads.at[:, pl.ds(source * local, local)],
                local_sem,
            ).wait()

    total = tokens[...].astype(jnp.float32)
    depth, width = w_out.shape[3:]
    for i, r in enumerate((at.r, at.rx, at.ry, at.rd)):
        theirs = w_out.at[r, :, 1 - at.c]
        remote(theirs, theirs, pair_send.at[i], pair_recv.at[i], at.r, at.sibling).wait_recv()
    for r in range(4):
        lanes = slice(r * 8 * depth, (r + 1) * 8 * depth)
        total += dot(mixed_heads[:, lanes], w_out[r].reshape(8 * depth, width), ((1,), (0,)))
    resid_mid[...] = total
    unit, _ = norm_stats(total)
    normed[...] = (unit * feed_set[0:1] + feed_set[1:2]).astype(jnp.bfloat16)
    drive(gate_up_job)
    for to in range(8):
        pl.when(at.b != to)(lambda: deliver(to).wait_send())
    for copy in pairs:
        copy.wait_send()


def attend_forward(x, w, bias, start, tables, tokens, feed_set, gate_up, w_out):
    length, local = x.shape[0], w.shape[1] // 3
    bf, f32 = jnp.bfloat16, jnp.float32
    flat, spans = pack_sems(
        [
            [DMA((8,)), DMA((8,)), DMA], exchange_sems(), square_gather_sems(), [DMA((4,)), DMA((4,))],
            [DMA((2,))],
        ]
    )
    outs = [((length, local), bf, VMEM)] * 3 + [((length, local), f32, VMEM)] * 2
    outs += [(tokens.shape, bf, VMEM), (tokens.shape, f32, VMEM), (tokens.shape, bf, VMEM)]
    outs += [(gate_up.shape, bf, HBM), ((4, 4, 2) + w_out.shape[1:], bf, VMEM)]
    return call(
        grouped(attend_forward_kernel, 24, spans), [HBM] * 2 + [VMEM] * 7 + [HBM] * 2, outs,
        [VMEM((length, local), bf), VMEM(x.shape, bf), VMEM(w.shape, bf)] + flat, 1,
        x, w, bias, start, *tables, tokens, feed_set, gate_up, w_out,
    )


def feed_kernel(
    own, gate_up, cotangent, w_down, resid_mid, feed_gain, out_weight,
    grad_out, hidden_out, output, weight_result, grad_mid, feed_sums, grad,
    normed, w_gate_up, values, out_partial, partial, output_sum, result, grad_rows,
    line_sems, other_sems, square_sems, out_scratch, scatter_scratch, square_scratch, own_sems, load_sems,
):
    at = Place()
    at.barrier()
    count = own.shape[0]
    hidden = hidden_out.shape[1]
    line_job = line_gather(at, cuts_of(own), rows_of(normed, count), line_sems)
    square_job = square_gather(
        at, lambda half: half_of(gate_up, 0, half), row_halves(w_gate_up), square_sems
    )
    other_job = line_gather(at, cuts_of(cotangent), rows_of(grad_out, count), other_sems)

    def rows_at(z):
        return pl.ds(pl.multiple_of(z * 2 * count, 2 * count), 2 * count)

    def hidden_back(z):
        rows = rows_at(z)
        partial[rows, :hidden] = dot(grad_out[rows], w_down[...], ((1,), (1,))).astype(jnp.bfloat16)

    def forward(z):
        rows = rows_at(z)
        both = dot(normed[rows], w_gate_up[...], ((1,), (0,)))
        gate_value, up_value = both[:, :hidden], both[:, hidden:]
        low = (gate_value / (1.0 + jnp.exp(-gate_value)) * up_value).astype(jnp.bfloat16)
        hidden_out[rows] = low
        values[rows] = both.astype(jnp.bfloat16)
        out_partial[rows] = dot(low, w_down[...], ((1,), (0,))).astype(jnp.bfloat16)

    def backward(z):
        rows = rows_at(z)
        both = values[rows].astype(jnp.float32)
        gate_value, up_value = both[:, :hidden], both[:, hidden:]
        grad_hidden = partial[rows, :hidden].astype(jnp.float32)
        gate_sigmoid = 1.0 / (1.0 + jnp.exp(-gate_value))
        silu = gate_value * gate_sigmoid
        grad_gate = grad_hidden * up_value * gate_sigmoid * (1.0 + gate_value * (1.0 - gate_sigmoid))
        grads = jnp.concatenate([grad_gate, grad_hidden * silu], axis=1).astype(jnp.bfloat16)
        values[rows] = grads
        partial[rows] = dot(grads, w_gate_up[...], ((1,), (1,))).astype(jnp.bfloat16)

    def near(i):
        return at.z + (i + 1) // 2 * (1 - 2 * lax.rem(i, 2))

    def far(i):
        return at.z + 3 * (2 * i - 1)

    def each(count, place, work):
        @pl.loop(0, count)
        def _(i):
            z = place(i)
            pl.when((z >= 0) & (z <= 3))(lambda: work(z))

    out_job = line_scatter(at, rows_of(out_partial, count), output_sum, out_scratch)
    next(line_job)
    next(square_job)
    next(other_job)
    for i in range(4):
        steps(line_job, 1)
        steps(square_job, 1)
        steps(other_job, 1)
    each(5, near, hidden_back)
    drive(square_job)
    each(5, near, forward)
    steps(line_job, 2)
    each(2, far, forward)
    next(out_job)
    steps(other_job, 2)
    each(2, far, hidden_back)
    for z in range(4):
        backward(z)
        steps(out_job, 1)

    depth = weight_result.shape[0]
    step = depth // 2

    def prepare(r):
        for half in range(2):
            spot = pl.ds(pl.multiple_of(r * depth + half * step, step), step)
            w_gate_up[spot] = dot(normed[:, spot], values[...], ((0,), (0,))).astype(jnp.bfloat16)

    scatter_job = line_scatter(at, rows_of(partial, count), result, scatter_scratch)
    weight_job = square_scatter(at, row_halves(w_gate_up), weight_result, square_scratch, 0, prepare)
    next(scatter_job)
    steps(weight_job, 3)
    drive(scatter_job, limited(weight_job, 2), line_job)
    half = out_partial.shape[0]
    loads = [
        pltpu.make_async_copy(out_weight.at[pl.ds(i * half, half)], place, load_sems[0].at[i])
        for i, place in enumerate((normed, partial))
    ]
    for load in loads:
        load.start()
    unit, inverse = norm_stats(resid_mid[...])
    mid_part, gain_part, shift_part = norm_back(result[...], unit, inverse, feed_gain[...])
    total = cotangent[...].astype(jnp.float32) + mid_part
    grad_mid[...] = total
    low = total.astype(jnp.bfloat16)
    feed_sums[0:1] = gain_part[None]
    feed_sums[1:2] = shift_part[None]
    for i, place in enumerate((normed, partial)):
        loads[i].wait()
        grad_rows[:, i * half : (i + 1) * half] = dot(low, place[...], ((1,), (1,))).astype(jnp.bfloat16)
    local = grad.shape[1]
    own_job = exchange(
        at,
        lambda b, p: grad_rows.at[:, pl.ds(pl.multiple_of(b * local, local), local)],
        lambda b, p: grad.at[pl.ds(pl.multiple_of(b * count, count), count)],
        own_sems,
    )
    next(own_job)
    drive(out_job, weight_job, other_job)
    output[...] = (resid_mid[...] + output_sum[...]).astype(jnp.bfloat16)
    drive(own_job)


def feed(own, gate_up, cotangent, w_down, resid_mid, feed_gain, w_out):
    bf, f32 = jnp.bfloat16, jnp.float32
    rows, width = own.shape
    hidden = w_down.shape[0]
    owned = (width // 4, 2 * hidden)
    full, mine = (8 * rows, width), (rows, width)
    flat, spans = pack_sems(
        [
            line_gather_sems(), line_gather_sems(), square_gather_sems(),
            line_scatter_scratch(rows, width), line_scatter_scratch(rows, width),
            square_scatter_scratch(*owned), exchange_sems(), [DMA((2,))],
        ]
    )
    outs = [(full, bf, VMEM), ((8 * rows, hidden), bf, VMEM), (mine, bf, VMEM), (owned, bf, VMEM)]
    outs += [(mine, f32, VMEM), ((2, width), f32, VMEM), ((8 * rows, width // 8), bf, VMEM)]
    scratch = [
        VMEM(full, bf), VMEM((width, 2 * hidden), bf), VMEM((8 * rows, 2 * hidden), bf), VMEM(full, bf),
        VMEM(full, bf), VMEM(mine, f32), VMEM(mine, f32), VMEM(mine, bf),
    ]
    return call(
        grouped(feed_kernel, 22, spans), [VMEM, HBM, VMEM, VMEM, VMEM, VMEM, HBM], outs, scratch + flat, 2,
        own, gate_up, cotangent, w_down, resid_mid, feed_gain, w_out,
    )


def limited(job, count):
    for _ in range(count):
        next(job)
        yield


def attend_backward_kernel(
    grad, grad_mid, queries, keys, values, attended, log_total,
    start, cosine, minus, plus, mixed_heads, gate_up,
    grad_mixed, out_result, gate_result, up_result,
    keys_sum, values_sum, pieces, halves, heads_pair, mid_pair, product_rows,
    square_scratch, pair_sems, gate_up_sems,
):
    at = Place()
    at.barrier()
    gate_up_job = exchange(at, lambda b, p: gate_up.at[b], lambda b, p: pieces.at[b], gate_up_sems)
    next(gate_up_job)
    mid_pair[:128] = grad_mid[...].astype(jnp.bfloat16)
    heads_pair[:128] = mixed_heads[...]
    pair_send, pair_recv = pair_sems
    pairs = [
        remote(ref.at[pl.ds(0, 128)], ref.at[pl.ds(128, 128)], pair_send.at[i], pair_recv.at[i], at.r, at.sibling)
        for i, ref in enumerate((heads_pair, mid_pair))
    ]
    for copy in pairs:
        copy.start()
    length, local = queries.shape
    scale = 1.0 / math.sqrt(local * 8 // HEADS)
    blocks = length // QROWS
    keys_sum[...] = jnp.zeros_like(keys_sum)
    values_sum[...] = jnp.zeros_like(values_sum)
    for copy in pairs:
        copy.wait()
    depth = halves.shape[2]

    def prepare(r):
        for z in range(4):
            lanes = pl.ds(pl.multiple_of((r * 4 + z) * 2 * depth, 2 * depth), 2 * depth)
            product_rows[...] = dot(heads_pair[:, lanes], mid_pair[...], ((0,), (0,)))
            mine = product_rows[pl.ds(pl.multiple_of(at.c * depth, depth), depth)]
            halves[r, z] = mine.astype(jnp.bfloat16)

    out_job = square_scatter(
        at, lambda r, half: halves.at[r, pl.ds(2 * half, 2)], out_result, square_scratch, 0, prepare
    )
    steps(out_job, 3)
    for i in range(blocks):
        rows = slice(i * QROWS, (i + 1) * QROWS)
        count = (i + 1) * QROWS

        @pl.loop(0, local // 128)
        def _(pair):
            lanes = pl.ds(pl.multiple_of(pair * 128, 128), 128)
            lane = lax.broadcasted_iota(jnp.int32, (QROWS, 128), 1)
            q, g = queries[rows, lanes], grad[rows, lanes]
            k, v = keys[:count, lanes], values[:count, lanes]
            allowed = score_mask(i * QROWS, QROWS, count, start[rows, 0:1])
            product = g.astype(jnp.float32) * attended[rows, lanes]
            logs = log_total[rows, lanes]
            queries_part, keys_part, values_part = [], [], []
            for head in range(2):
                mine = (lane >= 64) if head else (lane < 64)
                q_head = jnp.where(mine, q, jnp.zeros_like(q))
                g_head = jnp.where(mine, g, jnp.zeros_like(g))
                delta = jnp.sum(jnp.where(mine, product, 0.0), axis=1, keepdims=True)
                log_head = jnp.max(jnp.where(mine, logs, masked_value), axis=1, keepdims=True)
                scores = dot(q_head, k, ((1,), (1,))) * scale
                probs = jnp.exp(jnp.where(allowed, scores - log_head, masked_value))
                grad_probs = dot(g_head, v, ((1,), (1,)))
                grad_scores = (probs * (grad_probs - delta) * scale).astype(jnp.bfloat16)
                queries_part.append(dot(grad_scores, k, ((1,), (0,))))
                keys_part.append(dot(grad_scores, q_head, ((0,), (0,))))
                values_part.append(dot(probs.astype(jnp.bfloat16), g_head, ((0,), (0,))))
            both = jnp.where(lane < 64, queries_part[0], queries_part[1])
            tables = (cosine[rows], -minus[rows], -plus[rows])
            grad_mixed[rows, lanes] = turned(both, *tables).astype(jnp.bfloat16)
            keys_sum[:count, lanes] += keys_part[0] + keys_part[1]
            values_sum[:count, lanes] += values_part[0] + values_part[1]

        next(out_job, None)

    @pl.loop(0, blocks)
    def _(i):
        rows = pl.ds(pl.multiple_of(i * QROWS, QROWS), QROWS)
        tables = (cosine[rows], -minus[rows], -plus[rows])
        for pair in range(local // 128):
            lanes = slice(pair * 128, pair * 128 + 128)
            shifted = slice(local + pair * 128, local + pair * 128 + 128)
            grad_mixed[rows, shifted] = turned(keys_sum[rows, lanes], *tables).astype(jnp.bfloat16)
        grad_mixed[rows, slice(2 * local, 3 * local)] = values_sum[rows].astype(jnp.bfloat16)

    drive(out_job)
    drive(gate_up_job)
    hidden = pieces.shape[2] // 8
    for b in range(8):
        for r in range(4):
            source = slice((8 * r + b) * hidden, (8 * r + b + 1) * hidden)
            gate_result[:, source] = pieces[b, :, r * hidden : (r + 1) * hidden]
            up_result[:, source] = pieces[b, :, (4 + r) * hidden : (5 + r) * hidden]


def attend_backward(
    grad, grad_mid, queries, keys, values, attended, log_total, start, tables, mixed_heads, gate_up
):
    length, local = queries.shape
    bf, f32 = jnp.bfloat16, jnp.float32
    depth = gate_up.shape[1]
    rows, width = mixed_heads.shape
    quarter = [VMEM((4, depth, width), bf)] * 2 + [VMEM((2, depth, width), bf)] * 4
    flat, spans = pack_sems(
        [quarter + [DMA((6,)), DMA((6,))], [DMA((2,)), DMA((2,))], exchange_sems()]
    )
    shard = (depth, 4 * gate_up.shape[2])
    outs = [((length, 3 * local), bf, VMEM), ((4, depth, width), bf, VMEM)] + [(shard, bf, VMEM)] * 2
    scratch = [VMEM((length, local), f32), VMEM((length, local), f32)]
    scratch += [VMEM(gate_up.shape, bf), VMEM((4, 4, depth, width), bf)]
    scratch += [VMEM((2 * rows, width), bf)] * 2 + [VMEM((2 * depth, width), f32)]
    return call(
        grouped(attend_backward_kernel, 24, spans), [VMEM] * 12 + [HBM], outs, scratch + flat, 4,
        grad, grad_mid, queries, keys, values, attended, log_total, start, *tables, mixed_heads, gate_up,
    )


def finish_kernel(
    w_project, grad_mixed, out_part, x_ref, gain, feed_sums, bias_sums, normed_all, hidden_all,
    grad_out_all, tokens_part, project_grad, down_grad, out_grad, vector_out,
    weight, weight_result, pieces, first, sums, arrived, summed, rows_in, down_partial, partial, overlap,
    normed, hidden, grad_out,
    line_scratch, project_scratch, down_scratch, out_scratch, piece_sems, vector_sems, row_sems, load_sems,
):
    at = Place()
    loads = [
        pltpu.make_async_copy(*pair, load_sems[0].at[i])
        for i, pair in enumerate(((normed_all, normed), (hidden_all, hidden), (grad_out_all, grad_out)))
    ]
    for load in loads:
        load.start()
    at.barrier(diagonal=True)
    rows, width = first.shape
    depth = weight_result.shape[0]

    def prepare(r):
        spot = pl.ds(pl.multiple_of(r * depth, depth), depth)
        product = dot(normed[:, spot], grad_mixed[...], ((0,), (0,)))
        weight[spot] = product.astype(jnp.bfloat16)
        found = jnp.sum(product * w_project[spot].astype(jnp.float32), axis=1, keepdims=True)
        overlap[spot] = jnp.broadcast_to(found, (depth, 128))

    def prepare_down(r):
        count = down_grad.shape[0]
        for i in range(4):
            pl.when(r == i)(lambda: down_quarter(i, count))

    def down_quarter(i, count):
        rows_ = slice(i * count, (i + 1) * count)
        down_partial[rows_] = dot(hidden[:, rows_], grad_out[...], ((0,), (0,))).astype(jnp.bfloat16)

    shard = depth // 8
    size = shard // CHUNKS

    def prepare_rows(z):
        spot = slice(z * 2 * rows, (z + 1) * 2 * rows)
        partial[spot] = dot(grad_mixed[spot], w_project[...], ((1,), (1,))).astype(jnp.bfloat16)

    line_job = line_scatter(at, rows_of(partial, rows), first, line_scratch, True, prepare_rows)
    out_job = line_scatter(
        at, lambda z, c, k: out_part.at[z, pl.ds(k * size, size)], out_grad, out_scratch, False
    )

    def project_work():
        yield from square_scatter(at, row_halves(weight), weight_result, project_scratch, 0, prepare)
        yield from exchange(
            at,
            lambda b, p: weight_result.at[pl.ds(pl.multiple_of(b * shard, shard), shard)],
            lambda b, p: pieces.at[b],
            piece_sems,
        )

    project_job = project_work()
    down_job = square_scatter(
        at, row_halves(down_partial, 1), down_grad, down_scratch, 1, prepare_down
    )

    def vector_work():
        column = jnp.sum(grad_mixed[...].astype(jnp.float32), axis=0, keepdims=True)
        high = column.astype(jnp.bfloat16)
        low = (column - high.astype(jnp.float32)).astype(jnp.bfloat16)
        row = lax.broadcasted_iota(jnp.int32, (16, column.shape[1]), 0)
        both = jnp.where(row == 0, high, jnp.where(row == 1, low, jnp.zeros_like(low)))
        plain = dot(both, w_project[...], ((1,), (1,)))
        times = jnp.concatenate(
            [jnp.transpose(overlap[t * 128 : t * 128 + 128])[0:1] for t in range(width // 128)], axis=1
        )
        parts = jnp.concatenate([times, plain[0:1] + plain[1:2], feed_sums[...]], axis=0)
        for b in range(8):
            for r in range(4):
                lanes = slice((4 * r + b // 2) * 128, (4 * r + b // 2 + 1) * 128)
                sums[b, r, 0:4] = parts[:, lanes]
                sums[b, r, 4:6] = bias_sums[b, r]
                sums[b, r, 6:8] = jnp.zeros((2, 128), jnp.float32)
        spread = exchange(at, lambda b, p: sums.at[b], lambda b, p: arrived.at[b], vector_sems)
        next(spread)
        yield
        drive(spread)
        summed[...] = jnp.sum(arrived[...], axis=0)
        send, recv = row_sems
        copies = [
            remote(summed.at[row], rows_in.at[i], send.at[i], recv.at[i], row, at.b)
            for i, row in enumerate((at.rx, at.ry, at.rd))
        ]
        for copy in copies:
            copy.start()
        yield
        for copy in copies:
            copy.wait()
        vector_out[...] = summed[at.r] + rows_in[0] + rows_in[1] + rows_in[2]

    def tokens_work():
        unit, inverse = norm_stats(x_ref[...].astype(jnp.float32))
        part, _, _ = norm_back(first[...], unit, inverse, gain[...])
        tokens_part[...] = part

    vector_job = vector_work()
    next(line_job)
    loads[0].wait()
    steps(project_job, 3)
    next(line_job)
    next(out_job)
    next(line_job)
    next(project_job)
    next(out_job)
    next(line_job)
    loads[1].wait()
    loads[2].wait()
    steps(down_job, 3)
    next(out_job)
    next(project_job)
    next(line_job)
    next(project_job)
    next(out_job)
    next(vector_job)
    next(line_job)
    next(out_job)
    next(line_job)
    next(down_job)
    next(vector_job)
    drive(line_job)
    next(out_job)
    tokens_work()
    drive(out_job)
    drive(vector_job)
    drive(down_job)
    drive(project_job)
    inner = pieces.shape[2] // 3
    for b in range(8):
        for p in range(3):
            lanes = slice(p * width + b * inner, p * width + (b + 1) * inner)
            project_grad[:, lanes] = pieces[b, :, p * inner : (p + 1) * inner]


def finish(
    w_project, normed, grad_mixed, hidden, grad_out, out_part, x, gain, feed_sums, bias_sums
):
    bf, f32 = jnp.bfloat16, jnp.float32
    rows, width = x.shape
    inner = grad_mixed.shape[1]
    depth = width // 4
    shard = depth // 8
    down_owned = (hidden.shape[1] // 4, width)
    flat, spans = pack_sems(
        [
            line_scatter_scratch(rows, width),
            square_scatter_scratch(depth, inner),
            square_scatter_scratch(*down_owned, 1),
            line_scatter_scratch(shard, width),
            exchange_sems(), exchange_sems(), [DMA((3,)), DMA((3,))], [DMA((3,))],
        ]
    )
    outs = [
        ((rows, width), f32, VMEM), ((shard, 8 * inner), bf, VMEM), (down_owned, bf, VMEM),
        ((shard, width), bf, VMEM), ((8, 128), f32, VMEM),
    ]
    scratch = [
        VMEM((width, inner), bf), VMEM((depth, inner), bf), VMEM((8, shard, inner), bf),
        VMEM((rows, width), f32), VMEM((8, 4, 8, 128), f32), VMEM((8, 4, 8, 128), f32),
        VMEM((4, 8, 128), f32), VMEM((3, 8, 128), f32),
        VMEM((hidden.shape[1], width), bf), VMEM((8 * rows, width), bf),
        VMEM((width, 128), f32), VMEM(normed.shape, bf), VMEM(hidden.shape, bf), VMEM(grad_out.shape, bf),
    ]
    return call(
        grouped(finish_kernel, 29, spans), [VMEM] * 7 + [HBM] * 3, outs, scratch + flat, 5,
        w_project, grad_mixed, out_part, x, gain, feed_sums, bias_sums, normed, hidden, grad_out,
    )


def widen_kernel(part, base, *refs):
    count = len(refs) // 2
    sources, total, results = refs[:count], refs[count], refs[count + 1 :]
    total[...] = part[...] + base[...]
    for source, result in zip(sources, results):
        result[...] = source[...].astype(jnp.float32)


def widen(part, base, *arrays):
    kinds = [jax.ShapeDtypeStruct(array.shape, jnp.float32) for array in (part,) + arrays]
    return pl.pallas_call(
        widen_kernel,
        out_shape=kinds,
        in_specs=[pl.BlockSpec(memory_space=VMEM)] * (2 + len(arrays)),
        out_specs=[pl.BlockSpec(memory_space=VMEM)] * len(kinds),
        compiler_params=pltpu.CompilerParams(vmem_limit_bytes=LIMIT),
    )(part, base, *arrays)


def fast_body(
    tokens, segments, cotangent, attend_gain, attend_shift, project_weight, project_bias,
    output_weight, feed_gain, feed_shift, gate_weight, up_weight, down_weight,
):
    bf, f32 = jnp.bfloat16, jnp.float32
    own_rows, width = tokens.shape[1], tokens.shape[2]
    length = own_rows * 8
    head_width = width // HEADS
    local = width // 8
    hidden = down_weight.shape[0]
    shard = attend_gain.shape[0]
    b = lax.axis_index("blk")

    small = jnp.stack([attend_gain, attend_shift, feed_gain, feed_shift])
    zeros = jnp.zeros_like(small)
    small = jnp.where(
        b % 2 == 0, jnp.concatenate([small, zeros], 1), jnp.concatenate([zeros, small], 1)
    )
    rest = jnp.pad(project_bias, (0, 64)).reshape(2, 128)
    vector = jnp.concatenate(
        [small, rest, segments.astype(bf), jnp.zeros((9, 128), bf)], axis=0
    )

    vectors, normed_first, w_project, w_down, w_out, gate_up, start, tables = start_call(
        tokens[0], vector, project_weight, down_weight, output_weight, gate_weight, up_weight
    )

    def whole(row):
        pairs = vectors[:, row].reshape(16, 2, 128).astype(f32)
        return (pairs[:, 0] + pairs[:, 1]).reshape(-1)

    a_gain, f_gain, f_shift = whole(0), whole(2), whole(3)
    bias = vectors[:, 4:6].reshape(32, 256)[:, : 3 * shard].reshape(3, 8, local)
    bias = lax.dynamic_index_in_dim(bias, b, 1, False).reshape(1, -1).astype(f32)

    (
        queries, keys, values, attended, log_total, attended_low, resid_mid, normed_second, gate_up, w_out
    ) = attend_forward(
        normed_first, w_project, bias, start, tables, tokens[0], jnp.stack([f_gain, f_shift]), gate_up, w_out
    )
    grad_out, hidden_low, output, gate_up_grad, grad_mid, feed_sums, grad = feed(
        normed_second, gate_up.reshape(8 * shard, 8 * hidden), cotangent[0], w_down, resid_mid, f_gain[None],
        w_out.reshape(width, width),
    )
    grad_mixed, out_part, gate_grad, up_grad = attend_backward(
        grad, grad_mid, queries, keys, values, attended, log_total, start, tables, attended_low,
        gate_up_grad.reshape(8, shard, 8 * hidden),
    )

    bias_part = jnp.sum(grad_mixed.astype(f32), axis=0).reshape(3, 1, local)
    bias_part = jnp.where(jnp.arange(8)[None, :, None] == b, bias_part, 0.0)
    bias_part = jnp.pad(bias_part.reshape(32, 3 * shard), ((0, 0), (0, 64)))
    bias_part = bias_part.reshape(4, 8, 2, 128).transpose(1, 0, 2, 3)
    tokens_part, project_grad, down_grad, out_grad, vector = finish(
        w_project, normed_first, grad_mixed, hidden_low, grad_out, out_part, tokens[0], a_gain[None],
        feed_sums, bias_part,
    )
    grad_tokens, project_grad, down_grad, out_grad, gate_grad, up_grad = widen(
        tokens_part, grad_mid, project_grad, down_grad, out_grad, gate_grad, up_grad
    )
    gains = jnp.where(b % 2 == 0, vector[:4, :shard], vector[:4, shard:])
    gain_grad = (gains[0] - attend_shift.astype(f32) * gains[1]) / attend_gain.astype(f32)
    return (
        output[None], grad_tokens[None], gain_grad, gains[1], project_grad,
        vector[4:6].reshape(-1)[: 3 * shard], out_grad, gains[2], gains[3], gate_grad, up_grad, down_grad,
    )


def solution(mesh):
    tokens = P("rows", "blk", None)
    vector, matrix = P(BOTH), P(BOTH, None)
    in_specs = (
        tokens, P("rows", "blk"), tokens, vector, vector, matrix, vector, matrix, vector, vector,
        matrix, matrix, matrix,
    )
    out_specs = (
        tokens, tokens, vector, vector, matrix, vector, matrix, vector, vector, matrix, matrix, matrix,
    )
    if (mesh.shape["rows"], mesh.shape["blk"]) == (4, 8):
        body = fast_body
    else:
        body = make_body(mesh.shape["rows"], mesh.shape["blk"])
    return jax.shard_map(body, mesh=mesh, in_specs=in_specs, out_specs=out_specs, check_vma=False)
```
